32 devices in a mesh: dp: 8 (over z, y), tm: 4 (over x, core).
Axes of the slice: x: 2, y: 2, z: 4, core: 2. Of those that a mesh axis runs over, the one named last changes fastest.
Arguments:
- frames: bfloat16 [8, 3072, 1536], P('dp', 'tm')
- w_qkv: bfloat16 [1536, 2304], P('dp'), may hold values from -0.15625 to 0.15625
- utt_start: int32 [8, 3], P('dp'), may hold values from 0 to 2943, as said below
- stretch_utt: int32 [8, 12], P('dp'), may hold values from 0 to 2, as said below
- left_stretches: int32 [8, 12], P('dp'), may hold values from 0 to 2, as said below
Outputs:
- context: bfloat16 [8, 3072, 768], P('dp', 'tm')
The draws below stay inside these ranges and needn't reach their ends.
Inputs may be any that keep to these rules, and one draw needn't show every extreme that they name: `stretch_utt`: in each pack nondecreasing along blocks; utterance u covers one or more whole consecutive blocks; every utterance of 0 to 2 occurs, block 0 in utterance 0. `utt_start`: for utterance u with first block b, at least 256 * b and less than 256 * b + 128. `left_stretches`: at most the number of earlier blocks of the same utterance.
All inputs are finite; a program needn't handle non-finite values.
Results may differ from the reference program's by a relative error of at most 0.0045.
The reference program's roundings to bfloat16 on the way (of `qkv` and `probs`) count: a program that leaves them out, or rounds other values in their place, can miss the bound.
Values may be sent and summed in bfloat16 or wider, within the bound.
No kernel may reach another device: no remote copies, remote signals or barrier semaphores. Data moves between devices by JAX's collectives and lax.ppermute only.
A program may use at most 64 MiB of HBM per device.

```python
import jax
import jax.numpy as jnp
from jax import lax

D = 1536
HEADS = 8
HEAD_DIM = 96
STRETCH = 256
LEFT = 2
HW = 768
FRAMES = 3072
NCH = 12
UTT = 3
PACKS = 8


def layout(key):

    def single(sub):
        order = jax.random.permutation(sub, NCH - 1).astype(jnp.int32)
        bounds = order[:UTT - 1] + 1
        stretch = jnp.arange(NCH, dtype=jnp.int32)
        owners = jnp.sum((bounds[None, :] <= stretch[:, None]).astype(jnp.int32), axis=1)
        ids = jnp.arange(UTT, dtype=jnp.int32)
        firsts = jnp.sum((owners[None, :] < ids[:, None]).astype(jnp.int32), axis=1)
        return (owners, firsts)
    return jax.vmap(single)(jax.random.split(key, PACKS))


def draw_frames(key, part):
    key = jax.random.fold_in(key, 3)
    return jax.random.normal(key, (PACKS, FRAMES, D), jnp.float32).astype(jnp.bfloat16)


def draw_stretch_utt(key, part):
    owners, firsts = layout(key)
    return owners


def draw_utt_start(key, part):
    owners, firsts = layout(key)
    key = jax.random.fold_in(key, 7)
    offsets = jax.random.randint(key, (PACKS, UTT), 0, STRETCH // 2, dtype=jnp.int32)
    return STRETCH * firsts + offsets


def draw_left_stretches(key, part):
    owners, firsts = layout(key)
    key = jax.random.fold_in(key, 11)
    wanted = jax.random.randint(key, (PACKS, NCH), 0, LEFT + 1, dtype=jnp.int32)
    ids = jnp.arange(UTT, dtype=jnp.int32)
    own_first = jnp.sum(jnp.where(owners[:, :, None] == ids[None, None, :], firsts[:, None, :], 0), axis=-1)
    position = jnp.arange(NCH, dtype=jnp.int32)[None, :] - own_first
    return jnp.minimum(wanted, position)


def block_levels(stream_key, shape, cuts, low, high):
    def one(axis_at, blocks):
        draws = jax.random.uniform(jax.random.fold_in(jax.random.fold_in(stream_key, 6), axis_at), (blocks,), jnp.float32, low / len(cuts), high / len(cuts))
        return jnp.repeat(jnp.exp(draws), shape[axis_at] // blocks).reshape((-1,) + (1,) * (len(shape) - axis_at - 1))

    factor_of = one(*cuts[0])
    for cut in cuts[1:]:
        factor_of = factor_of * one(*cut)
    return factor_of


def normal_values(key, extent, spread, limit, pieces=(), kind=jnp.bfloat16):
    array = jax.random.normal(key, extent, jnp.float32) * spread
    if len(pieces) > 0:
        array = block_levels(key, extent, pieces, -0.22, 0.18) * array
    return jnp.clip(array, min=-limit, max=limit).astype(kind)


def setup_inputs(seed: int = 0) -> dict:
    seeds = jax.random.split(jax.random.key(seed), 6)
    frames = draw_frames(jax.random.fold_in(seeds[5], 71), 0)
    w_qkv = normal_values(seeds[1], (D, 3 * HW), D ** -0.5, 0.15625, ((0, 8),))
    utt_start = draw_utt_start(jax.random.fold_in(seeds[5], 71), 0)
    stretch_utt = draw_stretch_utt(jax.random.fold_in(seeds[5], 71), 0)
    left_stretches = draw_left_stretches(jax.random.fold_in(seeds[5], 71), 0)
    return dict(frames=frames, w_qkv=w_qkv, utt_start=utt_start, stretch_utt=stretch_utt, left_stretches=left_stretches)


def reference(frames, w_qkv, utt_start, stretch_utt, left_stretches):
    inner = HEADS * HEAD_DIM
    reach = LEFT * STRETCH
    scale = HEAD_DIM ** -0.5

    def one_pack(pack):
        inputs, starts, owners, lefts = pack
        qkv = jnp.dot(inputs, w_qkv, preferred_element_type=jnp.float32).astype(jnp.bfloat16)
        query = qkv[:, :inner]
        keys = qkv[:, inner:2 * inner]
        values = qkv[:, 2 * inner:]
        frame = jnp.arange(inputs.shape[0], dtype=jnp.int32)
        fowner = owners[frame // STRETCH]
        live = frame >= starts[fowner]
        keys_pad = jnp.pad(keys, ((reach, 0), (0, 0)))
        values_pad = jnp.pad(values, ((reach, 0), (0, 0)))
        key_owner = jnp.concatenate([jnp.full((reach,), -1, jnp.int32), fowner])
        key_live = jnp.concatenate([jnp.zeros((reach,), bool), live])
        relative = jnp.arange(reach + STRETCH, dtype=jnp.int32) // STRETCH

        def one_stretch(block):
            start = block * STRETCH
            qblock = lax.dynamic_slice_in_dim(query, start, STRETCH, 0).astype(jnp.float32)
            kblock = lax.dynamic_slice_in_dim(keys_pad, start, reach + STRETCH, 0).astype(jnp.float32)
            vblock = lax.dynamic_slice_in_dim(values_pad, start, reach + STRETCH, 0).astype(jnp.float32)
            kown = lax.dynamic_slice_in_dim(key_owner, start, reach + STRETCH, 0)
            klive = lax.dynamic_slice_in_dim(key_live, start, reach + STRETCH, 0)
            usable = (relative >= LEFT - lefts[block]) & (kown == owners[block]) & klive
            qh = qblock.reshape(STRETCH, HEADS, HEAD_DIM)
            kh = kblock.reshape(reach + STRETCH, HEADS, HEAD_DIM)
            vh = vblock.reshape(reach + STRETCH, HEADS, HEAD_DIM)
            scores = jnp.einsum('qhd,khd->hqk', qh, kh) * scale
            scores = jnp.where(usable[None, None, :], scores, -jnp.inf)
            top = jnp.max(scores, axis=-1, keepdims=True)
            expo = jnp.exp(scores - top)
            probs = (expo / jnp.sum(expo, axis=-1, keepdims=True)).astype(jnp.bfloat16)
            probs = lax.optimization_barrier(probs).astype(jnp.float32)
            mixed = jnp.einsum('hqk,khd->qhd', probs, vh).reshape(STRETCH, inner)
            qlive = lax.dynamic_slice_in_dim(live, start, STRETCH, 0)
            return jnp.where(qlive[:, None], mixed, jnp.zeros_like(mixed)).astype(jnp.bfloat16)

        result = lax.map(one_stretch, jnp.arange(NCH, dtype=jnp.int32))
        return result.reshape(inputs.shape[0], inner)

    return lax.map(one_pack, (frames, utt_start, stretch_utt, left_stretches))
```

```python
import functools
import math

import jax
import jax.numpy as jnp
from jax import lax
from jax.experimental import pallas as pl
from jax.experimental.pallas import tpu as pltpu
from jax.sharding import PartitionSpec as P

HEAD_DIM = 96
STRETCH = 256
LEFT = 2
LANES = 128
SPAN = (LEFT + 1) * STRETCH
EXP_SCALE = HEAD_DIM**-0.5 * math.log2(math.e)


def dot(a, b, dims=((1,), (0,))):
    return lax.dot_general(a, b, (dims, ((), ())), preferred_element_type=jnp.float32)


def head_window(head):
    first = head * HEAD_DIM // LANES * LANES
    last = -(-(head + 1) * HEAD_DIM // LANES) * LANES
    return first, last


def attend_kernel(
    where_ref, start_ref, owner_ref, left_ref, own_ref, partner_ref, halo_ref, w_ref,
    own_out, partner_out, q_s, k_s, v_s,
):
    rows = own_ref.shape[0]
    width = q_s.shape[1]
    reach = LEFT * STRETCH
    blocks = rows // STRETCH
    core = where_ref[0]
    pair = where_ref[1]

    def project(x_ref, row, q_row, k_row):
        x = x_ref[pl.ds(row, STRETCH), :]
        if q_row is not None:
            q = dot(x, w_ref[:, :width])
            q_s[pl.ds(q_row, STRETCH), :] = q.astype(jnp.bfloat16)
        k = dot(x, w_ref[:, width : 2 * width])
        k_s[pl.ds(k_row, STRETCH), :] = k.astype(jnp.bfloat16)
        v = dot(x, w_ref[:, 2 * width :])
        v_s[pl.ds(k_row, STRETCH), :] = v.astype(jnp.bfloat16)

    @pl.loop(0, LEFT)
    def _(i):
        row = pl.multiple_of(i * STRETCH, STRETCH)
        project(halo_ref, row, None, row)

    for x_ref, place in ((partner_ref, 1 - core), (own_ref, core)):

        @pl.loop(0, blocks)
        def _(i):
            row = pl.multiple_of(i * STRETCH, STRETCH)
            q_row = pl.multiple_of(place * rows + row, STRETCH)
            project(x_ref, row, q_row, pl.multiple_of(q_row + reach, STRETCH))

    lane = lax.broadcasted_iota(jnp.int32, (1, width), 1)

    def attend(place, out_ref):
        @pl.loop(0, blocks)
        def _(i):
            row = pl.multiple_of(i * STRETCH, STRETCH)
            local_row = pl.multiple_of(place * rows + row, STRETCH)
            chunk = (pair * 2 + place) * blocks + i
            start = start_ref[0, owner_ref[0, chunk]]
            lowest = jnp.maximum((chunk - left_ref[0, chunk]) * STRETCH, start)
            key_frame = (chunk - LEFT) * STRETCH + lax.broadcasted_iota(jnp.int32, (1, SPAN), 1)
            bias = jnp.where(key_frame >= lowest, 0.0, -jnp.inf).astype(jnp.float32)
            frame = chunk * STRETCH + lax.broadcasted_iota(jnp.int32, (STRETCH, 1), 0)
            live = frame >= start
            tiles = [jnp.zeros((STRETCH, LANES), jnp.float32) for _ in range(width // LANES)]
            for head in range(width // HEAD_DIM):
                first, last = head_window(head)
                inside = (lane >= head * HEAD_DIM) & (lane < (head + 1) * HEAD_DIM)
                inside = inside[:, first:last]
                q = q_s[pl.ds(local_row, STRETCH), first:last]
                q = jnp.where(inside, q, jnp.zeros_like(q))
                k = k_s[pl.ds(local_row, SPAN), first:last]
                scores = dot(q, k, ((1,), (1,))) + bias
                top = jnp.max(scores, axis=-1, keepdims=True)
                expo = jnp.exp2((scores - top) * EXP_SCALE)
                total = jnp.sum(expo, axis=-1, keepdims=True)
                probs = (expo * (1.0 / total)).astype(jnp.bfloat16)
                mixed = dot(probs, v_s[pl.ds(local_row, SPAN), first:last])
                for tile in range(first // LANES, last // LANES):
                    at = tile * LANES
                    tiles[tile] = jnp.where(
                        inside[:, at - first : at - first + LANES],
                        mixed[:, at - first : at - first + LANES],
                        tiles[tile],
                    )
            for tile, value in enumerate(tiles):
                value = jnp.where(live, value, 0.0).astype(jnp.bfloat16)
                out_ref[pl.ds(row, STRETCH), tile * LANES : (tile + 1) * LANES] = value

    attend(1 - core, partner_out)
    attend(core, own_out)


def local(frames, w_qkv, utt_start, stretch_utt, left_stretches):
    inputs = frames[0]
    rows, depth = inputs.shape
    inner = w_qkv.shape[1] // 3
    width = inner // 2
    reach = LEFT * STRETCH
    members = lax.axis_size("tm")
    place = lax.axis_index("tm")
    core = place % 2
    pair = place // 2

    thirds = w_qkv.reshape(w_qkv.shape[0], 3, 2, width)
    half = lax.dynamic_index_in_dim(thirds, core, 2, keepdims=False)
    half = half.reshape(w_qkv.shape[0], 3 * width)
    weights = lax.all_gather(half, "dp", axis=0, tiled=True)

    swap = [(i, i ^ 1) for i in range(members)]
    partner = lax.ppermute(inputs, "tm", swap)
    tail = inputs[rows - reach :]
    halo = lax.ppermute(tail, "tm", [(i, i + 1) for i in range(1, members - 1, 2)])
    halo_odd = lax.ppermute(halo, "tm", [(i, i + 1) for i in range(0, members, 2)])
    halo = jnp.where(core == 0, halo, halo_odd)

    where = jnp.stack([core, pair]).astype(jnp.int32)
    smem = pl.BlockSpec(memory_space=pltpu.SMEM)
    vmem = pl.BlockSpec(memory_space=pltpu.VMEM)
    own_out, partner_out = pl.pallas_call(
        attend_kernel,
        out_shape=[jax.ShapeDtypeStruct((rows, width), jnp.bfloat16)] * 2,
        in_specs=[smem] * 4 + [vmem] * 4,
        out_specs=[vmem, vmem],
        scratch_shapes=[
            pltpu.VMEM((2 * rows, width), jnp.bfloat16),
            pltpu.VMEM((2 * rows + reach, width), jnp.bfloat16),
            pltpu.VMEM((2 * rows + reach, width), jnp.bfloat16),
        ],
        compiler_params=pltpu.CompilerParams(vmem_limit_bytes=48 * 1024 * 1024),
        name="project_attend",
    )(where, utt_start, stretch_utt, left_stretches, inputs, partner, halo, weights)
    other = lax.ppermute(partner_out, "tm", swap)
    left = jnp.where(core == 0, own_out, other)
    right = jnp.where(core == 0, other, own_out)
    return jnp.concatenate([left, right], axis=1)[None]


def solution(mesh):
    return jax.shard_map(
        local,
        mesh=mesh,
        in_specs=(P("dp", "tm", None), P("dp", None), P("dp", None), P("dp", None), P("dp", None)),
        out_specs=P("dp", "tm", None),
        check_vma=False,
    )
```

```python
import functools
import math

import jax
import jax.numpy as jnp
from jax import lax
from jax.experimental import pallas as pl
from jax.experimental.pallas import tpu as pltpu
from jax.sharding import PartitionSpec as P

HEAD_DIM = 96
STRETCH = 256
LEFT = 2
LANES = 128
GROUPS = 4
EXP_SCALE = HEAD_DIM**-0.5 * math.log2(math.e)
REACH = LEFT * STRETCH
MIB = 1024 * 1024


def dot(a, b, dims=((1,), (0,))):
    return lax.dot_general(a, b, (dims, ((), ())), preferred_element_type=jnp.float32)


def head_window(head):
    first = head * HEAD_DIM // LANES * LANES
    last = -(-(head + 1) * HEAD_DIM // LANES) * LANES
    return first, last


def start_all(sems, pairs):
    copies = [pltpu.make_async_copy(src, dst, sems.at[i]) for i, (src, dst) in enumerate(pairs)]
    for copy in copies:
        copy.start()
    return copies


def early_kernel(n_blocks, at_ref, *refs):
    blocks = refs[:n_blocks]
    own_ref, partner_ref, halo_ref, own_sum, partner_sum, halo_sum = refs[n_blocks : n_blocks + 6]
    w_s, own_s, partner_s, halo_s, sems = refs[n_blocks + 6 :]
    depth = w_s.shape[0]
    base = pl.multiple_of(at_ref[0], LANES)
    pairs = []
    for i, block in enumerate(blocks):
        rows = block.shape[0]
        pairs.append((block, w_s.at[pl.ds(pl.multiple_of(at_ref[1 + i], rows), rows)]))
    for src, dst in ((own_ref, own_s), (partner_ref, partner_s), (halo_ref, halo_s)):
        pairs.append((src.at[:, pl.ds(base, depth)], dst))
    for copy in start_all(sems, pairs):
        copy.wait()
    width = w_s.shape[1] // 3
    for x_s, out in ((own_s, own_sum), (partner_s, partner_sum)):
        for third in range(3):
            cols = slice(third * width, (third + 1) * width)
            out[:, cols] = dot(x_s[...], w_s[:, cols])
    for third in range(2):
        cols = slice(third * width, (third + 1) * width)
        halo_sum[:, cols] = dot(halo_s[...], w_s[:, width + third * width : width + (third + 1) * width])


def late_kernel(
    n_blocks, where_ref, at_ref, start_ref, owner_ref, left_ref, *refs,
):
    blocks = refs[:n_blocks]
    own_ref, partner_ref, halo_ref, own_sum, partner_sum, halo_sum = refs[n_blocks : n_blocks + 6]
    own_out, partner_out = refs[n_blocks + 6 : n_blocks + 8]
    (w_s, own_s, partner_s, halo_s, own_acc, partner_acc, halo_acc, q_s, k_s, v_s, sems) = refs[
        n_blocks + 8 :
    ]
    depth = w_s.shape[0]
    width = w_s.shape[1] // 3
    rows = own_s.shape[0]
    chunks = rows // STRETCH
    core = where_ref[0]
    pair = where_ref[1]
    base = pl.multiple_of(at_ref[0], LANES)
    pairs = []
    for i, block in enumerate(blocks):
        size = block.shape[0]
        pairs.append((block, w_s.at[pl.ds(pl.multiple_of(at_ref[1 + i], size), size)]))
    for src, dst in ((halo_ref, halo_s), (partner_ref, partner_s), (own_ref, own_s)):
        pairs.append((src.at[:, pl.ds(base, depth)], dst))
    for src, dst in ((halo_sum, halo_acc), (partner_sum, partner_acc), (own_sum, own_acc)):
        pairs.append((src, dst))
    copies = start_all(sems, pairs)
    for copy in copies[:n_blocks]:
        copy.wait()
    copies = copies[n_blocks:]

    copies[0].wait()
    copies[3].wait()
    for third, dst in ((0, k_s), (1, v_s)):
        cols = slice(width + third * width, width + (third + 1) * width)
        value = halo_acc[:, third * width : (third + 1) * width] + dot(halo_s[...], w_s[:, cols])
        dst[:REACH, :] = value.astype(jnp.bfloat16)
    for n, x_s, acc, place in ((1, partner_s, partner_acc, 1 - core), (2, own_s, own_acc, core)):
        copies[n].wait()
        copies[3 + n].wait()
        row = pl.multiple_of(place * rows, STRETCH)
        for third, dst, skip in ((0, q_s, 0), (1, k_s, REACH), (2, v_s, REACH)):
            cols = slice(third * width, (third + 1) * width)
            value = acc[:, cols] + dot(x_s[...], w_s[:, cols])
            dst[pl.ds(pl.multiple_of(row + skip, STRETCH), rows), :] = value.astype(jnp.bfloat16)

    lane = lax.broadcasted_iota(jnp.int32, (1, width), 1)

    def attend_block(chunk, start, lowest, q_row, k_row, span, out_ref, out_row):
        key_frame = (chunk + 1) * STRETCH - span + lax.broadcasted_iota(jnp.int32, (1, span), 1)
        bias = jnp.where(key_frame >= lowest, 0.0, -jnp.inf).astype(jnp.float32)
        frame = chunk * STRETCH + lax.broadcasted_iota(jnp.int32, (STRETCH, 1), 0)
        live = frame >= start
        tiles = [jnp.zeros((STRETCH, LANES), jnp.float32) for _ in range(width // LANES)]
        for head in range(width // HEAD_DIM):
            first, last = head_window(head)
            inside = (lane >= head * HEAD_DIM) & (lane < (head + 1) * HEAD_DIM)
            inside = inside[:, first:last]
            q = q_s[pl.ds(q_row, STRETCH), first:last]
            q = jnp.where(inside, q, jnp.zeros_like(q))
            k = k_s[pl.ds(k_row, span), first:last]
            scores = dot(q, k, ((1,), (1,))) + bias
            top = jnp.max(scores, axis=-1, keepdims=True)
            expo = jnp.exp2((scores - top) * EXP_SCALE)
            total = jnp.sum(expo, axis=-1, keepdims=True)
            probs = (expo * (1.0 / total)).astype(jnp.bfloat16)
            mixed = dot(probs, v_s[pl.ds(k_row, span), first:last])
            for tile in range(first // LANES, last // LANES):
                at = tile * LANES - first
                tiles[tile] = jnp.where(
                    inside[:, at : at + LANES], mixed[:, at : at + LANES], tiles[tile]
                )
        for tile, value in enumerate(tiles):
            value = jnp.where(live, value, 0.0).astype(jnp.bfloat16)
            out_ref[pl.ds(out_row, STRETCH), tile * LANES : (tile + 1) * LANES] = value

    def attend(place, out_ref):
        @pl.loop(0, chunks)
        def _(i):
            out_row = pl.multiple_of(i * STRETCH, STRETCH)
            q_row = pl.multiple_of(place * rows + out_row, STRETCH)
            chunk = (pair * 2 + place) * chunks + i
            left = left_ref[0, chunk]
            start = start_ref[0, owner_ref[0, chunk]]
            lowest = jnp.maximum((chunk - left) * STRETCH, start)
            for back in range(LEFT + 1):

                @pl.when(left == back)
                def _():
                    k_row = pl.multiple_of(q_row + (LEFT - back) * STRETCH, STRETCH)
                    span = (back + 1) * STRETCH
                    attend_block(chunk, start, lowest, q_row, k_row, span, out_ref, out_row)

    attend(1 - core, partner_out)
    attend(core, own_out)


def project_early(at, blocks, inputs, partner, halo, depth):
    rows = inputs.shape[0]
    cols = blocks[0].shape[1]
    anywhere = pl.BlockSpec(memory_space=pl.ANY)
    return pl.pallas_call(
        functools.partial(early_kernel, len(blocks)),
        out_shape=[
            jax.ShapeDtypeStruct((rows, cols), jnp.float32),
            jax.ShapeDtypeStruct((rows, cols), jnp.float32),
            jax.ShapeDtypeStruct((REACH, cols // 3 * 2), jnp.float32),
        ],
        in_specs=[pl.BlockSpec(memory_space=pltpu.SMEM)] + [anywhere] * (len(blocks) + 3),
        out_specs=[pl.BlockSpec(memory_space=pltpu.VMEM)] * 3,
        scratch_shapes=[
            pltpu.VMEM((depth, cols), jnp.bfloat16),
            pltpu.VMEM((rows, depth), jnp.bfloat16),
            pltpu.VMEM((rows, depth), jnp.bfloat16),
            pltpu.VMEM((REACH, depth), jnp.bfloat16),
            pltpu.SemaphoreType.DMA((len(blocks) + 3,)),
        ],
        compiler_params=pltpu.CompilerParams(vmem_limit_bytes=44 * MIB),
        name="project_early",
    )(at, *blocks, inputs, partner, halo)


def project_late_attend(where, at, tables, blocks, inputs, partner, halo, sums, depth):
    rows = inputs.shape[0]
    cols = blocks[0].shape[1]
    width = cols // 3
    smem = pl.BlockSpec(memory_space=pltpu.SMEM)
    anywhere = pl.BlockSpec(memory_space=pl.ANY)
    vmem = pl.BlockSpec(memory_space=pltpu.VMEM)
    return pl.pallas_call(
        functools.partial(late_kernel, len(blocks)),
        out_shape=[jax.ShapeDtypeStruct((rows, width), jnp.bfloat16)] * 2,
        in_specs=[smem] * 5 + [anywhere] * (len(blocks) + 6),
        out_specs=[vmem, vmem],
        scratch_shapes=[
            pltpu.VMEM((depth, cols), jnp.bfloat16),
            pltpu.VMEM((rows, depth), jnp.bfloat16),
            pltpu.VMEM((rows, depth), jnp.bfloat16),
            pltpu.VMEM((REACH, depth), jnp.bfloat16),
            pltpu.VMEM((rows, cols), jnp.float32),
            pltpu.VMEM((rows, cols), jnp.float32),
            pltpu.VMEM((REACH, 2 * width), jnp.float32),
            pltpu.VMEM((2 * rows, width), jnp.bfloat16),
            pltpu.VMEM((2 * rows + REACH, width), jnp.bfloat16),
            pltpu.VMEM((2 * rows + REACH, width), jnp.bfloat16),
            pltpu.SemaphoreType.DMA((len(blocks) + 6,)),
        ],
        compiler_params=pltpu.CompilerParams(vmem_limit_bytes=44 * MIB),
        name="project_late_attend",
    )(where, at, *tables, *blocks, inputs, partner, halo, *sums)


def gather_neighbours(half):
    index = lax.axis_index("dp")
    place, side = index // 2, index % 2
    is_end = (place == 0) | (place == 3)

    def along(block, hops):
        return lax.ppermute(
            block, "dp", [(2 * a + s, 2 * b + s) for a, b in hops for s in range(2)]
        )

    def across(block):
        return lax.ppermute(block, "dp", [(i, i ^ 1) for i in range(8)])

    outward = [(1, 0), (2, 3)]
    middle = [(1, 2), (2, 1)]
    near = along(half, outward + [(0, 1), (3, 2)])
    mid = along(half, middle)
    half_across = across(half)
    mid_far = along(near, middle)
    near_across = across(near)
    end_mid = along(mid, outward)
    second = jnp.where(is_end, end_mid, mid)
    second_across = across(second)
    end_far = along(mid_far, outward)
    third = jnp.where(is_end, end_far, mid_far)
    third_across = across(third)
    places = [place, place ^ 1, 3 - (place ^ 1), 3 - place]
    order = [jnp.where(is_end, a, b) for a, b in zip(places, [place, place ^ 1, 3 - place, 3 - (place ^ 1)])]
    found = [half, half_across, near, near_across, second, second_across, third, third_across]
    indices = []
    for spot in order:
        indices += [2 * spot + side, 2 * spot + 1 - side]
    return found, indices


def local(frames, w_qkv, utt_start, stretch_utt, left_stretches):
    inputs = frames[0]
    rows, depth = inputs.shape
    size = w_qkv.shape[0]
    inner = w_qkv.shape[1] // 3
    width = inner // 2
    members = lax.axis_size("tm")
    place = lax.axis_index("tm")
    core = place % 2
    pair = place // 2

    thirds = [w_qkv[:, i * inner : (i + 1) * inner] for i in range(3)]
    half = jnp.concatenate(
        [jnp.where(core == 0, third[:, :width], third[:, width:]) for third in thirds], axis=1
    )

    late_depth = depth // GROUPS
    early_depth = depth - late_depth
    if lax.axis_size("dp") == 8:
        blocks, indices = gather_neighbours(half)
        n_early = len(blocks) // GROUPS * (GROUPS - 1)
        early_blocks, late_blocks = blocks[:n_early], blocks[n_early:]
        late_first = jnp.minimum(indices[-1], indices[-2]) * size
        early_first = jnp.where(late_first == 0, late_depth, 0)
        early_at = [early_first] + [i * size - early_first for i in indices[:n_early]]
        late_at = [late_first] + [i * size - late_first for i in indices[n_early:]]
    else:
        weights = lax.all_gather(half, "dp", axis=0, tiled=True)
        early_blocks, late_blocks = [weights[:early_depth]], [weights[early_depth:]]
        early_at, late_at = [0, 0], [early_depth, 0]
    early_at = jnp.stack([jnp.asarray(i, jnp.int32) for i in early_at])
    late_at = jnp.stack([jnp.asarray(i, jnp.int32) for i in late_at])

    swap = [(i, i ^ 1) for i in range(members)]
    halo = lax.ppermute(
        inputs[rows - REACH :], "tm", [(i, i + 1) for i in range(1, members - 1, 2)]
    )
    partner = lax.ppermute(inputs, "tm", swap)
    halo_odd = lax.ppermute(halo, "tm", [(i, i + 1) for i in range(0, members, 2)])
    halo = jnp.where(core == 0, halo, halo_odd)

    where = jnp.stack([core, pair]).astype(jnp.int32)
    tables = (utt_start, stretch_utt, left_stretches)
    sums = project_early(early_at, early_blocks, inputs, partner, halo, early_depth)
    sums = [sums[0], sums[1], sums[2]]
    own_out, partner_out = project_late_attend(
        where, late_at, tables, late_blocks, inputs, partner, halo, sums, late_depth
    )
    other = lax.ppermute(partner_out, "tm", swap)
    left = jnp.where(core == 0, own_out, other)
    right = jnp.where(core == 0, other, own_out)
    return jnp.concatenate([left, right], axis=1)[None]


def solution(mesh):
    return jax.shard_map(
        local,
        mesh=mesh,
        in_specs=(P("dp", "tm", None), P("dp", None), P("dp", None), P("dp", None), P("dp", None)),
        out_specs=P("dp", "tm", None),
        check_vma=False,
    )
```

```python
import functools
import math

import jax
import jax.numpy as jnp
from jax import lax
from jax.experimental import pallas as pl
from jax.experimental.pallas import tpu as pltpu
from jax.sharding import PartitionSpec as P

HEAD_DIM = 96
STRETCH = 256
LEFT = 2
LANES = 128
GROUPS = 4
EXP_SCALE = HEAD_DIM**-0.5 * math.log2(math.e)
REACH = LEFT * STRETCH
MIB = 1024 * 1024


def dot(a, b, dims=((1,), (0,))):
    return lax.dot_general(a, b, (dims, ((), ())), preferred_element_type=jnp.float32)


def head_window(head):
    first = head * HEAD_DIM // LANES * LANES
    last = -(-(head + 1) * HEAD_DIM // LANES) * LANES
    return first, last


def start_all(sems, pairs):
    copies = []
    for i, (src, dst) in enumerate(pairs):
        if isinstance(src, tuple):
            choices, which = src
            for n, choice in enumerate(choices):
                copy = pltpu.make_async_copy(choice, dst, sems.at[i])
                pl.when(which == n)(copy.start)
        else:
            copy = pltpu.make_async_copy(src, dst, sems.at[i])
            copy.start()
        copies.append(copy)
    return copies


def early_kernel(n_blocks, where_ref, at_ref, *refs):
    blocks = refs[:n_blocks]
    own_ref, partner_ref, *halo_refs = refs[n_blocks : n_blocks + 4]
    own_sum, partner_sum, halo_sum = refs[n_blocks + 4 : n_blocks + 7]
    w_s, own_s, partner_s, halo_s, sems = refs[n_blocks + 7 :]
    depth = w_s.shape[0]
    base = pl.multiple_of(at_ref[0], LANES)
    pairs = []
    for i, block in enumerate(blocks):
        rows = block.shape[0]
        pairs.append((block, w_s.at[pl.ds(pl.multiple_of(at_ref[1 + i], rows), rows)]))
    columns = pl.ds(base, depth)
    pairs.append((own_ref.at[:, columns], own_s))
    pairs.append((partner_ref.at[:, columns], partner_s))
    pairs.append((([ref.at[:, columns] for ref in halo_refs], where_ref[0]), halo_s))
    for copy in start_all(sems, pairs):
        copy.wait()
    width = w_s.shape[1] // 3
    for x_s, out in ((own_s, own_sum), (partner_s, partner_sum)):
        for third in range(3):
            cols = slice(third * width, (third + 1) * width)
            out[:, cols] = dot(x_s[...], w_s[:, cols])
    for third in range(2):
        cols = slice(third * width, (third + 1) * width)
        halo_sum[:, cols] = dot(halo_s[...], w_s[:, width + third * width : width + (third + 1) * width])


def late_kernel(
    n_blocks, where_ref, at_ref, start_ref, owner_ref, left_ref, *refs,
):
    blocks = refs[:n_blocks]
    own_ref, partner_ref, *halo_refs = refs[n_blocks : n_blocks + 4]
    own_sum, partner_sum, halo_sum = refs[n_blocks + 4 : n_blocks + 7]
    own_out, partner_out = refs[n_blocks + 7 : n_blocks + 9]
    (w_s, own_s, partner_s, halo_s, own_acc, partner_acc, halo_acc, q_s, k_s, v_s, sems) = refs[
        n_blocks + 9 :
    ]
    depth = w_s.shape[0]
    width = w_s.shape[1] // 3
    rows = own_s.shape[0]
    chunks = rows // STRETCH
    core = where_ref[0]
    pair = where_ref[1]
    base = pl.multiple_of(at_ref[0], LANES)
    pairs = []
    for i, block in enumerate(blocks):
        size = block.shape[0]
        pairs.append((block, w_s.at[pl.ds(pl.multiple_of(at_ref[1 + i], size), size)]))
    columns = pl.ds(base, depth)
    pairs.append((([ref.at[:, columns] for ref in halo_refs], core), halo_s))
    pairs.append((partner_ref.at[:, columns], partner_s))
    pairs.append((own_ref.at[:, columns], own_s))
    for src, dst in ((halo_sum, halo_acc), (partner_sum, partner_acc), (own_sum, own_acc)):
        pairs.append((src, dst))
    copies = start_all(sems, pairs)
    for copy in copies[:n_blocks]:
        copy.wait()
    copies = copies[n_blocks:]

    copies[0].wait()
    copies[3].wait()
    keys, values = (
        (halo_acc[:, i * width : (i + 1) * width] + dot(halo_s[...], w_s[:, cols])).astype(jnp.bfloat16)
        for i, cols in enumerate((slice(width, 2 * width), slice(2 * width, 3 * width)))
    )
    k_s[:REACH, :] = keys
    v_s[:, :REACH] = values.T
    for n, x_s, acc, place in ((1, partner_s, partner_acc, 1 - core), (2, own_s, own_acc, core)):
        copies[n].wait()
        copies[3 + n].wait()
        row = pl.multiple_of(place * rows, STRETCH)
        after = pl.multiple_of(row + REACH, STRETCH)
        query, keys, values = (
            (acc[:, cols] + dot(x_s[...], w_s[:, cols])).astype(jnp.bfloat16)
            for cols in (slice(i * width, (i + 1) * width) for i in range(3))
        )
        q_s[pl.ds(row, rows), :] = query
        k_s[pl.ds(after, rows), :] = keys
        v_s[:, pl.ds(after, rows)] = values.T

    lane = lax.broadcasted_iota(jnp.int32, (1, width), 1)
    key_row = lax.broadcasted_iota(jnp.int32, (STRETCH, STRETCH), 0)
    query_lane = lax.broadcasted_iota(jnp.int32, (1, STRETCH), 1)

    def attend_block(chunk, start, lowest, q_row, k_row, span, out_ref, out_row):
        first_key = (chunk + 1) * STRETCH - span
        allowed = key_row >= lowest - first_key
        live = query_lane >= start - chunk * STRETCH
        outs = []
        for head in range(width // HEAD_DIM):
            first, last = head_window(head)
            inside = (lane >= head * HEAD_DIM) & (lane < (head + 1) * HEAD_DIM)
            q = q_s[pl.ds(q_row, STRETCH), first:last]
            q = jnp.where(inside[:, first:last], q, jnp.zeros_like(q))
            k = k_s[pl.ds(k_row, span), first:last]
            scores = dot(k, q, ((1,), (1,)))
            masked = jnp.where(allowed, scores[:STRETCH], -jnp.inf)
            if span > STRETCH:
                masked = jnp.concatenate([masked, scores[STRETCH:]], axis=0)
            scores = masked
            top = jnp.max(scores, axis=0, keepdims=True)
            expo = jnp.exp2((scores - top) * EXP_SCALE)
            total = jnp.sum(expo, axis=0, keepdims=True)
            probs = (expo * (1.0 / total)).astype(jnp.bfloat16)
            values = v_s[head * HEAD_DIM : (head + 1) * HEAD_DIM, pl.ds(k_row, span)]
            outs.append(dot(values, probs))
        out = jnp.where(live, jnp.concatenate(outs, axis=0), 0.0)
        out_ref[pl.ds(out_row, STRETCH), :] = out.T.astype(jnp.bfloat16)

    def attend(place, out_ref):
        @pl.loop(0, chunks)
        def _(i):
            out_row = pl.multiple_of(i * STRETCH, STRETCH)
            q_row = pl.multiple_of(place * rows + out_row, STRETCH)
            chunk = (pair * 2 + place) * chunks + i
            left = left_ref[0, chunk]
            start = start_ref[0, owner_ref[0, chunk]]
            lowest = jnp.maximum((chunk - left) * STRETCH, start)
            for back in range(LEFT + 1):

                @pl.when(left == back)
                def _():
                    k_row = pl.multiple_of(q_row + (LEFT - back) * STRETCH, STRETCH)
                    span = (back + 1) * STRETCH
                    attend_block(chunk, start, lowest, q_row, k_row, span, out_ref, out_row)

    attend(1 - core, partner_out)
    attend(core, own_out)


def half_kernel(core_ref, w_ref, out_ref, sems):
    width = out_ref.shape[1] // 3
    pairs = []
    for third in range(3):
        at = pl.multiple_of((2 * third + core_ref[0]) * width, LANES)
        pairs.append((w_ref.at[:, pl.ds(at, width)], out_ref.at[:, third * width : (third + 1) * width]))
    for copy in start_all(sems, pairs):
        copy.wait()


def tail_kernel(x_ref, out_ref, sems):
    rows = out_ref.shape[0]
    for copy in start_all(sems, [(x_ref.at[x_ref.shape[0] - rows :, :], out_ref)]):
        copy.wait()


def take_half(core, w):
    anywhere = pl.BlockSpec(memory_space=pl.ANY)
    return pl.pallas_call(
        half_kernel,
        out_shape=jax.ShapeDtypeStruct((w.shape[0], w.shape[1] // 2), w.dtype),
        in_specs=[pl.BlockSpec(memory_space=pltpu.SMEM), anywhere],
        out_specs=anywhere,
        scratch_shapes=[pltpu.SemaphoreType.DMA((3,))],
        name="take_half",
    )(core[None], w)


def take_tail(x):
    anywhere = pl.BlockSpec(memory_space=pl.ANY)
    return pl.pallas_call(
        tail_kernel,
        out_shape=jax.ShapeDtypeStruct((REACH, x.shape[1]), x.dtype),
        in_specs=[anywhere],
        out_specs=anywhere,
        scratch_shapes=[pltpu.SemaphoreType.DMA((1,))],
        name="take_tail",
    )(x)


def after(value, *others):
    return lax.optimization_barrier((value, *others))[0]


def project_early(where, at, blocks, inputs, partner, halos, depth):
    rows = inputs.shape[0]
    cols = blocks[0].shape[1]
    anywhere = pl.BlockSpec(memory_space=pl.ANY)
    return pl.pallas_call(
        functools.partial(early_kernel, len(blocks)),
        out_shape=[
            jax.ShapeDtypeStruct((rows, cols), jnp.float32),
            jax.ShapeDtypeStruct((rows, cols), jnp.float32),
            jax.ShapeDtypeStruct((REACH, cols // 3 * 2), jnp.float32),
        ],
        in_specs=[pl.BlockSpec(memory_space=pltpu.SMEM)] * 2 + [anywhere] * (len(blocks) + 4),
        out_specs=[pl.BlockSpec(memory_space=pltpu.VMEM)] * 3,
        scratch_shapes=[
            pltpu.VMEM((depth, cols), jnp.bfloat16),
            pltpu.VMEM((rows, depth), jnp.bfloat16),
            pltpu.VMEM((rows, depth), jnp.bfloat16),
            pltpu.VMEM((REACH, depth), jnp.bfloat16),
            pltpu.SemaphoreType.DMA((len(blocks) + 3,)),
        ],
        compiler_params=pltpu.CompilerParams(vmem_limit_bytes=44 * MIB),
        name="project_early",
    )(where, at, *blocks, inputs, partner, *halos)


def project_late_attend(where, at, tables, blocks, inputs, partner, halos, sums, depth):
    rows = inputs.shape[0]
    cols = blocks[0].shape[1]
    width = cols // 3
    smem = pl.BlockSpec(memory_space=pltpu.SMEM)
    anywhere = pl.BlockSpec(memory_space=pl.ANY)
    vmem = pl.BlockSpec(memory_space=pltpu.VMEM)
    return pl.pallas_call(
        functools.partial(late_kernel, len(blocks)),
        out_shape=[jax.ShapeDtypeStruct((rows, width), jnp.bfloat16)] * 2,
        in_specs=[smem] * 5 + [anywhere] * (len(blocks) + 7),
        out_specs=[vmem, vmem],
        scratch_shapes=[
            pltpu.VMEM((depth, cols), jnp.bfloat16),
            pltpu.VMEM((rows, depth), jnp.bfloat16),
            pltpu.VMEM((rows, depth), jnp.bfloat16),
            pltpu.VMEM((REACH, depth), jnp.bfloat16),
            pltpu.VMEM((rows, cols), jnp.float32),
            pltpu.VMEM((rows, cols), jnp.float32),
            pltpu.VMEM((REACH, 2 * width), jnp.float32),
            pltpu.VMEM((2 * rows, width), jnp.bfloat16),
            pltpu.VMEM((2 * rows + REACH, width), jnp.bfloat16),
            pltpu.VMEM((width, 2 * rows + REACH), jnp.bfloat16),
            pltpu.SemaphoreType.DMA((len(blocks) + 6,)),
        ],
        compiler_params=pltpu.CompilerParams(vmem_limit_bytes=44 * MIB),
        name="project_late_attend",
    )(where, at, *tables, *blocks, inputs, partner, *halos, *sums)


def gather_neighbours(half):
    index = lax.axis_index("dp")
    place, side = index // 2, index % 2
    is_end = (place == 0) | (place == 3)

    def along(block, hops):
        return lax.ppermute(
            block, "dp", [(2 * a + s, 2 * b + s) for a, b in hops for s in range(2)]
        )

    def across(block):
        return lax.ppermute(block, "dp", [(i, i ^ 1) for i in range(8)])

    outward = [(1, 0), (2, 3)]
    middle = [(1, 2), (2, 1)]
    near = along(half, outward + [(0, 1), (3, 2)])
    mid = along(half, middle)
    half_across = across(half)
    mid_far = along(near, middle)
    near_across = across(after(near, half_across))
    end_mid = along(mid, outward)
    second = jnp.where(is_end, end_mid, mid)
    second_across = across(after(second, near_across))
    end_far = along(mid_far, outward)
    third = jnp.where(is_end, end_far, mid_far)
    third_across = across(after(third, second_across))
    places = [place, place ^ 1, 3 - (place ^ 1), 3 - place]
    order = [jnp.where(is_end, a, b) for a, b in zip(places, [place, place ^ 1, 3 - place, 3 - (place ^ 1)])]
    found = [half, half_across, near, near_across, second, second_across, third, third_across]
    indices = []
    for spot in order:
        indices += [2 * spot + side, 2 * spot + 1 - side]
    return found, indices


def local(frames, w_qkv, utt_start, stretch_utt, left_stretches):
    inputs = frames[0]
    rows, depth = inputs.shape
    size = w_qkv.shape[0]
    members = lax.axis_size("tm")
    place = lax.axis_index("tm")
    core = place % 2
    pair = place // 2

    half = take_half(core, w_qkv)

    late_depth = depth // GROUPS
    early_depth = depth - late_depth
    if lax.axis_size("dp") == 8:
        blocks, indices = gather_neighbours(half)
        mark = blocks[3]
        n_early = len(blocks) // GROUPS * (GROUPS - 1)
        early_blocks, late_blocks = blocks[:n_early], blocks[n_early:]
        late_first = jnp.minimum(indices[-1], indices[-2]) * size
        early_first = jnp.where(late_first == 0, late_depth, 0)
        early_at = [early_first] + [i * size - early_first for i in indices[:n_early]]
        late_at = [late_first] + [i * size - late_first for i in indices[n_early:]]
    else:
        weights = lax.all_gather(half, "dp", axis=0, tiled=True)
        mark = half
        early_blocks, late_blocks = [weights[:early_depth]], [weights[early_depth:]]
        early_at, late_at = [0, 0], [early_depth, 0]
    early_at = jnp.stack([jnp.asarray(i, jnp.int32) for i in early_at])
    late_at = jnp.stack([jnp.asarray(i, jnp.int32) for i in late_at])

    swap = [(i, i ^ 1) for i in range(members)]
    halo = lax.ppermute(
        take_tail(after(inputs, half)), "tm", [(i, i + 1) for i in range(1, members - 1, 2)]
    )
    partner = lax.ppermute(inputs, "tm", swap)
    halo_odd = lax.ppermute(after(halo, mark), "tm", [(i, i + 1) for i in range(0, members, 2)])
    halos = (halo, halo_odd)

    where = jnp.stack([core, pair]).astype(jnp.int32)
    tables = (utt_start, stretch_utt, left_stretches)
    sums = project_early(where, early_at, early_blocks, inputs, partner, halos, early_depth)
    own_out, partner_out = project_late_attend(
        where, late_at, tables, late_blocks, inputs, partner, halos, sums, late_depth
    )
    other = lax.ppermute(partner_out, "tm", swap)
    left = jnp.where(core == 0, own_out, other)
    right = jnp.where(core == 0, other, own_out)
    return jnp.concatenate([left, right], axis=1)[None]


def solution(mesh):
    return jax.shard_map(
        local,
        mesh=mesh,
        in_specs=(P("dp", "tm", None), P("dp", None), P("dp", None), P("dp", None), P("dp", None)),
        out_specs=P("dp", "tm", None),
        check_vma=False,
    )
```

```python
import functools
import math

import jax
import jax.numpy as jnp
from jax import lax
from jax.experimental import pallas as pl
from jax.experimental.pallas import tpu as pltpu
from jax.sharding import PartitionSpec as P

HEAD_DIM = 96
STRETCH = 256
LEFT = 2
LANES = 128
GROUPS = 4
EXP_SCALE = HEAD_DIM**-0.5 * math.log2(math.e)
REACH = LEFT * STRETCH
MIB = 1024 * 1024


def dot(a, b, dims=((1,), (0,))):
    return lax.dot_general(a, b, (dims, ((), ())), preferred_element_type=jnp.float32)


def head_window(head):
    first = head * HEAD_DIM // LANES * LANES
    last = -(-(head + 1) * HEAD_DIM // LANES) * LANES
    return first, last


def start_all(sems, pairs):
    copies = []
    for i, (*source, target) in enumerate(pairs):
        if len(source) == 1:
            copy = pltpu.make_async_copy(source[0], target, sems.at[i])
            copy.start()
        else:
            for n, choice in enumerate(source[0]):
                copy = pltpu.make_async_copy(choice, target, sems.at[i])
                pl.when(source[1] == n)(copy.start)
        copies.append(copy)
    return copies


def early_kernel(n_blocks, at_ref, *refs):
    blocks = refs[:n_blocks]
    own_ref, partner_ref, own_sum, partner_sum, w_s, own_s, partner_s, sems = refs[n_blocks:]
    depth = w_s.shape[0]
    pairs = place_blocks(at_ref, blocks, w_s)
    columns = pl.ds(pl.multiple_of(at_ref[0], LANES), depth)
    pairs.append((own_ref.at[:, columns], own_s))
    pairs.append((partner_ref.at[:, columns], partner_s))
    for copy in start_all(sems, pairs):
        copy.wait()
    width = w_s.shape[1] // 3
    for x_s, out in ((own_s, own_sum), (partner_s, partner_sum)):
        for third in range(3):
            cols = slice(third * width, (third + 1) * width)
            out[:, cols] = dot(x_s[...], w_s[:, cols])


def place_blocks(at_ref, blocks, target, first=1, columns=slice(None)):
    pairs = []
    for i, block in enumerate(blocks):
        rows = block.shape[0]
        at = pl.multiple_of(at_ref[first + i], rows)
        pairs.append((block.at[:, columns], target.at[pl.ds(at, rows)]))
    return pairs


def late_kernel(
    n_blocks, n_late, where_ref, at_ref, start_ref, owner_ref, left_ref, *refs,
):
    blocks = refs[:n_blocks]
    own_ref, partner_ref, *halo_refs = refs[n_blocks : n_blocks + 4]
    own_sum, partner_sum, own_out, partner_out = refs[n_blocks + 4 : n_blocks + 8]
    (w_s, kv_s, halo_s, own_s, partner_s, own_acc, partner_acc, q_s, k_s, v_s, sems) = refs[
        n_blocks + 8 :
    ]
    depth = w_s.shape[0]
    width = w_s.shape[1] // 3
    rows = own_s.shape[0]
    chunks = rows // STRETCH
    core = where_ref[0]
    pair = where_ref[1]
    pairs = place_blocks(at_ref, blocks, kv_s, 1 + n_late, slice(width, 3 * width))
    pairs.append(([ref.at[rows - REACH :, :] for ref in halo_refs], core, halo_s))
    n_first = len(pairs)
    pairs += place_blocks(at_ref, blocks[n_blocks - n_late :], w_s)
    columns = pl.ds(pl.multiple_of(at_ref[0], LANES), depth)
    pairs.append((partner_ref.at[:, columns], partner_s))
    pairs.append((partner_sum, partner_acc))
    n_second = len(pairs)
    pairs.append((own_ref.at[:, columns], own_s))
    pairs.append((own_sum, own_acc))
    copies = start_all(sems, pairs)

    for copy in copies[:n_first]:
        copy.wait()
    k_s[:REACH, :] = dot(halo_s[...], kv_s[:, :width]).astype(jnp.bfloat16)
    v_s[:REACH, :] = dot(halo_s[...], kv_s[:, width:]).astype(jnp.bfloat16)
    for waits, x_s, acc, place in (
        (copies[n_first:n_second], partner_s, partner_acc, 1 - core),
        (copies[n_second:], own_s, own_acc, core),
    ):
        for copy in waits:
            copy.wait()
        row = pl.multiple_of(place * rows, STRETCH)
        for third, dst, skip in ((0, q_s, 0), (1, k_s, REACH), (2, v_s, REACH)):
            cols = slice(third * width, (third + 1) * width)
            value = acc[:, cols] + dot(x_s[...], w_s[:, cols])
            dst[pl.ds(pl.multiple_of(row + skip, STRETCH), rows), :] = value.astype(jnp.bfloat16)

    lane = lax.broadcasted_iota(jnp.int32, (1, width), 1)
    heads = width // HEAD_DIM

    def attend_block(chunk, start, lowest, q_row, k_row, span, out_ref, out_row):
        first_key = (chunk + 1) * STRETCH - span
        key_frame = first_key + lax.broadcasted_iota(jnp.int32, (1, STRETCH), 1)
        bias = jnp.where(key_frame >= lowest, 0.0, -jnp.inf).astype(jnp.float32)
        frame = chunk * STRETCH + lax.broadcasted_iota(jnp.int32, (STRETCH, 1), 0)
        live = frame >= start
        windows = [head_window(head) for head in range(heads)]
        insides = [
            ((lane >= head * HEAD_DIM) & (lane < (head + 1) * HEAD_DIM))[:, first:last]
            for head, (first, last) in enumerate(windows)
        ]
        tiles = [jnp.zeros((STRETCH, LANES), jnp.float32) for _ in range(width // LANES)]

        def score(head):
            first, last = windows[head]
            q = q_s[pl.ds(q_row, STRETCH), first:last]
            q = jnp.where(insides[head], q, jnp.zeros_like(q))
            return dot(q, k_s[pl.ds(k_row, span), first:last], ((1,), (1,)))

        def weigh(scores):
            scores = [scores[:, at : at + STRETCH] for at in range(0, span, STRETCH)]
            scores[0] = scores[0] + bias
            top = functools.reduce(jnp.maximum, scores)
            top = jnp.max(top, axis=-1, keepdims=True)
            expo = [jnp.exp2((part - top) * EXP_SCALE) for part in scores]
            total = jnp.sum(functools.reduce(jnp.add, expo), axis=-1, keepdims=True)
            share = 1.0 / total
            return jnp.concatenate([(part * share).astype(jnp.bfloat16) for part in expo], axis=1)

        def mix(head, probs):
            first, last = windows[head]
            mixed = dot(probs, v_s[pl.ds(k_row, span), first:last])
            for tile in range(first // LANES, last // LANES):
                at = tile * LANES - first
                tiles[tile] = jnp.where(
                    insides[head][:, at : at + LANES], mixed[:, at : at + LANES], tiles[tile]
                )

        scores = score(0)
        probs = None
        for head in range(heads):
            following = score(head + 1) if head + 1 < heads else None
            weighed = weigh(scores)
            if probs is not None:
                mix(head - 1, probs)
            scores, probs = following, weighed
        mix(heads - 1, probs)
        for tile, value in enumerate(tiles):
            value = jnp.where(live, value, 0.0).astype(jnp.bfloat16)
            out_ref[pl.ds(out_row, STRETCH), tile * LANES : (tile + 1) * LANES] = value

    def attend(place, out_ref):
        @pl.loop(0, chunks)
        def _(i):
            out_row = pl.multiple_of(i * STRETCH, STRETCH)
            q_row = pl.multiple_of(place * rows + out_row, STRETCH)
            chunk = (pair * 2 + place) * chunks + i
            left = left_ref[0, chunk]
            start = start_ref[0, owner_ref[0, chunk]]
            lowest = jnp.maximum((chunk - left) * STRETCH, start)
            for back in range(LEFT + 1):

                @pl.when(left == back)
                def _():
                    k_row = pl.multiple_of(q_row + (LEFT - back) * STRETCH, STRETCH)
                    span = (back + 1) * STRETCH
                    attend_block(chunk, start, lowest, q_row, k_row, span, out_ref, out_row)

    attend(1 - core, partner_out)
    attend(core, own_out)


def after(value, *others):
    return lax.optimization_barrier((value, *others))[0]


def project_early(at, blocks, inputs, partner, depth):
    rows = inputs.shape[0]
    cols = blocks[0].shape[1]
    anywhere = pl.BlockSpec(memory_space=pl.ANY)
    return pl.pallas_call(
        functools.partial(early_kernel, len(blocks)),
        out_shape=[jax.ShapeDtypeStruct((rows, cols), jnp.float32)] * 2,
        in_specs=[pl.BlockSpec(memory_space=pltpu.SMEM)] + [anywhere] * (len(blocks) + 2),
        out_specs=[pl.BlockSpec(memory_space=pltpu.VMEM)] * 2,
        scratch_shapes=[
            pltpu.VMEM((depth, cols), jnp.bfloat16),
            pltpu.VMEM((rows, depth), jnp.bfloat16),
            pltpu.VMEM((rows, depth), jnp.bfloat16),
            pltpu.SemaphoreType.DMA((len(blocks) + 2,)),
        ],
        compiler_params=pltpu.CompilerParams(vmem_limit_bytes=40 * MIB),
        name="project_early",
    )(at, *blocks, inputs, partner)


def project_late_attend(where, at, tables, blocks, n_late, inputs, partner, halos, sums, late_depth):
    rows, depth = inputs.shape
    cols = blocks[0].shape[1]
    width = cols // 3
    smem = pl.BlockSpec(memory_space=pltpu.SMEM)
    anywhere = pl.BlockSpec(memory_space=pl.ANY)
    vmem = pl.BlockSpec(memory_space=pltpu.VMEM)
    return pl.pallas_call(
        functools.partial(late_kernel, len(blocks), n_late),
        out_shape=[jax.ShapeDtypeStruct((rows, width), jnp.bfloat16)] * 2,
        in_specs=[smem] * 5 + [anywhere] * (len(blocks) + 6),
        out_specs=[vmem, vmem],
        scratch_shapes=[
            pltpu.VMEM((late_depth, cols), jnp.bfloat16),
            pltpu.VMEM((depth, 2 * width), jnp.bfloat16),
            pltpu.VMEM((REACH, depth), jnp.bfloat16),
            pltpu.VMEM((rows, late_depth), jnp.bfloat16),
            pltpu.VMEM((rows, late_depth), jnp.bfloat16),
            pltpu.VMEM((rows, cols), jnp.float32),
            pltpu.VMEM((rows, cols), jnp.float32),
            pltpu.VMEM((2 * rows, width), jnp.bfloat16),
            pltpu.VMEM((2 * rows + REACH, width), jnp.bfloat16),
            pltpu.VMEM((2 * rows + REACH, width), jnp.bfloat16),
            pltpu.SemaphoreType.DMA((len(blocks) + n_late + 5,)),
        ],
        compiler_params=pltpu.CompilerParams(vmem_limit_bytes=40 * MIB),
        name="project_late_attend",
    )(where, at, *tables, *blocks, inputs, partner, *halos, *sums)


def gather_neighbours(half):
    index = lax.axis_index("dp")
    place, side = index // 2, index % 2
    is_end = (place == 0) | (place == 3)

    def along(block, hops):
        return lax.ppermute(
            block, "dp", [(2 * a + s, 2 * b + s) for a, b in hops for s in range(2)]
        )

    def across(block):
        return lax.ppermute(block, "dp", [(i, i ^ 1) for i in range(8)])

    outward = [(1, 0), (2, 3)]
    middle = [(1, 2), (2, 1)]
    near = along(half, outward + [(0, 1), (3, 2)])
    mid = along(half, middle)
    half_across = across(half)
    mid_far = along(near, middle)
    near_across = across(after(near, half_across))
    end_mid = along(mid, outward)
    second = jnp.where(is_end, end_mid, mid)
    second_across = across(after(second, near_across, mid_far))
    end_far = along(mid_far, outward)
    third = jnp.where(is_end, end_far, mid_far)
    third_across = across(after(third, second_across))
    places = [place, place ^ 1, 3 - (place ^ 1), 3 - place]
    order = [jnp.where(is_end, a, b) for a, b in zip(places, [place, place ^ 1, 3 - place, 3 - (place ^ 1)])]
    found = [half, half_across, near, near_across, second, second_across, third, third_across]
    indices = []
    for spot in order:
        indices += [2 * spot + side, 2 * spot + 1 - side]
    return found, indices, ((near_across,), (second_across, end_far))


def local(frames, w_qkv, utt_start, stretch_utt, left_stretches):
    inputs = frames[0]
    rows, depth = inputs.shape
    size = w_qkv.shape[0]
    members = lax.axis_size("tm")
    place = lax.axis_index("tm")
    core = place % 2
    pair = place // 2

    inner = w_qkv.shape[1] // 3
    width = inner // 2
    thirds = [w_qkv[:, i * inner : (i + 1) * inner] for i in range(3)]
    half = jnp.concatenate(
        [jnp.where(core == 0, third[:, :width], third[:, width:]) for third in thirds], axis=1
    )

    late_depth = depth // GROUPS
    early_depth = depth - late_depth
    if lax.axis_size("dp") == 8:
        blocks, indices, marks = gather_neighbours(half)
        n_early = len(blocks) // GROUPS * (GROUPS - 1)
        early_blocks, late_blocks = blocks[:n_early], blocks[n_early:]
        late_first = jnp.minimum(indices[-1], indices[-2]) * size
        early_first = jnp.where(late_first == 0, late_depth, 0)
        early_at = [early_first] + [i * size - early_first for i in indices[:n_early]]
        late_at = [late_first] + [i * size - late_first for i in indices[n_early:]]
        late_at += [i * size for i in indices]
    else:
        weights = lax.all_gather(half, "dp", axis=0, tiled=True)
        marks = (half,), (half,)
        early_blocks, late_blocks = [weights[:early_depth]], [weights[early_depth:]]
        blocks = early_blocks + late_blocks
        early_at, late_at = [0, 0], [early_depth, 0, 0, early_depth]
    early_at = jnp.stack([jnp.asarray(i, jnp.int32) for i in early_at])
    late_at = jnp.stack([jnp.asarray(i, jnp.int32) for i in late_at])

    swap = [(i, i ^ 1) for i in range(members)]
    halo = lax.ppermute(inputs, "tm", [(i, i + 1) for i in range(1, members - 1, 2)])
    partner = lax.ppermute(after(inputs, *marks[0]), "tm", swap)
    halo_odd = lax.ppermute(
        after(halo, *marks[1]), "tm", [(i, i + 1) for i in range(0, members, 2)]
    )
    halos = (halo, halo_odd)

    where = jnp.stack([core, pair]).astype(jnp.int32)
    tables = (utt_start, stretch_utt, left_stretches)
    sums = project_early(early_at, early_blocks, inputs, partner, early_depth)
    own_out, partner_out = project_late_attend(
        where, late_at, tables, blocks, len(late_blocks), inputs, partner, halos, sums, late_depth
    )
    other = lax.ppermute(partner_out, "tm", swap)
    left = jnp.where(core == 0, own_out, other)
    right = jnp.where(core == 0, other, own_out)
    return jnp.concatenate([left, right], axis=1)[None]


def solution(mesh):
    return jax.shard_map(
        local,
        mesh=mesh,
        in_specs=(P("dp", "tm", None), P("dp", None), P("dp", None), P("dp", None), P("dp", None)),
        out_specs=P("dp", "tm", None),
        check_vma=False,
    )
```

```python
import functools
import math

import jax
import jax.numpy as jnp
from jax import lax
from jax.experimental import pallas as pl
from jax.experimental.pallas import tpu as pltpu
from jax.sharding import PartitionSpec as P

HEAD_DIM = 96
STRETCH = 256
LEFT = 2
LANES = 128
GROUPS = 4
EXP_SCALE = HEAD_DIM**-0.5 * math.log2(math.e)
REACH = LEFT * STRETCH
MIB = 1024 * 1024


def dot(a, b, dims=((1,), (0,))):
    return lax.dot_general(a, b, (dims, ((), ())), preferred_element_type=jnp.float32)


def head_window(head):
    first = head * HEAD_DIM // LANES * LANES
    last = -(-(head + 1) * HEAD_DIM // LANES) * LANES
    return first, last


def start_all(sems, pairs):
    copies = []
    for i, (*source, target) in enumerate(pairs):
        if len(source) == 1:
            copy = pltpu.make_async_copy(source[0], target, sems.at[i])
            copy.start()
        else:
            for n, choice in enumerate(source[0]):
                copy = pltpu.make_async_copy(choice, target, sems.at[i])
                pl.when(source[1] == n)(copy.start)
        copies.append(copy)
    return copies


def early_kernel(n_blocks, at_ref, *refs):
    blocks = refs[:n_blocks]
    own_ref, partner_ref, own_sum, partner_sum, w_s, own_s, partner_s, sems = refs[n_blocks:]
    depth = w_s.shape[0]
    pairs = place_blocks(at_ref, blocks, w_s)
    columns = pl.ds(pl.multiple_of(at_ref[0], LANES), depth)
    pairs.append((own_ref.at[:, columns], own_s))
    pairs.append((partner_ref.at[:, columns], partner_s))
    for copy in start_all(sems, pairs):
        copy.wait()
    width = w_s.shape[1] // 3
    for x_s, out in ((own_s, own_sum), (partner_s, partner_sum)):
        for third in range(3):
            cols = slice(third * width, (third + 1) * width)
            out[:, cols] = dot(x_s[...], w_s[:, cols])


def place_blocks(at_ref, blocks, target, first=1, columns=slice(None)):
    pairs = []
    for i, block in enumerate(blocks):
        rows = block.shape[0]
        at = pl.multiple_of(at_ref[first + i], rows)
        pairs.append((block.at[:, columns], target.at[pl.ds(at, rows)]))
    return pairs


def late_kernel(
    n_blocks, n_late, where_ref, at_ref, start_ref, owner_ref, left_ref, *refs,
):
    blocks = refs[:n_blocks]
    own_ref, partner_ref, *halo_refs = refs[n_blocks : n_blocks + 4]
    own_sum, partner_sum, partner_out, q_own, k_out, v_out = refs[n_blocks + 4 : n_blocks + 10]
    w_s, kv_s, halo_s, own_s, partner_s, q_partner, sems = refs[n_blocks + 10 :]
    depth = w_s.shape[0]
    width = w_s.shape[1] // 3
    rows = own_s.shape[0]
    core = where_ref[0]
    pairs = place_blocks(at_ref, blocks, kv_s, 1 + n_late, slice(width, 3 * width))
    pairs.append(([ref.at[ref.shape[0] - REACH :, :] for ref in halo_refs], core, halo_s))
    n_first = len(pairs)
    pairs += place_blocks(at_ref, blocks[n_blocks - n_late :], w_s)
    columns = pl.ds(pl.multiple_of(at_ref[0], LANES), depth)
    pairs.append((partner_ref.at[:, columns], partner_s))
    pairs.append((own_ref.at[:, columns], own_s))
    copies = start_all(sems, pairs)

    for copy in copies[:n_first]:
        copy.wait()
    k_out[:REACH, :] = dot(halo_s[...], kv_s[:, :width]).astype(jnp.bfloat16)
    v_out[:REACH, :] = dot(halo_s[...], kv_s[:, width:]).astype(jnp.bfloat16)
    for copy in copies[n_first:]:
        copy.wait()
    for x_s, acc, query, place in (
        (partner_s, partner_sum, q_partner, 1 - core),
        (own_s, own_sum, q_own, core),
    ):
        row = pl.multiple_of(place * rows + REACH, STRETCH)
        for third, dst in enumerate((query, k_out, v_out)):
            cols = slice(third * width, (third + 1) * width)
            value = (acc[:, cols] + dot(x_s[...], w_s[:, cols])).astype(jnp.bfloat16)
            if third == 0:
                dst[...] = value
            else:
                dst[pl.ds(row, rows), :] = value
    attend(where_ref, start_ref, owner_ref, left_ref, 1 - core, q_partner, k_out, v_out, partner_out)


def own_kernel(where_ref, start_ref, owner_ref, left_ref, q_ref, k_ref, v_ref, out_ref):
    attend(where_ref, start_ref, owner_ref, left_ref, where_ref[0], q_ref, k_ref, v_ref, out_ref)


def attend(where_ref, start_ref, owner_ref, left_ref, place, q_s, k_s, v_s, out_ref):
    rows, width = out_ref.shape
    chunks = rows // STRETCH
    pair = where_ref[1]
    lane = lax.broadcasted_iota(jnp.int32, (1, width), 1)
    heads = width // HEAD_DIM

    def attend_block(chunk, start, lowest, q_row, k_row, span, out_ref, out_row):
        first_key = (chunk + 1) * STRETCH - span
        key_frame = first_key + lax.broadcasted_iota(jnp.int32, (1, STRETCH), 1)
        bias = jnp.where(key_frame >= lowest, 0.0, -jnp.inf).astype(jnp.float32)
        frame = chunk * STRETCH + lax.broadcasted_iota(jnp.int32, (STRETCH, 1), 0)
        live = frame >= start
        windows = [head_window(head) for head in range(heads)]
        insides = [
            ((lane >= head * HEAD_DIM) & (lane < (head + 1) * HEAD_DIM))[:, first:last]
            for head, (first, last) in enumerate(windows)
        ]
        tiles = [jnp.zeros((STRETCH, LANES), jnp.float32) for _ in range(width // LANES)]

        def score(head):
            first, last = windows[head]
            q = q_s[pl.ds(q_row, STRETCH), first:last]
            q = jnp.where(insides[head], q, jnp.zeros_like(q))
            return dot(q, k_s[pl.ds(k_row, span), first:last], ((1,), (1,)))

        def weigh(scores):
            scores = [scores[:, at : at + STRETCH] for at in range(0, span, STRETCH)]
            scores[0] = scores[0] + bias
            top = functools.reduce(jnp.maximum, scores)
            top = jnp.max(top, axis=-1, keepdims=True)
            expo = [jnp.exp2((part - top) * EXP_SCALE) for part in scores]
            total = jnp.sum(functools.reduce(jnp.add, expo), axis=-1, keepdims=True)
            share = 1.0 / total
            return jnp.concatenate([(part * share).astype(jnp.bfloat16) for part in expo], axis=1)

        def mix(head, probs):
            first, last = windows[head]
            mixed = dot(probs, v_s[pl.ds(k_row, span), first:last])
            for tile in range(first // LANES, last // LANES):
                at = tile * LANES - first
                tiles[tile] = jnp.where(
                    insides[head][:, at : at + LANES], mixed[:, at : at + LANES], tiles[tile]
                )

        scores = score(0)
        probs = None
        for head in range(heads):
            following = score(head + 1) if head + 1 < heads else None
            weighed = weigh(scores)
            if probs is not None:
                mix(head - 1, probs)
            scores, probs = following, weighed
        mix(heads - 1, probs)
        for tile, value in enumerate(tiles):
            value = jnp.where(live, value, 0.0).astype(jnp.bfloat16)
            out_ref[pl.ds(out_row, STRETCH), tile * LANES : (tile + 1) * LANES] = value

    @pl.loop(0, chunks)
    def _(i):
        row = pl.multiple_of(i * STRETCH, STRETCH)
        chunk = (pair * 2 + place) * chunks + i
        left = left_ref[0, chunk]
        start = start_ref[0, owner_ref[0, chunk]]
        lowest = jnp.maximum((chunk - left) * STRETCH, start)
        for back in range(LEFT + 1):

            @pl.when(left == back)
            def _():
                k_row = pl.multiple_of(place * rows + row + (LEFT - back) * STRETCH, STRETCH)
                attend_block(chunk, start, lowest, row, k_row, (back + 1) * STRETCH, out_ref, row)


def after(value, *others):
    return lax.optimization_barrier((value, *others))[0]


def project_early(at, blocks, inputs, partner, depth):
    rows = inputs.shape[0]
    cols = blocks[0].shape[1]
    anywhere = pl.BlockSpec(memory_space=pl.ANY)
    return pl.pallas_call(
        functools.partial(early_kernel, len(blocks)),
        out_shape=[jax.ShapeDtypeStruct((rows, cols), jnp.float32)] * 2,
        in_specs=[pl.BlockSpec(memory_space=pltpu.SMEM)] + [anywhere] * (len(blocks) + 2),
        out_specs=[pl.BlockSpec(memory_space=pltpu.VMEM)] * 2,
        scratch_shapes=[
            pltpu.VMEM((depth, cols), jnp.bfloat16),
            pltpu.VMEM((rows, depth), jnp.bfloat16),
            pltpu.VMEM((rows, depth), jnp.bfloat16),
            pltpu.SemaphoreType.DMA((len(blocks) + 2,)),
        ],
        compiler_params=pltpu.CompilerParams(vmem_limit_bytes=24 * MIB),
        cost_estimate=pl.CostEstimate(
            flops=4 * rows * depth * cols,
            bytes_accessed=2 * depth * (2 * rows + cols) + 8 * rows * cols,
            transcendentals=0,
        ),
        name="project_early",
    )(at, *blocks, inputs, partner)


def project_late_attend(where, at, tables, blocks, n_late, inputs, partner, halos, sums, late_depth):
    rows, depth = inputs.shape
    cols = blocks[0].shape[1]
    width = cols // 3
    smem = pl.BlockSpec(memory_space=pltpu.SMEM)
    anywhere = pl.BlockSpec(memory_space=pl.ANY)
    vmem = pl.BlockSpec(memory_space=pltpu.VMEM)
    return pl.pallas_call(
        functools.partial(late_kernel, len(blocks), n_late),
        out_shape=[
            jax.ShapeDtypeStruct((rows, width), jnp.bfloat16),
            jax.ShapeDtypeStruct((rows, width), jnp.bfloat16),
            jax.ShapeDtypeStruct((2 * rows + REACH, width), jnp.bfloat16),
            jax.ShapeDtypeStruct((2 * rows + REACH, width), jnp.bfloat16),
        ],
        in_specs=[smem] * 5 + [anywhere] * (len(blocks) + 4) + [vmem] * 2,
        out_specs=[vmem] * 4,
        scratch_shapes=[
            pltpu.VMEM((late_depth, cols), jnp.bfloat16),
            pltpu.VMEM((depth, 2 * width), jnp.bfloat16),
            pltpu.VMEM((REACH, depth), jnp.bfloat16),
            pltpu.VMEM((rows, late_depth), jnp.bfloat16),
            pltpu.VMEM((rows, late_depth), jnp.bfloat16),
            pltpu.VMEM((rows, width), jnp.bfloat16),
            pltpu.SemaphoreType.DMA((len(blocks) + n_late + 3,)),
        ],
        compiler_params=pltpu.CompilerParams(vmem_limit_bytes=24 * MIB),
        name="project_late_attend",
    )(where, at, *tables, *blocks, inputs, partner, *halos, *sums)


def attend_own(where, tables, query, keys, values):
    smem = pl.BlockSpec(memory_space=pltpu.SMEM)
    vmem = pl.BlockSpec(memory_space=pltpu.VMEM)
    return pl.pallas_call(
        own_kernel,
        out_shape=jax.ShapeDtypeStruct(query.shape, jnp.bfloat16),
        in_specs=[smem] * 4 + [vmem] * 3,
        out_specs=vmem,
        compiler_params=pltpu.CompilerParams(vmem_limit_bytes=20 * MIB),
        name="attend_own",
    )(where, *tables, query, keys, values)


def gather_neighbours(half):
    index = lax.axis_index("dp")
    place, side = index // 2, index % 2
    is_end = (place == 0) | (place == 3)

    def along(block, hops):
        return lax.ppermute(
            block, "dp", [(2 * a + s, 2 * b + s) for a, b in hops for s in range(2)]
        )

    def across(block):
        return lax.ppermute(block, "dp", [(i, i ^ 1) for i in range(8)])

    outward = [(1, 0), (2, 3)]
    middle = [(1, 2), (2, 1)]
    near = along(half, outward + [(0, 1), (3, 2)])
    mid = along(half, middle)
    half_across = across(half)
    mid_far = along(near, middle)
    near_across = across(after(near, half_across, mid))
    end_mid = along(mid, outward)
    second = jnp.where(is_end, end_mid, mid)
    second_across = across(after(second, near_across, mid_far))
    end_far = along(mid_far, outward)
    third = jnp.where(is_end, end_far, mid_far)
    third_across = across(after(third, second_across))
    places = [place, place ^ 1, 3 - (place ^ 1), 3 - place]
    order = [jnp.where(is_end, a, b) for a, b in zip(places, [place, place ^ 1, 3 - place, 3 - (place ^ 1)])]
    found = [half, half_across, near, near_across, second, second_across, third, third_across]
    indices = []
    for spot in order:
        indices += [2 * spot + side, 2 * spot + 1 - side]
    return found, indices, ((near_across, mid_far, end_mid), (second_across, end_far))


def local(frames, w_qkv, utt_start, stretch_utt, left_stretches):
    inputs = frames[0]
    rows, depth = inputs.shape
    size = w_qkv.shape[0]
    members = lax.axis_size("tm")
    place = lax.axis_index("tm")
    core = place % 2
    pair = place // 2

    inner = w_qkv.shape[1] // 3
    width = inner // 2
    thirds = [w_qkv[:, i * inner : (i + 1) * inner] for i in range(3)]
    half = jnp.concatenate(
        [jnp.where(core == 0, third[:, :width], third[:, width:]) for third in thirds], axis=1
    )

    late_depth = depth // GROUPS
    early_depth = depth - late_depth
    if lax.axis_size("dp") == 8:
        blocks, indices, marks = gather_neighbours(half)
        n_early = len(blocks) // GROUPS * (GROUPS - 1)
        early_blocks, late_blocks = blocks[:n_early], blocks[n_early:]
        late_first = jnp.minimum(indices[-1], indices[-2]) * size
        early_first = jnp.where(late_first == 0, late_depth, 0)
        early_at = [early_first] + [i * size - early_first for i in indices[:n_early]]
        late_at = [late_first] + [i * size - late_first for i in indices[n_early:]]
        late_at += [i * size for i in indices]
    else:
        weights = lax.all_gather(half, "dp", axis=0, tiled=True)
        marks = ((half,), (half,))
        early_blocks, late_blocks = [weights[:early_depth]], [weights[early_depth:]]
        blocks = early_blocks + late_blocks
        early_at, late_at = [0, 0], [early_depth, 0, 0, early_depth]
    early_at = jnp.stack([jnp.asarray(i, jnp.int32) for i in early_at])
    late_at = jnp.stack([jnp.asarray(i, jnp.int32) for i in late_at])

    swap = [(i, i ^ 1) for i in range(members)]
    halo = lax.ppermute(inputs, "tm", [(i, i + 1) for i in range(1, members - 1, 2)])
    partner = lax.ppermute(after(inputs, *marks[0]), "tm", swap)
    halo_odd = lax.ppermute(
        after(halo, *marks[1])[rows - REACH :], "tm", [(i, i + 1) for i in range(0, members, 2)]
    )
    halos = (halo, halo_odd)

    where = jnp.stack([core, pair]).astype(jnp.int32)
    tables = (utt_start, stretch_utt, left_stretches)
    sums = project_early(early_at, early_blocks, inputs, partner, early_depth)
    partner_out, query, keys, values = project_late_attend(
        where, late_at, tables, blocks, len(late_blocks), inputs, partner, halos, sums, late_depth
    )
    other = lax.ppermute(partner_out, "tm", swap)
    own_out = attend_own(where, tables, query, keys, values)
    left = jnp.where(core == 0, own_out, other)
    right = jnp.where(core == 0, other, own_out)
    return jnp.concatenate([left, right], axis=1)[None]


def solution(mesh):
    return jax.shard_map(
        local,
        mesh=mesh,
        in_specs=(P("dp", "tm", None), P("dp", None), P("dp", None), P("dp", None), P("dp", None)),
        out_specs=P("dp", "tm", None),
        check_vma=False,
    )
```

```python
import functools
import math

import jax
import jax.numpy as jnp
from jax import lax
from jax.experimental import pallas as pl
from jax.experimental.pallas import tpu as pltpu
from jax.sharding import PartitionSpec as P

HEAD_DIM = 96
STRETCH = 256
LEFT = 2
LANES = 128
GROUPS = 4
EXP_SCALE = HEAD_DIM**-0.5 * math.log2(math.e)
REACH = LEFT * STRETCH
MIB = 1024 * 1024


def dot(a, b, dims=((1,), (0,))):
    return lax.dot_general(a, b, (dims, ((), ())), preferred_element_type=jnp.float32)


def head_window(head):
    first = head * HEAD_DIM // LANES * LANES
    last = -(-(head + 1) * HEAD_DIM // LANES) * LANES
    return first, last


def start_all(sems, pairs):
    copies = []
    for i, (*source, target) in enumerate(pairs):
        if len(source) == 1:
            copy = pltpu.make_async_copy(source[0], target, sems.at[i])
            copy.start()
        else:
            for n, choice in enumerate(source[0]):
                copy = pltpu.make_async_copy(choice, target, sems.at[i])
                pl.when(source[1] == n)(copy.start)
        copies.append(copy)
    return copies


class Blocks:
    def __init__(self, blocks, n_late, find):
        self.operands = [operand for block in blocks for operand in block]
        self.counts = [len(block) for block in blocks]
        self.rows = [block[0].shape[0] for block in blocks]
        self.n_late = n_late
        self.early_operands = self.operands[: sum(self.counts[:-n_late])]
        self.find = find

    def copies(self, refs, found, members, target, first=0, columns=slice(None)):
        pairs = []
        for i in members:
            at = sum(self.counts[:i])
            choices = [ref.at[:, columns] for ref in refs[at : at + self.counts[i]]]
            row, which = found[i]
            goal = target.at[pl.ds(pl.multiple_of(row - first, self.rows[i]), self.rows[i])]
            pairs.append((choices[0], goal) if len(choices) == 1 else (choices, which, goal))
        return pairs


def early_kernel(blocks, *refs):
    n = len(blocks.early_operands)
    own_ref, partner_ref, own_sum, partner_sum, w_s, own_s, partner_s, sems = refs[n:]
    found, late_first = blocks.find()
    depth = w_s.shape[0]
    first = jnp.where(late_first == 0, own_ref.shape[1] - depth, 0)
    members = range(len(found) - blocks.n_late)
    pairs = blocks.copies(refs, found, members, w_s, first)
    columns = pl.ds(pl.multiple_of(first, LANES), depth)
    pairs.append((own_ref.at[:, columns], own_s))
    pairs.append((partner_ref.at[:, columns], partner_s))
    for copy in start_all(sems, pairs):
        copy.wait()
    width = w_s.shape[1] // 3
    for x_s, out in ((own_s, own_sum), (partner_s, partner_sum)):
        for third in range(3):
            cols = slice(third * width, (third + 1) * width)
            out[:, cols] = dot(x_s[...], w_s[:, cols])


def late_kernel(blocks, start_ref, owner_ref, left_ref, *refs):
    n = len(blocks.operands)
    own_ref, partner_ref, *halo_refs = refs[n : n + 4]
    own_sum, partner_sum, partner_out, q_own, k_out, v_out = refs[n + 4 : n + 10]
    w_s, kv_s, halo_s, own_s, partner_s, q_partner, sems = refs[n + 10 :]
    depth = w_s.shape[0]
    width = w_s.shape[1] // 3
    rows = own_s.shape[0]
    core = lax.axis_index("tm") % 2
    found, late_first = blocks.find()
    everything = range(len(found))
    pairs = blocks.copies(refs, found, everything, kv_s, 0, slice(width, 3 * width))
    pairs.append(([ref.at[rows - REACH :, :] for ref in halo_refs], core, halo_s))
    n_first = len(pairs)
    pairs += blocks.copies(refs, found, everything[-blocks.n_late :], w_s, late_first)
    columns = pl.ds(pl.multiple_of(late_first, LANES), depth)
    pairs.append((partner_ref.at[:, columns], partner_s))
    pairs.append((own_ref.at[:, columns], own_s))
    copies = start_all(sems, pairs)

    for copy in copies[:n_first]:
        copy.wait()
    k_out[:REACH, :] = dot(halo_s[...], kv_s[:, :width]).astype(jnp.bfloat16)
    v_out[:REACH, :] = dot(halo_s[...], kv_s[:, width:]).astype(jnp.bfloat16)
    for copy in copies[n_first:]:
        copy.wait()
    for x_s, acc, query, place in (
        (partner_s, partner_sum, q_partner, 1 - core),
        (own_s, own_sum, q_own, core),
    ):
        row = pl.multiple_of(place * rows + REACH, STRETCH)
        for third, dst in enumerate((query, k_out, v_out)):
            cols = slice(third * width, (third + 1) * width)
            value = (acc[:, cols] + dot(x_s[...], w_s[:, cols])).astype(jnp.bfloat16)
            if third == 0:
                dst[...] = value
            else:
                dst[pl.ds(row, rows), :] = value
    attend(start_ref, owner_ref, left_ref, 1 - core, q_partner, k_out, v_out, partner_out)


def own_kernel(start_ref, owner_ref, left_ref, q_ref, k_ref, v_ref, out_ref):
    core = lax.axis_index("tm") % 2
    attend(start_ref, owner_ref, left_ref, core, q_ref, k_ref, v_ref, out_ref)


def attend(start_ref, owner_ref, left_ref, place, q_s, k_s, v_s, out_ref):
    rows, width = out_ref.shape
    chunks = rows // STRETCH
    pair = lax.axis_index("tm") // 2
    lane = lax.broadcasted_iota(jnp.int32, (1, width), 1)
    heads = width // HEAD_DIM

    def attend_block(chunk, start, lowest, q_row, k_row, span, out_ref, out_row):
        first_key = (chunk + 1) * STRETCH - span
        key_frame = first_key + lax.broadcasted_iota(jnp.int32, (1, STRETCH), 1)
        bias = jnp.where(key_frame >= lowest, 0.0, -jnp.inf).astype(jnp.float32)
        frame = chunk * STRETCH + lax.broadcasted_iota(jnp.int32, (STRETCH, 1), 0)
        live = frame >= start
        windows = [head_window(head) for head in range(heads)]
        insides = [
            ((lane >= head * HEAD_DIM) & (lane < (head + 1) * HEAD_DIM))[:, first:last]
            for head, (first, last) in enumerate(windows)
        ]
        tiles = [jnp.zeros((STRETCH, LANES), jnp.float32) for _ in range(width // LANES)]

        def score(head):
            first, last = windows[head]
            q = q_s[pl.ds(q_row, STRETCH), first:last]
            q = jnp.where(insides[head], q, jnp.zeros_like(q))
            return dot(q, k_s[pl.ds(k_row, span), first:last], ((1,), (1,)))

        def weigh(scores):
            scores = [scores[:, at : at + STRETCH] for at in range(0, span, STRETCH)]
            scores[0] = scores[0] + bias
            top = functools.reduce(jnp.maximum, scores)
            top = jnp.max(top, axis=-1, keepdims=True)
            expo = [jnp.exp2((part - top) * EXP_SCALE) for part in scores]
            total = jnp.sum(functools.reduce(jnp.add, expo), axis=-1, keepdims=True)
            share = 1.0 / total
            return jnp.concatenate([(part * share).astype(jnp.bfloat16) for part in expo], axis=1)

        def mix(head, probs):
            first, last = windows[head]
            mixed = dot(probs, v_s[pl.ds(k_row, span), first:last])
            for tile in range(first // LANES, last // LANES):
                at = tile * LANES - first
                tiles[tile] = jnp.where(
                    insides[head][:, at : at + LANES], mixed[:, at : at + LANES], tiles[tile]
                )

        scores = score(0)
        probs = None
        for head in range(heads):
            following = score(head + 1) if head + 1 < heads else None
            weighed = weigh(scores)
            if probs is not None:
                mix(head - 1, probs)
            scores, probs = following, weighed
        mix(heads - 1, probs)
        for tile, value in enumerate(tiles):
            value = jnp.where(live, value, 0.0).astype(jnp.bfloat16)
            out_ref[pl.ds(out_row, STRETCH), tile * LANES : (tile + 1) * LANES] = value

    @pl.loop(0, chunks)
    def _(i):
        row = pl.multiple_of(i * STRETCH, STRETCH)
        chunk = (pair * 2 + place) * chunks + i
        left = left_ref[0, chunk]
        start = start_ref[0, owner_ref[0, chunk]]
        lowest = jnp.maximum((chunk - left) * STRETCH, start)
        for back in range(LEFT + 1):

            @pl.when(left == back)
            def _():
                k_row = pl.multiple_of(place * rows + row + (LEFT - back) * STRETCH, STRETCH)
                attend_block(chunk, start, lowest, row, k_row, (back + 1) * STRETCH, out_ref, row)


def after(value, *others):
    return lax.optimization_barrier((value, *others))[0]


SMEM_SPEC = pl.BlockSpec(memory_space=pltpu.SMEM)
VMEM_SPEC = pl.BlockSpec(memory_space=pltpu.VMEM)
ANY_SPEC = pl.BlockSpec(memory_space=pl.ANY)


def project_early(blocks, inputs, partner):
    rows, depth = inputs.shape
    depth -= depth // GROUPS
    cols = blocks.operands[0].shape[1]
    n_copies = len(blocks.counts) - blocks.n_late + 2
    return pl.pallas_call(
        functools.partial(early_kernel, blocks),
        out_shape=[jax.ShapeDtypeStruct((rows, cols), jnp.float32)] * 2,
        in_specs=[ANY_SPEC] * (len(blocks.early_operands) + 2),
        out_specs=[VMEM_SPEC] * 2,
        scratch_shapes=[
            pltpu.VMEM((depth, cols), jnp.bfloat16),
            pltpu.VMEM((rows, depth), jnp.bfloat16),
            pltpu.VMEM((rows, depth), jnp.bfloat16),
            pltpu.SemaphoreType.DMA((n_copies,)),
        ],
        compiler_params=pltpu.CompilerParams(vmem_limit_bytes=24 * MIB),
        cost_estimate=pl.CostEstimate(
            flops=4 * rows * depth * cols,
            bytes_accessed=2 * depth * (2 * rows + cols) + 8 * rows * cols,
            transcendentals=0,
        ),
        name="project_early",
    )(*blocks.early_operands, inputs, partner)


def project_late_attend(tables, blocks, inputs, partner, halos, sums):
    rows, depth = inputs.shape
    late_depth = depth // GROUPS
    cols = blocks.operands[0].shape[1]
    width = cols // 3
    return pl.pallas_call(
        functools.partial(late_kernel, blocks),
        out_shape=[
            jax.ShapeDtypeStruct((rows, width), jnp.bfloat16),
            jax.ShapeDtypeStruct((rows, width), jnp.bfloat16),
            jax.ShapeDtypeStruct((2 * rows + REACH, width), jnp.bfloat16),
            jax.ShapeDtypeStruct((2 * rows + REACH, width), jnp.bfloat16),
        ],
        in_specs=[SMEM_SPEC] * 3 + [ANY_SPEC] * (len(blocks.operands) + 4) + [VMEM_SPEC] * 2,
        out_specs=[VMEM_SPEC] * 4,
        scratch_shapes=[
            pltpu.VMEM((late_depth, cols), jnp.bfloat16),
            pltpu.VMEM((depth, 2 * width), jnp.bfloat16),
            pltpu.VMEM((REACH, depth), jnp.bfloat16),
            pltpu.VMEM((rows, late_depth), jnp.bfloat16),
            pltpu.VMEM((rows, late_depth), jnp.bfloat16),
            pltpu.VMEM((rows, width), jnp.bfloat16),
            pltpu.SemaphoreType.DMA((len(blocks.counts) + blocks.n_late + 3,)),
        ],
        compiler_params=pltpu.CompilerParams(vmem_limit_bytes=24 * MIB),
        name="project_late_attend",
    )(*tables, *blocks.operands, inputs, partner, *halos, *sums)


def attend_own(tables, query, keys, values):
    return pl.pallas_call(
        own_kernel,
        out_shape=jax.ShapeDtypeStruct(query.shape, jnp.bfloat16),
        in_specs=[SMEM_SPEC] * 3 + [VMEM_SPEC] * 3,
        out_specs=VMEM_SPEC,
        compiler_params=pltpu.CompilerParams(vmem_limit_bytes=20 * MIB),
        name="attend_own",
    )(*tables, query, keys, values)


def gather_neighbours(half):
    size = half.shape[0]

    def along(block, hops):
        return lax.ppermute(
            block, "dp", [(2 * a + s, 2 * b + s) for a, b in hops for s in range(2)]
        )

    def across(block, places):
        return lax.ppermute(block, "dp", [(2 * a + s, 2 * a + 1 - s) for a in places for s in range(2)])

    line, ends, middles = range(4), (0, 3), (1, 2)
    outward = [(1, 0), (2, 3)]
    between = [(1, 2), (2, 1)]
    near = along(half, outward + [(0, 1), (3, 2)])
    mid = along(half, between)
    half_across = across(half, line)
    mid_far = along(near, between)
    near_across = across(after(near, half_across, mid), line)
    end_mid = along(mid, outward)
    mid_across = across(after(mid, near_across, mid_far), middles)
    end_mid_across = across(after(end_mid, near_across), ends)
    end_far = along(mid_far, outward)
    mid_far_across = across(after(mid_far, mid_across, end_far), middles)
    end_far_across = across(after(end_far, end_mid_across), ends)

    def find():
        index = lax.axis_index("dp")
        place, side = index // 2, index % 2
        is_end = jnp.where((place == 0) | (place == 3), 1, 0)
        second = jnp.where(is_end == 1, place ^ 2, 3 - place)
        third = jnp.where(is_end == 1, 3 - place, place ^ 2)
        spots = (place, place ^ 1, second, third)
        found = [((2 * spot + (side ^ n)) * size, is_end) for spot in spots for n in range(2)]
        return found, third * 2 * size

    blocks = [
        (half,),
        (half_across,),
        (near,),
        (near_across,),
        (mid, end_mid),
        (mid_across, end_mid_across),
        (mid_far, end_far),
        (mid_far_across, end_far_across),
    ]
    marks = (near_across, mid_far, end_mid), (mid_across, end_mid_across, end_far)
    return Blocks(blocks, 2, find), marks


def local(frames, w_qkv, utt_start, stretch_utt, left_stretches):
    inputs = frames[0]
    depth = inputs.shape[1]
    members = lax.axis_size("tm")
    core = lax.axis_index("tm") % 2

    inner = w_qkv.shape[1] // 3
    width = inner // 2
    thirds = [w_qkv[:, i * inner : (i + 1) * inner] for i in range(3)]
    half = jnp.concatenate(
        [jnp.where(core == 0, third[:, :width], third[:, width:]) for third in thirds], axis=1
    )

    if lax.axis_size("dp") == 8:
        blocks, marks = gather_neighbours(half)
    else:
        weights = lax.all_gather(half, "dp", axis=0, tiled=True)
        late_first = depth - depth // GROUPS
        found = [(0, 0), (late_first, 0)], late_first
        parts = [(weights[:late_first],), (weights[late_first:],)]
        blocks, marks = Blocks(parts, 1, lambda: found), ((half,), (half,))

    swap = [(i, i ^ 1) for i in range(members)]
    halo = lax.ppermute(inputs, "tm", [(i, i + 1) for i in range(1, members - 1, 2)])
    partner = lax.ppermute(after(inputs, *marks[0]), "tm", swap)
    halo_odd = lax.ppermute(
        after(halo, *marks[1]), "tm", [(i, i + 1) for i in range(0, members, 2)]
    )

    tables = (utt_start, stretch_utt, left_stretches)
    sums = project_early(blocks, inputs, partner)
    partner_out, query, keys, values = project_late_attend(
        tables, blocks, inputs, partner, (halo, halo_odd), sums
    )
    other = lax.ppermute(partner_out, "tm", swap)
    own_out = attend_own(tables, query, keys, values)
    left = jnp.where(core == 0, own_out, other)
    right = jnp.where(core == 0, other, own_out)
    return jnp.concatenate([left, right], axis=1)[None]


def solution(mesh):
    return jax.shard_map(
        local,
        mesh=mesh,
        in_specs=(P("dp", "tm", None), P("dp", None), P("dp", None), P("dp", None), P("dp", None)),
        out_specs=P("dp", "tm", None),
        check_vma=False,
    )
```

```python
import functools
import math

import jax
import jax.numpy as jnp
from jax import lax
from jax.experimental import pallas as pl
from jax.experimental.pallas import tpu as pltpu
from jax.sharding import PartitionSpec as P

HEAD_DIM = 96
STRETCH = 256
LEFT = 2
LANES = 128
GROUPS = 4
EXP_SCALE = HEAD_DIM**-0.5 * math.log2(math.e)
REACH = LEFT * STRETCH
MIB = 1024 * 1024


def dot(a, b, dims=((1,), (0,))):
    return lax.dot_general(a, b, (dims, ((), ())), preferred_element_type=jnp.float32)


def head_window(head):
    first = head * HEAD_DIM // LANES * LANES
    last = -(-(head + 1) * HEAD_DIM // LANES) * LANES
    return first, last


def start_all(sems, pairs):
    copies = []
    for i, (*source, target) in enumerate(pairs):
        if len(source) == 1:
            copy = pltpu.make_async_copy(source[0], target, sems.at[i])
            copy.start()
        else:
            for n, choice in enumerate(source[0]):
                copy = pltpu.make_async_copy(choice, target, sems.at[i])
                pl.when(source[1] == n)(copy.start)
        copies.append(copy)
    return copies


class Blocks:
    def __init__(self, blocks, n_late, find):
        self.operands = [operand for block in blocks for operand in block]
        self.counts = [len(block) for block in blocks]
        self.rows = [block[0].shape[0] for block in blocks]
        self.n_late = n_late
        self.early_operands = self.operands[: sum(self.counts[:-n_late])]
        self.find = find

    def copies(self, refs, found, members, target, first=0, columns=slice(None)):
        pairs = []
        for i in members:
            at = sum(self.counts[:i])
            choices = [ref.at[:, columns] for ref in refs[at : at + self.counts[i]]]
            row, which = found[i]
            goal = target.at[pl.ds(pl.multiple_of(row - first, self.rows[i]), self.rows[i])]
            pairs.append((choices[0], goal) if len(choices) == 1 else (choices, which, goal))
        return pairs


def early_kernel(blocks, *refs):
    n = len(blocks.early_operands)
    own_ref, partner_ref, own_sum, partner_sum, w_s, own_s, partner_s, sems = refs[n:]
    found, late_first = blocks.find()
    depth = w_s.shape[0]
    first = jnp.where(late_first == 0, own_ref.shape[1] - depth, 0)
    members = range(len(found) - blocks.n_late)
    pairs = blocks.copies(refs, found, members, w_s, first)
    columns = pl.ds(pl.multiple_of(first, LANES), depth)
    pairs.append((own_ref.at[:, columns], own_s))
    pairs.append((partner_ref.at[:, columns], partner_s))
    for copy in start_all(sems, pairs):
        copy.wait()
    width = w_s.shape[1] // 3
    for x_s, out in ((own_s, own_sum), (partner_s, partner_sum)):
        for third in range(3):
            cols = slice(third * width, (third + 1) * width)
            out[:, cols] = dot(x_s[...], w_s[:, cols])


def late_kernel(blocks, start_ref, owner_ref, left_ref, *refs):
    n = len(blocks.operands)
    own_ref, partner_ref, *halo_refs = refs[n : n + 4]
    own_sum, partner_sum, partner_out, q_own, k_out, v_out = refs[n + 4 : n + 10]
    w_s, kv_s, halo_s, own_s, partner_s, q_partner, sems = refs[n + 10 :]
    depth = w_s.shape[0]
    width = w_s.shape[1] // 3
    rows = own_s.shape[0]
    core = lax.axis_index("tm") % 2
    found, late_first = blocks.find()
    everything = range(len(found))
    pairs = blocks.copies(refs, found, everything, kv_s, 0, slice(width, 3 * width))
    pairs.append((halo_refs, core, halo_s))
    n_first = len(pairs)
    pairs += blocks.copies(refs, found, everything[-blocks.n_late :], w_s, late_first)
    columns = pl.ds(pl.multiple_of(late_first, LANES), depth)
    pairs.append((partner_ref.at[:, columns], partner_s))
    pairs.append((own_ref.at[:, columns], own_s))
    copies = start_all(sems, pairs)

    for copy in copies[:n_first]:
        copy.wait()
    k_out[:REACH, :] = dot(halo_s[...], kv_s[:, :width]).astype(jnp.bfloat16)
    v_out[:REACH, :] = dot(halo_s[...], kv_s[:, width:]).astype(jnp.bfloat16)
    for copy in copies[n_first:]:
        copy.wait()
    for x_s, acc, query, place in (
        (partner_s, partner_sum, q_partner, 1 - core),
        (own_s, own_sum, q_own, core),
    ):
        row = pl.multiple_of(place * rows + REACH, STRETCH)
        for third, dst in enumerate((query, k_out, v_out)):
            cols = slice(third * width, (third + 1) * width)
            value = (acc[:, cols] + dot(x_s[...], w_s[:, cols])).astype(jnp.bfloat16)
            if third == 0:
                dst[...] = value
            else:
                dst[pl.ds(row, rows), :] = value
    attend(start_ref, owner_ref, left_ref, 1 - core, q_partner, k_out, v_out, partner_out)


def own_kernel(start_ref, owner_ref, left_ref, q_ref, k_ref, v_ref, out_ref):
    core = lax.axis_index("tm") % 2
    attend(start_ref, owner_ref, left_ref, core, q_ref, k_ref, v_ref, out_ref)


def attend(start_ref, owner_ref, left_ref, place, q_s, k_s, v_s, out_ref):
    rows, width = out_ref.shape
    chunks = rows // STRETCH
    pair = lax.axis_index("tm") // 2
    lane = lax.broadcasted_iota(jnp.int32, (1, width), 1)
    heads = width // HEAD_DIM

    def attend_block(chunk, start, lowest, q_row, k_row, span, out_ref, out_row):
        first_key = (chunk + 1) * STRETCH - span
        key_frame = first_key + lax.broadcasted_iota(jnp.int32, (1, STRETCH), 1)
        bias = jnp.where(key_frame >= lowest, 0.0, -jnp.inf).astype(jnp.float32)
        frame = chunk * STRETCH + lax.broadcasted_iota(jnp.int32, (STRETCH, 1), 0)
        live = frame >= start
        windows = [head_window(head) for head in range(heads)]
        insides = [
            ((lane >= head * HEAD_DIM) & (lane < (head + 1) * HEAD_DIM))[:, first:last]
            for head, (first, last) in enumerate(windows)
        ]
        tiles = [jnp.zeros((STRETCH, LANES), jnp.float32) for _ in range(width // LANES)]

        def score(head):
            first, last = windows[head]
            q = q_s[pl.ds(q_row, STRETCH), first:last]
            q = jnp.where(insides[head], q, jnp.zeros_like(q))
            return dot(q, k_s[pl.ds(k_row, span), first:last], ((1,), (1,)))

        def weigh(scores):
            scores = [scores[:, at : at + STRETCH] for at in range(0, span, STRETCH)]
            scores[0] = scores[0] + bias
            top = functools.reduce(jnp.maximum, scores)
            top = jnp.max(top, axis=-1, keepdims=True)
            expo = [jnp.exp2((part - top) * EXP_SCALE) for part in scores]
            total = jnp.sum(functools.reduce(jnp.add, expo), axis=-1, keepdims=True)
            share = 1.0 / total
            return jnp.concatenate([(part * share).astype(jnp.bfloat16) for part in expo], axis=1)

        def mix(head, probs):
            first, last = windows[head]
            mixed = dot(probs, v_s[pl.ds(k_row, span), first:last])
            for tile in range(first // LANES, last // LANES):
                at = tile * LANES - first
                tiles[tile] = jnp.where(
                    insides[head][:, at : at + LANES], mixed[:, at : at + LANES], tiles[tile]
                )

        scores = score(0)
        probs = None
        for head in range(heads):
            following = score(head + 1) if head + 1 < heads else None
            weighed = weigh(scores)
            if probs is not None:
                mix(head - 1, probs)
            scores, probs = following, weighed
        mix(heads - 1, probs)
        for tile, value in enumerate(tiles):
            value = jnp.where(live, value, 0.0).astype(jnp.bfloat16)
            out_ref[pl.ds(out_row, STRETCH), tile * LANES : (tile + 1) * LANES] = value

    @pl.loop(0, chunks)
    def _(i):
        row = pl.multiple_of(i * STRETCH, STRETCH)
        chunk = (pair * 2 + place) * chunks + i
        left = left_ref[0, chunk]
        start = start_ref[0, owner_ref[0, chunk]]
        lowest = jnp.maximum((chunk - left) * STRETCH, start)
        for back in range(LEFT + 1):

            @pl.when(left == back)
            def _():
                k_row = pl.multiple_of(place * rows + row + (LEFT - back) * STRETCH, STRETCH)
                attend_block(chunk, start, lowest, row, k_row, (back + 1) * STRETCH, out_ref, row)


def after(value, *others):
    return lax.optimization_barrier((value, *others))[0]


SMEM_SPEC = pl.BlockSpec(memory_space=pltpu.SMEM)
VMEM_SPEC = pl.BlockSpec(memory_space=pltpu.VMEM)
ANY_SPEC = pl.BlockSpec(memory_space=pl.ANY)


def tail_kernel(x_ref, out_ref, sems):
    rows = out_ref.shape[0]
    for copy in start_all(sems, [(x_ref.at[x_ref.shape[0] - rows :, :], out_ref)]):
        copy.wait()


def take_tail(x):
    return pl.pallas_call(
        tail_kernel,
        out_shape=jax.ShapeDtypeStruct((REACH, x.shape[1]), x.dtype),
        in_specs=[ANY_SPEC],
        out_specs=VMEM_SPEC,
        scratch_shapes=[pltpu.SemaphoreType.DMA((1,))],
        compiler_params=pltpu.CompilerParams(vmem_limit_bytes=4 * MIB),
        name="take_tail",
    )(x)


def project_early(blocks, inputs, partner):
    rows, depth = inputs.shape
    depth -= depth // GROUPS
    cols = blocks.operands[0].shape[1]
    n_copies = len(blocks.counts) - blocks.n_late + 2
    return pl.pallas_call(
        functools.partial(early_kernel, blocks),
        out_shape=[jax.ShapeDtypeStruct((rows, cols), jnp.float32)] * 2,
        in_specs=[ANY_SPEC] * (len(blocks.early_operands) + 2),
        out_specs=[VMEM_SPEC] * 2,
        scratch_shapes=[
            pltpu.VMEM((depth, cols), jnp.bfloat16),
            pltpu.VMEM((rows, depth), jnp.bfloat16),
            pltpu.VMEM((rows, depth), jnp.bfloat16),
            pltpu.SemaphoreType.DMA((n_copies,)),
        ],
        compiler_params=pltpu.CompilerParams(vmem_limit_bytes=24 * MIB),
        cost_estimate=pl.CostEstimate(
            flops=4 * rows * depth * cols,
            bytes_accessed=2 * depth * (2 * rows + cols) + 8 * rows * cols,
            transcendentals=0,
        ),
        name="project_early",
    )(*blocks.early_operands, inputs, partner)


def project_late_attend(tables, blocks, inputs, partner, halos, sums):
    rows, depth = inputs.shape
    late_depth = depth // GROUPS
    cols = blocks.operands[0].shape[1]
    width = cols // 3
    return pl.pallas_call(
        functools.partial(late_kernel, blocks),
        out_shape=[
            jax.ShapeDtypeStruct((rows, width), jnp.bfloat16),
            jax.ShapeDtypeStruct((rows, width), jnp.bfloat16),
            jax.ShapeDtypeStruct((2 * rows + REACH, width), jnp.bfloat16),
            jax.ShapeDtypeStruct((2 * rows + REACH, width), jnp.bfloat16),
        ],
        in_specs=[SMEM_SPEC] * 3 + [ANY_SPEC] * (len(blocks.operands) + 4) + [VMEM_SPEC] * 2,
        out_specs=[VMEM_SPEC] * 4,
        scratch_shapes=[
            pltpu.VMEM((late_depth, cols), jnp.bfloat16),
            pltpu.VMEM((depth, 2 * width), jnp.bfloat16),
            pltpu.VMEM((REACH, depth), jnp.bfloat16),
            pltpu.VMEM((rows, late_depth), jnp.bfloat16),
            pltpu.VMEM((rows, late_depth), jnp.bfloat16),
            pltpu.VMEM((rows, width), jnp.bfloat16),
            pltpu.SemaphoreType.DMA((len(blocks.counts) + blocks.n_late + 3,)),
        ],
        compiler_params=pltpu.CompilerParams(vmem_limit_bytes=24 * MIB),
        name="project_late_attend",
    )(*tables, *blocks.operands, inputs, partner, *halos, *sums)


def attend_own(tables, query, keys, values):
    return pl.pallas_call(
        own_kernel,
        out_shape=jax.ShapeDtypeStruct(query.shape, jnp.bfloat16),
        in_specs=[SMEM_SPEC] * 3 + [VMEM_SPEC] * 3,
        out_specs=VMEM_SPEC,
        compiler_params=pltpu.CompilerParams(vmem_limit_bytes=20 * MIB),
        name="attend_own",
    )(*tables, query, keys, values)


def gather_neighbours(half, halo):
    size = half.shape[0]

    def along(block, hops):
        return lax.ppermute(
            block, "dp", [(2 * a + s, 2 * b + s) for a, b in hops for s in range(2)]
        )

    def across(block, places):
        return lax.ppermute(block, "dp", [(2 * a + s, 2 * a + 1 - s) for a in places for s in range(2)])

    line, ends, middles = range(4), (0, 3), (1, 2)
    outward = [(1, 0), (2, 3)]
    between = [(1, 2), (2, 1)]
    near = along(half, outward + [(0, 1), (3, 2)])
    mid = along(half, between)
    half_across = across(half, line)
    mid_far = along(near, between)
    near_across = across(after(near, half_across, mid, halo), line)
    end_mid = along(mid, outward)
    mid_across = across(after(mid, near_across, mid_far), middles)
    end_mid_across = across(after(end_mid, near_across), ends)
    end_far = along(mid_far, outward)
    mid_far_across = across(after(mid_far, mid_across, end_far), middles)
    end_far_across = across(after(end_far, end_mid_across), ends)

    def find():
        index = lax.axis_index("dp")
        place, side = index // 2, index % 2
        is_end = jnp.where((place == 0) | (place == 3), 1, 0)
        second = jnp.where(is_end == 1, place ^ 2, 3 - place)
        third = jnp.where(is_end == 1, 3 - place, place ^ 2)
        spots = (place, place ^ 1, second, third)
        found = [((2 * spot + (side ^ n)) * size, is_end) for spot in spots for n in range(2)]
        return found, third * 2 * size

    blocks = [
        (half,),
        (half_across,),
        (near,),
        (near_across,),
        (mid, end_mid),
        (mid_across, end_mid_across),
        (mid_far, end_far),
        (mid_far_across, end_far_across),
    ]
    marks = (near_across, mid_far, end_mid), (mid_across, end_mid_across, end_far)
    return Blocks(blocks, 2, find), marks


def local(frames, w_qkv, utt_start, stretch_utt, left_stretches):
    inputs = frames[0]
    depth = inputs.shape[1]
    members = lax.axis_size("tm")
    core = lax.axis_index("tm") % 2

    inner = w_qkv.shape[1] // 3
    width = inner // 2
    thirds = [w_qkv[:, i * inner : (i + 1) * inner] for i in range(3)]
    half = jnp.concatenate(
        [jnp.where(core == 0, third[:, :width], third[:, width:]) for third in thirds], axis=1
    )

    tail = take_tail(inputs)
    halo = lax.ppermute(tail, "tm", [(i, i + 1) for i in range(1, members - 1, 2)])
    if lax.axis_size("dp") == 8:
        blocks, marks = gather_neighbours(after(half, tail), halo)
    else:
        weights = lax.all_gather(half, "dp", axis=0, tiled=True)
        late_first = depth - depth // GROUPS
        found = [(0, 0), (late_first, 0)], late_first
        parts = [(weights[:late_first],), (weights[late_first:],)]
        blocks, marks = Blocks(parts, 1, lambda: found), ((half,), (half,))

    swap = [(i, i ^ 1) for i in range(members)]
    partner = lax.ppermute(after(inputs, *marks[0]), "tm", swap)
    halo_odd = lax.ppermute(
        after(halo, *marks[1]), "tm", [(i, i + 1) for i in range(0, members, 2)]
    )

    tables = (utt_start, stretch_utt, left_stretches)
    sums = project_early(blocks, inputs, partner)
    partner_out, query, keys, values = project_late_attend(
        tables, blocks, inputs, partner, (halo, halo_odd), sums
    )
    other = lax.ppermute(partner_out, "tm", swap)
    own_out = attend_own(tables, query, keys, values)
    left = jnp.where(core == 0, own_out, other)
    right = jnp.where(core == 0, other, own_out)
    return jnp.concatenate([left, right], axis=1)[None]


def solution(mesh):
    return jax.shard_map(
        local,
        mesh=mesh,
        in_specs=(P("dp", "tm", None), P("dp", None), P("dp", None), P("dp", None), P("dp", None)),
        out_specs=P("dp", "tm", None),
        check_vma=False,
    )
```

```python
import functools
import math

import jax
import jax.numpy as jnp
from jax import lax
from jax.experimental import pallas as pl
from jax.experimental.pallas import tpu as pltpu
from jax.sharding import PartitionSpec as P

HEAD_DIM = 96
STRETCH = 256
LEFT = 2
LANES = 128
GROUPS = 4
EXP_SCALE = HEAD_DIM**-0.5 * math.log2(math.e)
REACH = LEFT * STRETCH
MIB = 1024 * 1024


def dot(a, b, dims=((1,), (0,))):
    return lax.dot_general(a, b, (dims, ((), ())), preferred_element_type=jnp.float32)


def head_window(head):
    first = head * HEAD_DIM // LANES * LANES
    last = -(-(head + 1) * HEAD_DIM // LANES) * LANES
    return first, last


def start_all(sems, pairs):
    copies = []
    for i, (*source, target) in enumerate(pairs):
        if len(source) == 1:
            copy = pltpu.make_async_copy(source[0], target, sems.at[i])
            copy.start()
        else:
            for n, choice in enumerate(source[0]):
                copy = pltpu.make_async_copy(choice, target, sems.at[i])
                pl.when(source[1] == n)(copy.start)
        copies.append(copy)
    return copies


class Blocks:
    def __init__(self, blocks, n_late, find):
        self.operands = [operand for block in blocks for operand in block]
        self.counts = [len(block) for block in blocks]
        self.rows = [block[0].shape[0] for block in blocks]
        self.n_late = n_late
        self.early_operands = self.operands[: sum(self.counts[:-n_late])]
        self.find = find

    def copies(self, refs, found, members, target, first=0, columns=slice(None)):
        pairs = []
        for i in members:
            at = sum(self.counts[:i])
            choices = [ref.at[:, columns] for ref in refs[at : at + self.counts[i]]]
            row, which = found[i]
            goal = target.at[pl.ds(pl.multiple_of(row - first, self.rows[i]), self.rows[i])]
            pairs.append((choices[0], goal) if len(choices) == 1 else (choices, which, goal))
        return pairs


def early_kernel(blocks, *refs):
    n = len(blocks.early_operands)
    own_ref, partner_ref, own_sum, partner_sum, w_s, own_s, partner_s, sems = refs[n:]
    found, late_first = blocks.find()
    depth = w_s.shape[0]
    first = jnp.where(late_first == 0, own_ref.shape[1] - depth, 0)
    members = range(len(found) - blocks.n_late)
    pairs = blocks.copies(refs, found, members, w_s, first)
    columns = pl.ds(pl.multiple_of(first, LANES), depth)
    pairs.append((own_ref.at[:, columns], own_s))
    pairs.append((partner_ref.at[:, columns], partner_s))
    for copy in start_all(sems, pairs):
        copy.wait()
    width = w_s.shape[1] // 3
    for x_s, out in ((own_s, own_sum), (partner_s, partner_sum)):
        for third in range(3):
            cols = slice(third * width, (third + 1) * width)
            out[:, cols] = dot(x_s[...], w_s[:, cols])


def late_kernel(blocks, start_ref, owner_ref, left_ref, *refs):
    n = len(blocks.operands)
    own_ref, partner_ref, *halo_refs = refs[n : n + 4]
    own_sum, partner_sum, partner_out, q_own, k_out, v_out = refs[n + 4 : n + 10]
    w_s, kv_s, halo_s, own_s, partner_s, q_partner, sems = refs[n + 10 :]
    depth = w_s.shape[0]
    width = w_s.shape[1] // 3
    rows = own_s.shape[0]
    core = lax.axis_index("tm") % 2
    found, late_first = blocks.find()
    everything = range(len(found))
    pairs = blocks.copies(refs, found, everything, kv_s, 0, slice(width, 3 * width))
    pairs.append((halo_refs, core, halo_s))
    n_first = len(pairs)
    pairs += blocks.copies(refs, found, everything[-blocks.n_late :], w_s, late_first)
    columns = pl.ds(pl.multiple_of(late_first, LANES), depth)
    pairs.append((partner_ref.at[:, columns], partner_s))
    pairs.append((own_ref.at[:, columns], own_s))
    copies = start_all(sems, pairs)

    for copy in copies[:n_first]:
        copy.wait()
    k_out[:REACH, :] = dot(halo_s[...], kv_s[:, :width]).astype(jnp.bfloat16)
    v_out[:REACH, :] = dot(halo_s[...], kv_s[:, width:]).astype(jnp.bfloat16)
    for copy in copies[n_first:]:
        copy.wait()
    for x_s, acc, query, place in (
        (partner_s, partner_sum, q_partner, 1 - core),
        (own_s, own_sum, q_own, core),
    ):
        row = pl.multiple_of(place * rows + REACH, STRETCH)
        for third, dst in enumerate((query, k_out, v_out)):
            cols = slice(third * width, (third + 1) * width)
            value = (acc[:, cols] + dot(x_s[...], w_s[:, cols])).astype(jnp.bfloat16)
            if third == 0:
                dst[...] = value
            else:
                dst[pl.ds(row, rows), :] = value
    attend(start_ref, owner_ref, left_ref, 1 - core, q_partner, k_out, v_out, partner_out)


def own_kernel(start_ref, owner_ref, left_ref, q_ref, k_ref, v_ref, out_ref):
    core = lax.axis_index("tm") % 2
    attend(start_ref, owner_ref, left_ref, core, q_ref, k_ref, v_ref, out_ref)


def attend(start_ref, owner_ref, left_ref, place, q_s, k_s, v_s, out_ref):
    rows, width = out_ref.shape
    chunks = rows // STRETCH
    pair = lax.axis_index("tm") // 2
    lane = lax.broadcasted_iota(jnp.int32, (1, width), 1)
    heads = width // HEAD_DIM

    def attend_block(chunk, start, lowest, q_row, k_row, span, out_ref, out_row):
        first_key = (chunk + 1) * STRETCH - span
        key_frame = first_key + lax.broadcasted_iota(jnp.int32, (1, STRETCH), 1)
        bias = jnp.where(key_frame >= lowest, 0.0, -jnp.inf).astype(jnp.float32)
        frame = chunk * STRETCH + lax.broadcasted_iota(jnp.int32, (STRETCH, 1), 0)
        live = frame >= start
        windows = [head_window(head) for head in range(heads)]
        insides = [
            ((lane >= head * HEAD_DIM) & (lane < (head + 1) * HEAD_DIM))[:, first:last]
            for head, (first, last) in enumerate(windows)
        ]
        tiles = [jnp.zeros((STRETCH, LANES), jnp.float32) for _ in range(width // LANES)]

        def score(head):
            first, last = windows[head]
            q = q_s[pl.ds(q_row, STRETCH), first:last]
            q = jnp.where(insides[head], q, jnp.zeros_like(q))
            return dot(q, k_s[pl.ds(k_row, span), first:last], ((1,), (1,)))

        def weigh(scores):
            scores = [scores[:, at : at + STRETCH] for at in range(0, span, STRETCH)]
            scores[0] = scores[0] + bias
            top = functools.reduce(jnp.maximum, scores)
            top = jnp.max(top, axis=-1, keepdims=True)
            expo = [jnp.exp2((part - top) * EXP_SCALE) for part in scores]
            total = jnp.sum(functools.reduce(jnp.add, expo), axis=-1, keepdims=True)
            share = 1.0 / total
            return jnp.concatenate([(part * share).astype(jnp.bfloat16) for part in expo], axis=1)

        def mix(head, probs):
            first, last = windows[head]
            mixed = dot(probs, v_s[pl.ds(k_row, span), first:last])
            for tile in range(first // LANES, last // LANES):
                at = tile * LANES - first
                tiles[tile] = jnp.where(
                    insides[head][:, at : at + LANES], mixed[:, at : at + LANES], tiles[tile]
                )

        scores = score(0)
        probs = None
        for head in range(heads):
            following = score(head + 1) if head + 1 < heads else None
            weighed = weigh(scores)
            if probs is not None:
                mix(head - 1, probs)
            scores, probs = following, weighed
        mix(heads - 1, probs)
        for tile, value in enumerate(tiles):
            value = jnp.where(live, value, 0.0).astype(jnp.bfloat16)
            out_ref[pl.ds(out_row, STRETCH), tile * LANES : (tile + 1) * LANES] = value

    @pl.loop(0, chunks)
    def _(i):
        row = pl.multiple_of(i * STRETCH, STRETCH)
        chunk = (pair * 2 + place) * chunks + i
        left = left_ref[0, chunk]
        start = start_ref[0, owner_ref[0, chunk]]
        lowest = jnp.maximum((chunk - left) * STRETCH, start)
        for back in range(LEFT + 1):

            @pl.when(left == back)
            def _():
                k_row = pl.multiple_of(place * rows + row + (LEFT - back) * STRETCH, STRETCH)
                attend_block(chunk, start, lowest, row, k_row, (back + 1) * STRETCH, out_ref, row)


def after(value, *others):
    return lax.optimization_barrier((value, *others))[0]


SMEM_SPEC = pl.BlockSpec(memory_space=pltpu.SMEM)
VMEM_SPEC = pl.BlockSpec(memory_space=pltpu.VMEM)
ANY_SPEC = pl.BlockSpec(memory_space=pl.ANY)


def tail_kernel(x_ref, out_ref, sems):
    rows = out_ref.shape[0]
    for copy in start_all(sems, [(x_ref.at[x_ref.shape[0] - rows :, :], out_ref)]):
        copy.wait()


def take_tail(x):
    return pl.pallas_call(
        tail_kernel,
        out_shape=jax.ShapeDtypeStruct((REACH, x.shape[1]), x.dtype),
        in_specs=[ANY_SPEC],
        out_specs=VMEM_SPEC,
        scratch_shapes=[pltpu.SemaphoreType.DMA((1,))],
        compiler_params=pltpu.CompilerParams(vmem_limit_bytes=4 * MIB),
        name="take_tail",
    )(x)


def project_early(blocks, inputs, partner):
    rows, depth = inputs.shape
    depth -= depth // GROUPS
    cols = blocks.operands[0].shape[1]
    n_copies = len(blocks.counts) - blocks.n_late + 2
    return pl.pallas_call(
        functools.partial(early_kernel, blocks),
        out_shape=[jax.ShapeDtypeStruct((rows, cols), jnp.float32)] * 2,
        in_specs=[ANY_SPEC] * (len(blocks.early_operands) + 2),
        out_specs=[VMEM_SPEC] * 2,
        scratch_shapes=[
            pltpu.VMEM((depth, cols), jnp.bfloat16),
            pltpu.VMEM((rows, depth), jnp.bfloat16),
            pltpu.VMEM((rows, depth), jnp.bfloat16),
            pltpu.SemaphoreType.DMA((n_copies,)),
        ],
        compiler_params=pltpu.CompilerParams(vmem_limit_bytes=24 * MIB),
        cost_estimate=pl.CostEstimate(
            flops=4 * rows * depth * cols,
            bytes_accessed=2 * depth * (2 * rows + cols) + 8 * rows * cols,
            transcendentals=0,
        ),
        name="project_early",
    )(*blocks.early_operands, inputs, partner)


def project_late_attend(tables, blocks, inputs, partner, halos, sums):
    rows, depth = inputs.shape
    late_depth = depth // GROUPS
    cols = blocks.operands[0].shape[1]
    width = cols // 3
    return pl.pallas_call(
        functools.partial(late_kernel, blocks),
        out_shape=[
            jax.ShapeDtypeStruct((rows, width), jnp.bfloat16),
            jax.ShapeDtypeStruct((rows, width), jnp.bfloat16),
            jax.ShapeDtypeStruct((2 * rows + REACH, width), jnp.bfloat16),
            jax.ShapeDtypeStruct((2 * rows + REACH, width), jnp.bfloat16),
        ],
        in_specs=[SMEM_SPEC] * 3 + [ANY_SPEC] * (len(blocks.operands) + 4) + [VMEM_SPEC] * 2,
        out_specs=[VMEM_SPEC] * 4,
        scratch_shapes=[
            pltpu.VMEM((late_depth, cols), jnp.bfloat16),
            pltpu.VMEM((depth, 2 * width), jnp.bfloat16),
            pltpu.VMEM((REACH, depth), jnp.bfloat16),
            pltpu.VMEM((rows, late_depth), jnp.bfloat16),
            pltpu.VMEM((rows, late_depth), jnp.bfloat16),
            pltpu.VMEM((rows, width), jnp.bfloat16),
            pltpu.SemaphoreType.DMA((len(blocks.counts) + blocks.n_late + 3,)),
        ],
        compiler_params=pltpu.CompilerParams(vmem_limit_bytes=24 * MIB),
        name="project_late_attend",
    )(*tables, *blocks.operands, inputs, partner, *halos, *sums)


def attend_own(tables, query, keys, values):
    return pl.pallas_call(
        own_kernel,
        out_shape=jax.ShapeDtypeStruct(query.shape, jnp.bfloat16),
        in_specs=[SMEM_SPEC] * 3 + [VMEM_SPEC] * 3,
        out_specs=VMEM_SPEC,
        compiler_params=pltpu.CompilerParams(vmem_limit_bytes=20 * MIB),
        name="attend_own",
    )(*tables, query, keys, values)


def gather_neighbours(half, halo):
    size = half.shape[0]

    def along(block, hops):
        return lax.ppermute(
            block, "dp", [(2 * a + s, 2 * b + s) for a, b in hops for s in range(2)]
        )

    def across(block, places):
        return lax.ppermute(block, "dp", [(2 * a + s, 2 * a + 1 - s) for a in places for s in range(2)])

    line, ends, middles = range(4), (0, 3), (1, 2)
    outward = [(1, 0), (2, 3)]
    between = [(1, 2), (2, 1)]
    near = along(half, outward + [(0, 1), (3, 2)])
    mid = along(half, between)
    half_across = across(half, line)
    mid_far = along(near, between)
    near_across = across(after(near, half_across, mid), line)
    end_mid = along(mid, outward)
    mid_across = across(after(mid, near_across, mid_far, halo), middles)
    end_mid_across = across(after(end_mid, near_across, halo), ends)
    end_far = along(mid_far, outward)
    mid_far_across = across(after(mid_far, mid_across, end_far), middles)
    end_far_across = across(after(end_far, end_mid_across), ends)

    def find():
        index = lax.axis_index("dp")
        place, side = index // 2, index % 2
        is_end = jnp.where((place == 0) | (place == 3), 1, 0)
        second = jnp.where(is_end == 1, place ^ 2, 3 - place)
        third = jnp.where(is_end == 1, 3 - place, place ^ 2)
        spots = (place, place ^ 1, second, third)
        found = [((2 * spot + (side ^ n)) * size, is_end) for spot in spots for n in range(2)]
        return found, third * 2 * size

    blocks = [
        (half,),
        (half_across,),
        (near,),
        (near_across,),
        (mid, end_mid),
        (mid_across, end_mid_across),
        (mid_far, end_far),
        (mid_far_across, end_far_across),
    ]
    marks = (near_across, mid_far, end_mid), (mid_across, end_mid_across, end_far)
    return Blocks(blocks, 2, find), marks


def local(frames, w_qkv, utt_start, stretch_utt, left_stretches):
    inputs = frames[0]
    depth = inputs.shape[1]
    members = lax.axis_size("tm")
    core = lax.axis_index("tm") % 2

    inner = w_qkv.shape[1] // 3
    width = inner // 2
    thirds = [w_qkv[:, i * inner : (i + 1) * inner] for i in range(3)]
    half = jnp.concatenate(
        [jnp.where(core == 0, third[:, :width], third[:, width:]) for third in thirds], axis=1
    )

    tail = take_tail(inputs)
    halo = lax.ppermute(tail, "tm", [(i, i + 1) for i in range(1, members - 1, 2)])
    if lax.axis_size("dp") == 8:
        blocks, marks = gather_neighbours(half, halo)
    else:
        weights = lax.all_gather(half, "dp", axis=0, tiled=True)
        late_first = depth - depth // GROUPS
        found = [(0, 0), (late_first, 0)], late_first
        parts = [(weights[:late_first],), (weights[late_first:],)]
        blocks, marks = Blocks(parts, 1, lambda: found), ((half,), (half,))

    swap = [(i, i ^ 1) for i in range(members)]
    partner = lax.ppermute(after(inputs, *marks[0]), "tm", swap)
    halo_odd = lax.ppermute(
        after(halo, *marks[1]), "tm", [(i, i + 1) for i in range(0, members, 2)]
    )

    tables = (utt_start, stretch_utt, left_stretches)
    sums = project_early(blocks, inputs, partner)
    partner_out, query, keys, values = project_late_attend(
        tables, blocks, inputs, partner, (halo, halo_odd), sums
    )
    other = lax.ppermute(partner_out, "tm", swap)
    own_out = attend_own(tables, query, keys, values)
    left = jnp.where(core == 0, own_out, other)
    right = jnp.where(core == 0, other, own_out)
    return jnp.concatenate([left, right], axis=1)[None]


def solution(mesh):
    return jax.shard_map(
        local,
        mesh=mesh,
        in_specs=(P("dp", "tm", None), P("dp", None), P("dp", None), P("dp", None), P("dp", None)),
        out_specs=P("dp", "tm", None),
        check_vma=False,
    )
```

```python
import functools
import math

import jax
import jax.numpy as jnp
from jax import lax
from jax.experimental import pallas as pl
from jax.experimental.pallas import tpu as pltpu
from jax.sharding import PartitionSpec as P

HEAD_DIM = 96
STRETCH = 256
LEFT = 2
LANES = 128
GROUPS = 4
EXP_SCALE = HEAD_DIM**-0.5 * math.log2(math.e)
REACH = LEFT * STRETCH
MIB = 1024 * 1024


def dot(a, b, dims=((1,), (0,))):
    return lax.dot_general(a, b, (dims, ((), ())), preferred_element_type=jnp.float32)


def head_window(head):
    first = head * HEAD_DIM // LANES * LANES
    last = -(-(head + 1) * HEAD_DIM // LANES) * LANES
    return first, last


def start_all(sems, pairs):
    copies = []
    for i, (*source, target) in enumerate(pairs):
        if len(source) == 1:
            copy = pltpu.make_async_copy(source[0], target, sems.at[i])
            copy.start()
        else:
            for n, choice in enumerate(source[0]):
                copy = pltpu.make_async_copy(choice, target, sems.at[i])
                pl.when(source[1] == n)(copy.start)
        copies.append(copy)
    return copies


class Blocks:
    def __init__(self, blocks, n_late, find):
        self.operands = [operand for block in blocks for operand in block]
        self.counts = [len(block) for block in blocks]
        self.rows = [block[0].shape[0] for block in blocks]
        self.n_late = n_late
        self.early_operands = self.operands[: sum(self.counts[:-n_late])]
        self.find = find

    def copies(self, refs, found, members, target, first=0, columns=slice(None)):
        pairs = []
        for i in members:
            at = sum(self.counts[:i])
            choices = [ref.at[:, columns] for ref in refs[at : at + self.counts[i]]]
            row, which = found[i]
            goal = target.at[pl.ds(pl.multiple_of(row - first, self.rows[i]), self.rows[i])]
            pairs.append((choices[0], goal) if len(choices) == 1 else (choices, which, goal))
        return pairs


def early_kernel(blocks, *refs):
    n = len(blocks.early_operands)
    own_ref, partner_ref, own_sum, partner_sum, w_s, own_s, partner_s, sems = refs[n:]
    found, late_first = blocks.find()
    depth = w_s.shape[0]
    first = jnp.where(late_first == 0, own_ref.shape[1] - depth, 0)
    members = range(len(found) - blocks.n_late)
    pairs = blocks.copies(refs, found, members, w_s, first)
    columns = pl.ds(pl.multiple_of(first, LANES), depth)
    pairs.append((own_ref.at[:, columns], own_s))
    pairs.append((partner_ref.at[:, columns], partner_s))
    for copy in start_all(sems, pairs):
        copy.wait()
    width = w_s.shape[1] // 3
    for x_s, out in ((own_s, own_sum), (partner_s, partner_sum)):
        for third in range(3):
            cols = slice(third * width, (third + 1) * width)
            out[:, cols] = dot(x_s[...], w_s[:, cols])


def late_kernel(blocks, start_ref, owner_ref, left_ref, *refs):
    n = len(blocks.operands)
    own_ref, partner_ref, *halo_refs = refs[n : n + 4]
    own_sum, partner_sum, partner_out, q_own, k_out, v_out = refs[n + 4 : n + 10]
    w_s, kv_s, halo_s, own_s, partner_s, q_partner, sems = refs[n + 10 :]
    depth = w_s.shape[0]
    width = w_s.shape[1] // 3
    rows = own_s.shape[0]
    core = lax.axis_index("tm") % 2
    found, late_first = blocks.find()
    everything = range(len(found))
    pairs = blocks.copies(refs, found, everything, kv_s, 0, slice(width, 3 * width))
    pairs.append((halo_refs, core, halo_s))
    n_first = len(pairs)
    pairs += blocks.copies(refs, found, everything[-blocks.n_late :], w_s, late_first)
    columns = pl.ds(pl.multiple_of(late_first, LANES), depth)
    pairs.append((partner_ref.at[:, columns], partner_s))
    pairs.append((own_ref.at[:, columns], own_s))
    copies = start_all(sems, pairs)

    for copy in copies[:n_first]:
        copy.wait()
    k_out[:REACH, :] = dot(halo_s[...], kv_s[:, :width]).astype(jnp.bfloat16)
    v_out[:REACH, :] = dot(halo_s[...], kv_s[:, width:]).astype(jnp.bfloat16)
    for copy in copies[n_first:]:
        copy.wait()
    for x_s, acc, query, place in (
        (partner_s, partner_sum, q_partner, 1 - core),
        (own_s, own_sum, q_own, core),
    ):
        row = pl.multiple_of(place * rows + REACH, STRETCH)
        for third, dst in enumerate((query, k_out, v_out)):
            cols = slice(third * width, (third + 1) * width)
            value = (acc[:, cols] + dot(x_s[...], w_s[:, cols])).astype(jnp.bfloat16)
            if third == 0:
                dst[...] = value
            else:
                dst[pl.ds(row, rows), :] = value
    attend(start_ref, owner_ref, left_ref, 1 - core, q_partner, k_out, v_out, partner_out)


def own_kernel(start_ref, owner_ref, left_ref, q_ref, k_ref, v_ref, out_ref):
    core = lax.axis_index("tm") % 2
    attend(start_ref, owner_ref, left_ref, core, q_ref, k_ref, v_ref, out_ref)


def attend(start_ref, owner_ref, left_ref, place, q_s, k_s, v_s, out_ref):
    rows, width = out_ref.shape
    chunks = rows // STRETCH
    pair = lax.axis_index("tm") // 2
    lane = lax.broadcasted_iota(jnp.int32, (1, width), 1)
    heads = width // HEAD_DIM

    def attend_block(chunk, start, lowest, q_row, k_row, span, out_ref, out_row):
        first_key = (chunk + 1) * STRETCH - span
        key_frame = first_key + lax.broadcasted_iota(jnp.int32, (1, STRETCH), 1)
        bias = jnp.where(key_frame >= lowest, 0.0, -jnp.inf).astype(jnp.float32)
        frame = chunk * STRETCH + lax.broadcasted_iota(jnp.int32, (STRETCH, 1), 0)
        live = frame >= start
        windows = [head_window(head) for head in range(heads)]
        insides = [
            ((lane >= head * HEAD_DIM) & (lane < (head + 1) * HEAD_DIM))[:, first:last]
            for head, (first, last) in enumerate(windows)
        ]
        tiles = [jnp.zeros((STRETCH, LANES), jnp.float32) for _ in range(width // LANES)]

        def score(head):
            first, last = windows[head]
            q = q_s[pl.ds(q_row, STRETCH), first:last]
            q = jnp.where(insides[head], q, jnp.zeros_like(q))
            return dot(q, k_s[pl.ds(k_row, span), first:last], ((1,), (1,)))

        def weigh(scores):
            scores = [scores[:, at : at + STRETCH] for at in range(0, span, STRETCH)]
            scores[0] = scores[0] + bias
            top = functools.reduce(jnp.maximum, scores)
            top = jnp.max(top, axis=-1, keepdims=True)
            expo = [jnp.exp2((part - top) * EXP_SCALE) for part in scores]
            total = jnp.sum(functools.reduce(jnp.add, expo), axis=-1, keepdims=True)
            share = 1.0 / total
            return jnp.concatenate([(part * share).astype(jnp.bfloat16) for part in expo], axis=1)

        def mix(head, probs):
            first, last = windows[head]
            mixed = dot(probs, v_s[pl.ds(k_row, span), first:last])
            for tile in range(first // LANES, last // LANES):
                at = tile * LANES - first
                tiles[tile] = jnp.where(
                    insides[head][:, at : at + LANES], mixed[:, at : at + LANES], tiles[tile]
                )

        scores = score(0)
        probs = None
        for head in range(heads):
            following = score(head + 1) if head + 1 < heads else None
            weighed = weigh(scores)
            if probs is not None:
                mix(head - 1, probs)
            scores, probs = following, weighed
        mix(heads - 1, probs)
        for tile, value in enumerate(tiles):
            value = jnp.where(live, value, 0.0).astype(jnp.bfloat16)
            out_ref[pl.ds(out_row, STRETCH), tile * LANES : (tile + 1) * LANES] = value

    @pl.loop(0, chunks)
    def _(i):
        row = pl.multiple_of(i * STRETCH, STRETCH)
        chunk = (pair * 2 + place) * chunks + i
        left = left_ref[0, chunk]
        start = start_ref[0, owner_ref[0, chunk]]
        lowest = jnp.maximum((chunk - left) * STRETCH, start)
        for back in range(LEFT + 1):

            @pl.when(left == back)
            def _():
                k_row = pl.multiple_of(place * rows + row + (LEFT - back) * STRETCH, STRETCH)
                attend_block(chunk, start, lowest, row, k_row, (back + 1) * STRETCH, out_ref, row)


def after(value, *others):
    return lax.optimization_barrier((value, *others))[0]


SMEM_SPEC = pl.BlockSpec(memory_space=pltpu.SMEM)
VMEM_SPEC = pl.BlockSpec(memory_space=pltpu.VMEM)
ANY_SPEC = pl.BlockSpec(memory_space=pl.ANY)


def tail_kernel(x_ref, out_ref, sems):
    rows = out_ref.shape[0]
    for copy in start_all(sems, [(x_ref.at[x_ref.shape[0] - rows :, :], out_ref)]):
        copy.wait()


def take_tail(x):
    return pl.pallas_call(
        tail_kernel,
        out_shape=jax.ShapeDtypeStruct((REACH, x.shape[1]), x.dtype),
        in_specs=[ANY_SPEC],
        out_specs=VMEM_SPEC,
        scratch_shapes=[pltpu.SemaphoreType.DMA((1,))],
        compiler_params=pltpu.CompilerParams(vmem_limit_bytes=4 * MIB),
        name="take_tail",
    )(x)


def project_early(blocks, inputs, partner):
    rows, depth = inputs.shape
    depth -= depth // GROUPS
    cols = blocks.operands[0].shape[1]
    n_copies = len(blocks.counts) - blocks.n_late + 2
    return pl.pallas_call(
        functools.partial(early_kernel, blocks),
        out_shape=[jax.ShapeDtypeStruct((rows, cols), jnp.float32)] * 2,
        in_specs=[ANY_SPEC] * (len(blocks.early_operands) + 2),
        out_specs=[VMEM_SPEC] * 2,
        scratch_shapes=[
            pltpu.VMEM((depth, cols), jnp.bfloat16),
            pltpu.VMEM((rows, depth), jnp.bfloat16),
            pltpu.VMEM((rows, depth), jnp.bfloat16),
            pltpu.SemaphoreType.DMA((n_copies,)),
        ],
        compiler_params=pltpu.CompilerParams(vmem_limit_bytes=24 * MIB),
        cost_estimate=pl.CostEstimate(
            flops=4 * rows * depth * cols,
            bytes_accessed=2 * depth * (2 * rows + cols) + 8 * rows * cols,
            transcendentals=0,
        ),
        name="project_early",
    )(*blocks.early_operands, inputs, partner)


def project_late_attend(tables, blocks, inputs, partner, halos, sums):
    rows, depth = inputs.shape
    late_depth = depth // GROUPS
    cols = blocks.operands[0].shape[1]
    width = cols // 3
    return pl.pallas_call(
        functools.partial(late_kernel, blocks),
        out_shape=[
            jax.ShapeDtypeStruct((rows, width), jnp.bfloat16),
            jax.ShapeDtypeStruct((rows, width), jnp.bfloat16),
            jax.ShapeDtypeStruct((2 * rows + REACH, width), jnp.bfloat16),
            jax.ShapeDtypeStruct((2 * rows + REACH, width), jnp.bfloat16),
        ],
        in_specs=[SMEM_SPEC] * 3 + [ANY_SPEC] * (len(blocks.operands) + 4) + [VMEM_SPEC] * 2,
        out_specs=[VMEM_SPEC] * 4,
        scratch_shapes=[
            pltpu.VMEM((late_depth, cols), jnp.bfloat16),
            pltpu.VMEM((depth, 2 * width), jnp.bfloat16),
            pltpu.VMEM((REACH, depth), jnp.bfloat16),
            pltpu.VMEM((rows, late_depth), jnp.bfloat16),
            pltpu.VMEM((rows, late_depth), jnp.bfloat16),
            pltpu.VMEM((rows, width), jnp.bfloat16),
            pltpu.SemaphoreType.DMA((len(blocks.counts) + blocks.n_late + 3,)),
        ],
        compiler_params=pltpu.CompilerParams(vmem_limit_bytes=24 * MIB),
        name="project_late_attend",
    )(*tables, *blocks.operands, inputs, partner, *halos, *sums)


def attend_own(tables, query, keys, values):
    return pl.pallas_call(
        own_kernel,
        out_shape=jax.ShapeDtypeStruct(query.shape, jnp.bfloat16),
        in_specs=[SMEM_SPEC] * 3 + [VMEM_SPEC] * 3,
        out_specs=VMEM_SPEC,
        compiler_params=pltpu.CompilerParams(vmem_limit_bytes=20 * MIB),
        name="attend_own",
    )(*tables, query, keys, values)


def gather_neighbours(half, halo, partner):
    size = half.shape[0]

    def along(block, hops):
        return lax.ppermute(
            block, "dp", [(2 * a + s, 2 * b + s) for a, b in hops for s in range(2)]
        )

    def across(block, places):
        return lax.ppermute(block, "dp", [(2 * a + s, 2 * a + 1 - s) for a in places for s in range(2)])

    line, ends, middles = range(4), (0, 3), (1, 2)
    outward = [(1, 0), (2, 3)]
    between = [(1, 2), (2, 1)]
    near = along(half, outward + [(0, 1), (3, 2)])
    mid = along(half, between)
    half_across = across(half, line)
    mid_far = along(near, between)
    near_across = across(after(near, half_across, mid), line)
    end_mid = along(mid, outward)
    mid_across = across(after(mid, near_across, mid_far, halo), middles)
    end_mid_across = across(after(end_mid, near_across, halo), ends)
    end_far = along(mid_far, outward)
    mid_far_across = across(after(mid_far, mid_across, end_far), middles)
    end_far_across = across(after(end_far, end_mid_across), ends)

    def find():
        index = lax.axis_index("dp")
        place, side = index // 2, index % 2
        is_end = jnp.where((place == 0) | (place == 3), 1, 0)
        second = jnp.where(is_end == 1, place ^ 2, 3 - place)
        third = jnp.where(is_end == 1, 3 - place, place ^ 2)
        spots = (place, place ^ 1, second, third)
        found = [((2 * spot + (side ^ n)) * size, is_end) for spot in spots for n in range(2)]
        return found, third * 2 * size

    blocks = [
        (half,),
        (half_across,),
        (near,),
        (near_across,),
        (mid, end_mid),
        (mid_across, end_mid_across),
        (mid_far, end_far),
        (mid_far_across, end_far_across),
    ]
    marks = (near_across, mid_far, end_mid), (mid_across, end_mid_across, end_far)
    return Blocks(blocks, 2, find), marks


def local(frames, w_qkv, utt_start, stretch_utt, left_stretches):
    inputs = frames[0]
    depth = inputs.shape[1]
    members = lax.axis_size("tm")
    core = lax.axis_index("tm") % 2

    inner = w_qkv.shape[1] // 3
    width = inner // 2
    thirds = [w_qkv[:, i * inner : (i + 1) * inner] for i in range(3)]
    half = jnp.concatenate(
        [jnp.where(core == 0, third[:, :width], third[:, width:]) for third in thirds], axis=1
    )

    swap = [(i, i ^ 1) for i in range(members)]
    partner = lax.ppermute(inputs, "tm", swap)
    tail = take_tail(after(inputs, half))
    halo = lax.ppermute(tail, "tm", [(i, i + 1) for i in range(1, members - 1, 2)])
    if lax.axis_size("dp") == 8:
        blocks, marks = gather_neighbours(half, halo, partner)
    else:
        weights = lax.all_gather(half, "dp", axis=0, tiled=True)
        late_first = depth - depth // GROUPS
        found = [(0, 0), (late_first, 0)], late_first
        parts = [(weights[:late_first],), (weights[late_first:],)]
        blocks, marks = Blocks(parts, 1, lambda: found), ((half,), (half,))

    halo_odd = lax.ppermute(
        after(halo, *marks[1]), "tm", [(i, i + 1) for i in range(0, members, 2)]
    )

    tables = (utt_start, stretch_utt, left_stretches)
    sums = project_early(blocks, inputs, partner)
    partner_out, query, keys, values = project_late_attend(
        tables, blocks, inputs, partner, (halo, halo_odd), sums
    )
    other = lax.ppermute(partner_out, "tm", swap)
    own_out = attend_own(tables, query, keys, values)
    left = jnp.where(core == 0, own_out, other)
    right = jnp.where(core == 0, other, own_out)
    return jnp.concatenate([left, right], axis=1)[None]


def solution(mesh):
    return jax.shard_map(
        local,
        mesh=mesh,
        in_specs=(P("dp", "tm", None), P("dp", None), P("dp", None), P("dp", None), P("dp", None)),
        out_specs=P("dp", "tm", None),
        check_vma=False,
    )
```

```python
import functools
import math

import jax
import jax.numpy as jnp
from jax import lax
from jax.experimental import pallas as pl
from jax.experimental.pallas import tpu as pltpu
from jax.sharding import PartitionSpec as P

HEAD_DIM = 96
STRETCH = 256
LEFT = 2
LANES = 128
GROUPS = 4
EXP_SCALE = HEAD_DIM**-0.5 * math.log2(math.e)
REACH = LEFT * STRETCH
MIB = 1024 * 1024


def dot(a, b, dims=((1,), (0,))):
    return lax.dot_general(a, b, (dims, ((), ())), preferred_element_type=jnp.float32)


def head_window(head):
    first = head * HEAD_DIM // LANES * LANES
    last = -(-(head + 1) * HEAD_DIM // LANES) * LANES
    return first, last


def start_all(sems, pairs):
    copies = []
    for i, (*source, target) in enumerate(pairs):
        if len(source) == 1:
            copy = pltpu.make_async_copy(source[0], target, sems.at[i])
            copy.start()
        else:
            for n, choice in enumerate(source[0]):
                copy = pltpu.make_async_copy(choice, target, sems.at[i])
                pl.when(source[1] == n)(copy.start)
        copies.append(copy)
    return copies


class Blocks:
    def __init__(self, blocks, n_late, find):
        self.operands = [operand for block in blocks for operand in block]
        self.counts = [len(block) for block in blocks]
        self.rows = [block[0].shape[0] for block in blocks]
        self.n_late = n_late
        self.early_operands = self.operands[: sum(self.counts[:-n_late])]
        self.find = find

    def copies(self, refs, found, members, target, first=0, columns=slice(None)):
        pairs = []
        for i in members:
            at = sum(self.counts[:i])
            choices = [ref.at[:, columns] for ref in refs[at : at + self.counts[i]]]
            row, which = found[i]
            goal = target.at[pl.ds(pl.multiple_of(row - first, self.rows[i]), self.rows[i])]
            pairs.append((choices[0], goal) if len(choices) == 1 else (choices, which, goal))
        return pairs


def early_kernel(blocks, *refs):
    n = len(blocks.early_operands)
    own_ref, partner_ref, own_sum, partner_sum, w_s, own_s, partner_s, sems = refs[n:]
    found, late_first = blocks.find()
    depth = w_s.shape[0]
    first = jnp.where(late_first == 0, own_ref.shape[1] - depth, 0)
    members = range(len(found) - blocks.n_late)
    pairs = blocks.copies(refs, found, members, w_s, first)
    columns = pl.ds(pl.multiple_of(first, LANES), depth)
    pairs.append((own_ref.at[:, columns], own_s))
    pairs.append((partner_ref.at[:, columns], partner_s))
    for copy in start_all(sems, pairs):
        copy.wait()
    width = w_s.shape[1] // 3
    for x_s, out in ((own_s, own_sum), (partner_s, partner_sum)):
        for third in range(3):
            cols = slice(third * width, (third + 1) * width)
            out[:, cols] = dot(x_s[...], w_s[:, cols])


def late_kernel(blocks, start_ref, owner_ref, left_ref, *refs):
    n = len(blocks.operands)
    own_ref, partner_ref, own_sum, partner_sum = refs[n : n + 4]
    out_ref, q_out, k_out, v_out, kv_out, w_s, own_s, partner_s, sems = refs[n + 4 :]
    depth = w_s.shape[0]
    width = w_s.shape[1] // 3
    rows = own_s.shape[0]
    core = lax.axis_index("tm") % 2
    found, late_first = blocks.find()
    everything = range(len(found))
    pairs = blocks.copies(refs, found, everything[-blocks.n_late :], w_s, late_first)
    columns = pl.ds(pl.multiple_of(late_first, LANES), depth)
    pairs.append((partner_ref.at[:, columns], partner_s))
    pairs.append((own_ref.at[:, columns], own_s))
    n_first = len(pairs)
    pairs += blocks.copies(refs, found, everything, kv_out, 0, slice(width, 3 * width))
    copies = start_all(sems, pairs)
    for copy in copies[:n_first]:
        copy.wait()
    for x_s, acc, place in ((partner_s, partner_sum, 1 - core), (own_s, own_sum, core)):
        row = pl.multiple_of(place * rows, STRETCH)
        for third, dst in enumerate((q_out, k_out, v_out)):
            cols = slice(third * width, (third + 1) * width)
            value = acc[:, cols] + dot(x_s[...], w_s[:, cols])
            dst[pl.ds(row, rows), :] = value.astype(jnp.bfloat16)
    attend(start_ref, owner_ref, left_ref, 1, q_out, rows, k_out, v_out, rows - REACH, out_ref)
    for copy in copies[n_first:]:
        copy.wait()


def first_kernel(start_ref, owner_ref, left_ref, q_ref, k_ref, v_ref, kv_ref, *refs):
    *halo_refs, out_ref, k_s, v_s = refs
    rows, width = out_ref.shape
    core = lax.axis_index("tm") % 2
    for n in range(2):

        @pl.when(core == n)
        def _():
            for i, frames_ref in enumerate(halo_refs[n * LEFT : (n + 1) * LEFT]):
                at = slice(i * STRETCH, (i + 1) * STRETCH)
                k_s[at, :] = dot(frames_ref[...], kv_ref[:, :width]).astype(jnp.bfloat16)
                v_s[at, :] = dot(frames_ref[...], kv_ref[:, width:]).astype(jnp.bfloat16)

    k_s[REACH:, :] = k_ref[:rows, :]
    v_s[REACH:, :] = v_ref[:rows, :]
    attend(start_ref, owner_ref, left_ref, 0, q_ref, 0, k_s, v_s, 0, out_ref)


def attend(start_ref, owner_ref, left_ref, place, q_s, q_first, k_s, v_s, k_first, out_ref):
    rows, width = out_ref.shape
    chunks = rows // STRETCH
    pair = lax.axis_index("tm") // 2
    lane = lax.broadcasted_iota(jnp.int32, (1, width), 1)
    heads = width // HEAD_DIM

    def attend_block(chunk, start, lowest, q_row, k_row, span, out_ref, out_row):
        first_key = (chunk + 1) * STRETCH - span
        key_frame = first_key + lax.broadcasted_iota(jnp.int32, (1, STRETCH), 1)
        bias = jnp.where(key_frame >= lowest, 0.0, -jnp.inf).astype(jnp.float32)
        frame = chunk * STRETCH + lax.broadcasted_iota(jnp.int32, (STRETCH, 1), 0)
        live = frame >= start
        windows = [head_window(head) for head in range(heads)]
        insides = [
            ((lane >= head * HEAD_DIM) & (lane < (head + 1) * HEAD_DIM))[:, first:last]
            for head, (first, last) in enumerate(windows)
        ]
        tiles = [jnp.zeros((STRETCH, LANES), jnp.float32) for _ in range(width // LANES)]

        def score(head):
            first, last = windows[head]
            q = q_s[pl.ds(q_row, STRETCH), first:last]
            q = jnp.where(insides[head], q, jnp.zeros_like(q))
            return dot(q, k_s[pl.ds(k_row, span), first:last], ((1,), (1,)))

        def weigh(scores):
            scores = [scores[:, at : at + STRETCH] for at in range(0, span, STRETCH)]
            scores[0] = scores[0] + bias
            top = functools.reduce(jnp.maximum, scores)
            top = jnp.max(top, axis=-1, keepdims=True)
            expo = [jnp.exp2((part - top) * EXP_SCALE) for part in scores]
            total = jnp.sum(functools.reduce(jnp.add, expo), axis=-1, keepdims=True)
            share = 1.0 / total
            return jnp.concatenate([(part * share).astype(jnp.bfloat16) for part in expo], axis=1)

        def mix(head, probs):
            first, last = windows[head]
            mixed = dot(probs, v_s[pl.ds(k_row, span), first:last])
            for tile in range(first // LANES, last // LANES):
                at = tile * LANES - first
                tiles[tile] = jnp.where(
                    insides[head][:, at : at + LANES], mixed[:, at : at + LANES], tiles[tile]
                )

        scores = score(0)
        probs = None
        for head in range(heads):
            following = score(head + 1) if head + 1 < heads else None
            weighed = weigh(scores)
            if probs is not None:
                mix(head - 1, probs)
            scores, probs = following, weighed
        mix(heads - 1, probs)
        for tile, value in enumerate(tiles):
            value = jnp.where(live, value, 0.0).astype(jnp.bfloat16)
            out_ref[pl.ds(out_row, STRETCH), tile * LANES : (tile + 1) * LANES] = value

    @pl.loop(0, chunks)
    def _(i):
        row = pl.multiple_of(i * STRETCH, STRETCH)
        chunk = (pair * 2 + place) * chunks + i
        left = left_ref[0, chunk]
        start = start_ref[0, owner_ref[0, chunk]]
        lowest = jnp.maximum((chunk - left) * STRETCH, start)
        for back in range(LEFT + 1):

            @pl.when(left == back)
            def _():
                q_row = pl.multiple_of(q_first + row, STRETCH)
                k_row = pl.multiple_of(k_first + row + (LEFT - back) * STRETCH, STRETCH)
                attend_block(chunk, start, lowest, q_row, k_row, (back + 1) * STRETCH, out_ref, row)


def after(value, *others):
    return lax.optimization_barrier((value, *others))[0]


SMEM_SPEC = pl.BlockSpec(memory_space=pltpu.SMEM)
VMEM_SPEC = pl.BlockSpec(memory_space=pltpu.VMEM)
ANY_SPEC = pl.BlockSpec(memory_space=pl.ANY)


def project_early(blocks, inputs, partner):
    rows, depth = inputs.shape
    depth -= depth // GROUPS
    cols = blocks.operands[0].shape[1]
    n_copies = len(blocks.counts) - blocks.n_late + 2
    return pl.pallas_call(
        functools.partial(early_kernel, blocks),
        out_shape=[jax.ShapeDtypeStruct((rows, cols), jnp.float32)] * 2,
        in_specs=[ANY_SPEC] * (len(blocks.early_operands) + 2),
        out_specs=[VMEM_SPEC] * 2,
        scratch_shapes=[
            pltpu.VMEM((depth, cols), jnp.bfloat16),
            pltpu.VMEM((rows, depth), jnp.bfloat16),
            pltpu.VMEM((rows, depth), jnp.bfloat16),
            pltpu.SemaphoreType.DMA((n_copies,)),
        ],
        compiler_params=pltpu.CompilerParams(vmem_limit_bytes=24 * MIB),
        cost_estimate=pl.CostEstimate(flops=0, bytes_accessed=0, transcendentals=0),
        name="project_early",
    )(*blocks.early_operands, inputs, partner)


def tail_kernel(x_ref, *refs):
    *outs, sems = refs
    first = x_ref.shape[0] - len(outs) * STRETCH
    pairs = [
        (x_ref.at[first + i * STRETCH : first + (i + 1) * STRETCH, :], out)
        for i, out in enumerate(outs)
    ]
    for copy in start_all(sems, pairs):
        copy.wait()


def take_tail(x):
    return pl.pallas_call(
        tail_kernel,
        out_shape=[jax.ShapeDtypeStruct((STRETCH, x.shape[1]), x.dtype)] * LEFT,
        in_specs=[ANY_SPEC],
        out_specs=[VMEM_SPEC] * LEFT,
        scratch_shapes=[pltpu.SemaphoreType.DMA((LEFT,))],
        compiler_params=pltpu.CompilerParams(vmem_limit_bytes=4 * MIB),
        name="take_tail",
    )(x)


def project_late_attend(tables, blocks, inputs, partner, sums):
    rows, depth = inputs.shape
    late_depth = depth // GROUPS
    cols = blocks.operands[0].shape[1]
    width = cols // 3
    return pl.pallas_call(
        functools.partial(late_kernel, blocks),
        out_shape=[jax.ShapeDtypeStruct((rows, width), jnp.bfloat16)]
        + [jax.ShapeDtypeStruct((2 * rows, width), jnp.bfloat16)] * 3
        + [jax.ShapeDtypeStruct((depth, 2 * width), jnp.bfloat16)],
        in_specs=[SMEM_SPEC] * 3 + [ANY_SPEC] * (len(blocks.operands) + 2) + [VMEM_SPEC] * 2,
        out_specs=[VMEM_SPEC] * 5,
        scratch_shapes=[
            pltpu.VMEM((late_depth, cols), jnp.bfloat16),
            pltpu.VMEM((rows, late_depth), jnp.bfloat16),
            pltpu.VMEM((rows, late_depth), jnp.bfloat16),
            pltpu.SemaphoreType.DMA((len(blocks.counts) + blocks.n_late + 2,)),
        ],
        compiler_params=pltpu.CompilerParams(vmem_limit_bytes=24 * MIB),
        name="project_late_attend",
    )(*tables, *blocks.operands, inputs, partner, *sums)


def attend_first(tables, query, keys, values, weights, halos):
    rows, width = query.shape
    rows //= 2
    return pl.pallas_call(
        first_kernel,
        out_shape=jax.ShapeDtypeStruct((rows, width), jnp.bfloat16),
        in_specs=[SMEM_SPEC] * 3 + [VMEM_SPEC] * (4 + len(halos)),
        out_specs=VMEM_SPEC,
        scratch_shapes=[pltpu.VMEM((rows + REACH, width), jnp.bfloat16)] * 2,
        compiler_params=pltpu.CompilerParams(vmem_limit_bytes=20 * MIB),
        name="attend_first",
    )(*tables, query, keys, values, weights, *halos)


def gather_neighbours(half):
    size = half.shape[0]

    def along(name, block, hops):
        with jax.named_scope(name):
            return lax.ppermute(
                block, "dp", [(2 * a + s, 2 * b + s) for a, b in hops for s in range(2)]
            )

    def across(name, block, places):
        with jax.named_scope(name):
            return lax.ppermute(
                block, "dp", [(2 * a + s, 2 * a + 1 - s) for a in places for s in range(2)]
            )

    line, ends, middles = range(4), (0, 3), (1, 2)
    outward = [(1, 0), (2, 3)]
    between = [(1, 2), (2, 1)]
    near = along("near", half, outward + [(0, 1), (3, 2)])
    mid = along("mid", half, between)
    half_across = across("half_across", half, line)
    mid_far = along("mid_far", near, between)
    near_across = across("near_across", after(near, half_across, mid), line)
    end_mid = along("end_mid", mid, outward)
    mid_across = across("mid_across", after(mid, near_across, mid_far), middles)
    end_mid_across = across("end_mid_across", after(end_mid, near_across), ends)
    end_far = along("end_far", mid_far, outward)
    mid_far_across = across("mid_far_across", after(mid_far, mid_across, end_far), middles)
    end_far_across = across("end_far_across", after(end_far, end_mid_across), ends)

    def find():
        index = lax.axis_index("dp")
        place, side = index // 2, index % 2
        is_end = jnp.where((place == 0) | (place == 3), 1, 0)
        second = jnp.where(is_end == 1, place ^ 2, 3 - place)
        third = jnp.where(is_end == 1, 3 - place, place ^ 2)
        spots = (place, place ^ 1, second, third)
        found = [((2 * spot + (side ^ n)) * size, is_end) for spot in spots for n in range(2)]
        return found, third * 2 * size

    blocks = [
        (half,),
        (half_across,),
        (near,),
        (near_across,),
        (mid, end_mid),
        (mid_across, end_mid_across),
        (mid_far, end_far),
        (mid_far_across, end_far_across),
    ]
    marks = (
        (near_across, mid_far, end_mid),
        (mid_across, end_mid_across, end_far),
        (mid_far_across, end_far_across),
    )
    return Blocks(blocks, 2, find), marks


def local(frames, w_qkv, utt_start, stretch_utt, left_stretches):
    inputs = frames[0]
    depth = inputs.shape[1]
    members = lax.axis_size("tm")
    core = lax.axis_index("tm") % 2

    inner = w_qkv.shape[1] // 3
    width = inner // 2
    thirds = [w_qkv[:, i * inner : (i + 1) * inner] for i in range(3)]
    half = jnp.concatenate(
        [jnp.where(core == 0, third[:, :width], third[:, width:]) for third in thirds], axis=1
    )

    tail = take_tail(after(inputs, half))
    with jax.named_scope("partner"):
        partner = lax.ppermute(inputs, "tm", [(i, i ^ 1) for i in range(members)])
    if lax.axis_size("dp") == 8:
        blocks, marks = gather_neighbours(half)
    else:
        weights = lax.all_gather(half, "dp", axis=0, tiled=True)
        late_first = depth - depth // GROUPS
        found = [(0, 0), (late_first, 0)], late_first
        parts = [(weights[:late_first],), (weights[late_first:],)]
        blocks, marks = Blocks(parts, 1, lambda: found), ((half,),) * 3

    up = [(i, i + 1) for i in range(0, members, 2)]
    down = [(i + 1, i) for i in range(0, members, 2)]
    with jax.named_scope("halo"):
        halo = [
            lax.ppermute(
                after(block, *marks[0]), "tm", [(i, i + 1) for i in range(1, members - 1, 2)]
            )
            for block in tail
        ]

    tables = (utt_start, stretch_utt, left_stretches)
    sums = project_early(blocks, inputs, after(partner, halo[0]))
    with jax.named_scope("halo_odd"):
        halo_odd = [lax.ppermute(after(block, *marks[2], *sums), "tm", up) for block in halo]
    second_out, query, keys, values, weights = project_late_attend(
        tables, blocks, inputs, partner, sums
    )
    second_swapped = lax.ppermute(second_out, "tm", up)
    first_out = attend_first(tables, query, keys, values, weights, halo + halo_odd)
    first_swapped = lax.ppermute(first_out, "tm", down)
    left = jnp.where(core == 0, first_out, second_swapped)
    right = jnp.where(core == 0, first_swapped, second_out)
    return jnp.concatenate([left, right], axis=1)[None]


def solution(mesh):
    return jax.shard_map(
        local,
        mesh=mesh,
        in_specs=(P("dp", "tm", None), P("dp", None), P("dp", None), P("dp", None), P("dp", None)),
        out_specs=P("dp", "tm", None),
        check_vma=False,
    )
```

```python
import functools
import math

import jax
import jax.numpy as jnp
from jax import lax
from jax.experimental import pallas as pl
from jax.experimental.pallas import tpu as pltpu
from jax.sharding import PartitionSpec as P

HEAD_DIM = 96
STRETCH = 256
LEFT = 2
LANES = 128
GROUPS = 4
EXP_SCALE = HEAD_DIM**-0.5 * math.log2(math.e)
REACH = LEFT * STRETCH
MIB = 1024 * 1024


def dot(a, b, dims=((1,), (0,))):
    return lax.dot_general(a, b, (dims, ((), ())), preferred_element_type=jnp.float32)


def head_window(head):
    first = head * HEAD_DIM // LANES * LANES
    last = -(-(head + 1) * HEAD_DIM // LANES) * LANES
    return first, last


def start_all(sems, pairs):
    copies = []
    for i, (*source, target) in enumerate(pairs):
        if len(source) == 1:
            copy = pltpu.make_async_copy(source[0], target, sems.at[i])
            copy.start()
        else:
            for n, choice in enumerate(source[0]):
                copy = pltpu.make_async_copy(choice, target, sems.at[i])
                pl.when(source[1] == n)(copy.start)
        copies.append(copy)
    return copies


class Blocks:
    def __init__(self, blocks, n_late, find):
        self.operands = [operand for block in blocks for operand in block]
        self.counts = [len(block) for block in blocks]
        self.rows = [block[0].shape[0] for block in blocks]
        self.n_late = n_late
        self.early_operands = self.operands[: sum(self.counts[:-n_late])]
        self.find = find

    def copies(self, refs, found, members, target, first=0, columns=slice(None)):
        pairs = []
        for i in members:
            at = sum(self.counts[:i])
            choices = [ref.at[:, columns] for ref in refs[at : at + self.counts[i]]]
            row, which = found[i]
            goal = target.at[pl.ds(pl.multiple_of(row - first, self.rows[i]), self.rows[i])]
            pairs.append((choices[0], goal) if len(choices) == 1 else (choices, which, goal))
        return pairs


def early_kernel(blocks, *refs):
    n = len(blocks.early_operands)
    own_ref, partner_ref, own_sum, partner_sum, w_s, own_s, partner_s, sems = refs[n:]
    found, late_first = blocks.find()
    depth = w_s.shape[0]
    first = jnp.where(late_first == 0, own_ref.shape[1] - depth, 0)
    members = range(len(found) - blocks.n_late)
    pairs = blocks.copies(refs, found, members, w_s, first)
    columns = pl.ds(pl.multiple_of(first, LANES), depth)
    pairs.append((own_ref.at[:, columns], own_s))
    pairs.append((partner_ref.at[:, columns], partner_s))
    for copy in start_all(sems, pairs):
        copy.wait()
    width = w_s.shape[1] // 3
    for x_s, out in ((own_s, own_sum), (partner_s, partner_sum)):
        for third in range(3):
            cols = slice(third * width, (third + 1) * width)
            out[:, cols] = dot(x_s[...], w_s[:, cols])


def late_kernel(blocks, start_ref, owner_ref, left_ref, *refs):
    n = len(blocks.operands)
    own_ref, partner_ref, halo_ref, own_sum, partner_sum = refs[n : n + 5]
    out_ref, q_own, k_out, v_out, kv_out, q_partner, w_s, own_s, partner_s, sems = refs[n + 5 :]
    depth = w_s.shape[0]
    width = w_s.shape[1] // 3
    rows = own_s.shape[0]
    core = lax.axis_index("tm") % 2
    found, late_first = blocks.find()
    everything = range(len(found))
    pairs = blocks.copies(refs, found, everything[-blocks.n_late :], w_s, late_first)
    columns = pl.ds(pl.multiple_of(late_first, LANES), depth)
    pairs.append((partner_ref.at[:, columns], partner_s))
    pairs.append((own_ref.at[:, columns], own_s))
    n_first = len(pairs)
    pairs += blocks.copies(refs, found, everything, kv_out, 0, slice(width, 3 * width))
    copies = start_all(sems, pairs)
    for copy in copies[:n_first]:
        copy.wait()
    for x_s, acc, query, place in (
        (partner_s, partner_sum, q_partner, 1 - core),
        (own_s, own_sum, q_own, core),
    ):
        row = pl.multiple_of(place * rows + REACH, STRETCH)
        for third, dst in enumerate((query, k_out, v_out)):
            cols = slice(third * width, (third + 1) * width)
            value = (acc[:, cols] + dot(x_s[...], w_s[:, cols])).astype(jnp.bfloat16)
            if third == 0:
                dst[...] = value
            else:
                dst[pl.ds(row, rows), :] = value
    for copy in copies[n_first:]:
        copy.wait()

    @pl.when(core == 1)
    def _():
        k_out[:REACH, :] = dot(halo_ref[...], kv_out[:, :width]).astype(jnp.bfloat16)
        v_out[:REACH, :] = dot(halo_ref[...], kv_out[:, width:]).astype(jnp.bfloat16)

    first = pl.multiple_of((1 - core) * rows, STRETCH)
    attend(start_ref, owner_ref, left_ref, 1 - core, q_partner, 0, k_out, v_out, first, out_ref)


def own_kernel(
    start_ref, owner_ref, left_ref, q_ref, k_ref, v_ref, kv_ref, halo_ref, out_ref, k_s, v_s
):
    rows, width = out_ref.shape
    core = lax.axis_index("tm") % 2
    own = pl.multiple_of(core * rows + REACH, STRETCH)
    k_s[REACH:, :] = k_ref[pl.ds(own, rows), :]
    v_s[REACH:, :] = v_ref[pl.ds(own, rows), :]

    @pl.when(core == 0)
    def _():
        k_s[:REACH, :] = dot(halo_ref[...], kv_ref[:, :width]).astype(jnp.bfloat16)
        v_s[:REACH, :] = dot(halo_ref[...], kv_ref[:, width:]).astype(jnp.bfloat16)

    @pl.when(core == 1)
    def _():
        k_s[:REACH, :] = k_ref[rows : rows + REACH, :]
        v_s[:REACH, :] = v_ref[rows : rows + REACH, :]

    attend(start_ref, owner_ref, left_ref, core, q_ref, 0, k_s, v_s, 0, out_ref)


def attend(start_ref, owner_ref, left_ref, place, q_s, q_first, k_s, v_s, k_first, out_ref):
    rows, width = out_ref.shape
    chunks = rows // STRETCH
    pair = lax.axis_index("tm") // 2
    lane = lax.broadcasted_iota(jnp.int32, (1, width), 1)
    heads = width // HEAD_DIM

    def attend_block(chunk, start, lowest, q_row, k_row, span, out_ref, out_row):
        first_key = (chunk + 1) * STRETCH - span
        key_frame = first_key + lax.broadcasted_iota(jnp.int32, (1, STRETCH), 1)
        bias = jnp.where(key_frame >= lowest, 0.0, -jnp.inf).astype(jnp.float32)
        frame = chunk * STRETCH + lax.broadcasted_iota(jnp.int32, (STRETCH, 1), 0)
        live = frame >= start
        windows = [head_window(head) for head in range(heads)]
        insides = [
            ((lane >= head * HEAD_DIM) & (lane < (head + 1) * HEAD_DIM))[:, first:last]
            for head, (first, last) in enumerate(windows)
        ]
        tiles = [jnp.zeros((STRETCH, LANES), jnp.float32) for _ in range(width // LANES)]

        def score(head):
            first, last = windows[head]
            q = q_s[pl.ds(q_row, STRETCH), first:last]
            q = jnp.where(insides[head], q, jnp.zeros_like(q))
            return dot(q, k_s[pl.ds(k_row, span), first:last], ((1,), (1,)))

        def weigh(scores):
            scores = [scores[:, at : at + STRETCH] for at in range(0, span, STRETCH)]
            scores[0] = scores[0] + bias
            top = functools.reduce(jnp.maximum, scores)
            top = jnp.max(top, axis=-1, keepdims=True)
            expo = [jnp.exp2((part - top) * EXP_SCALE) for part in scores]
            total = jnp.sum(functools.reduce(jnp.add, expo), axis=-1, keepdims=True)
            share = 1.0 / total
            return jnp.concatenate([(part * share).astype(jnp.bfloat16) for part in expo], axis=1)

        def mix(head, probs):
            first, last = windows[head]
            mixed = dot(probs, v_s[pl.ds(k_row, span), first:last])
            for tile in range(first // LANES, last // LANES):
                at = tile * LANES - first
                tiles[tile] = jnp.where(
                    insides[head][:, at : at + LANES], mixed[:, at : at + LANES], tiles[tile]
                )

        scores = score(0)
        probs = None
        for head in range(heads):
            following = score(head + 1) if head + 1 < heads else None
            weighed = weigh(scores)
            if probs is not None:
                mix(head - 1, probs)
            scores, probs = following, weighed
        mix(heads - 1, probs)
        for tile, value in enumerate(tiles):
            value = jnp.where(live, value, 0.0).astype(jnp.bfloat16)
            out_ref[pl.ds(out_row, STRETCH), tile * LANES : (tile + 1) * LANES] = value

    @pl.loop(0, chunks)
    def _(i):
        row = pl.multiple_of(i * STRETCH, STRETCH)
        chunk = (pair * 2 + place) * chunks + i
        left = left_ref[0, chunk]
        start = start_ref[0, owner_ref[0, chunk]]
        lowest = jnp.maximum((chunk - left) * STRETCH, start)
        for back in range(LEFT + 1):

            @pl.when(left == back)
            def _():
                q_row = pl.multiple_of(q_first + row, STRETCH)
                k_row = pl.multiple_of(k_first + row + (LEFT - back) * STRETCH, STRETCH)
                attend_block(chunk, start, lowest, q_row, k_row, (back + 1) * STRETCH, out_ref, row)


def after(value, *others):
    return lax.optimization_barrier((value, *others))[0]


SMEM_SPEC = pl.BlockSpec(memory_space=pltpu.SMEM)
VMEM_SPEC = pl.BlockSpec(memory_space=pltpu.VMEM)
ANY_SPEC = pl.BlockSpec(memory_space=pl.ANY)


def project_early(blocks, inputs, partner):
    rows, depth = inputs.shape
    depth -= depth // GROUPS
    cols = blocks.operands[0].shape[1]
    n_copies = len(blocks.counts) - blocks.n_late + 2
    return pl.pallas_call(
        functools.partial(early_kernel, blocks),
        out_shape=[jax.ShapeDtypeStruct((rows, cols), jnp.float32)] * 2,
        in_specs=[ANY_SPEC] * (len(blocks.early_operands) + 2),
        out_specs=[VMEM_SPEC] * 2,
        scratch_shapes=[
            pltpu.VMEM((depth, cols), jnp.bfloat16),
            pltpu.VMEM((rows, depth), jnp.bfloat16),
            pltpu.VMEM((rows, depth), jnp.bfloat16),
            pltpu.SemaphoreType.DMA((n_copies,)),
        ],
        compiler_params=pltpu.CompilerParams(vmem_limit_bytes=24 * MIB),
        cost_estimate=pl.CostEstimate(flops=0, bytes_accessed=0, transcendentals=0),
        name="project_early",
    )(*blocks.early_operands, inputs, partner)


def tail_kernel(x_ref, out_ref, sems):
    rows = out_ref.shape[0]
    for copy in start_all(sems, [(x_ref.at[x_ref.shape[0] - rows :, :], out_ref)]):
        copy.wait()


def take_tail(x):
    return pl.pallas_call(
        tail_kernel,
        out_shape=jax.ShapeDtypeStruct((REACH, x.shape[1]), x.dtype),
        in_specs=[ANY_SPEC],
        out_specs=VMEM_SPEC,
        scratch_shapes=[pltpu.SemaphoreType.DMA((1,))],
        compiler_params=pltpu.CompilerParams(vmem_limit_bytes=4 * MIB),
        name="take_tail",
    )(x)


def project_late_attend(tables, blocks, inputs, partner, halo, sums):
    rows, depth = inputs.shape
    late_depth = depth // GROUPS
    cols = blocks.operands[0].shape[1]
    width = cols // 3
    keys = jax.ShapeDtypeStruct((2 * rows + REACH, width), jnp.bfloat16)
    queries = jax.ShapeDtypeStruct((rows, width), jnp.bfloat16)
    return pl.pallas_call(
        functools.partial(late_kernel, blocks),
        out_shape=[
            queries,
            queries,
            keys,
            keys,
            jax.ShapeDtypeStruct((depth, 2 * width), jnp.bfloat16),
        ],
        in_specs=[SMEM_SPEC] * 3 + [ANY_SPEC] * (len(blocks.operands) + 2) + [VMEM_SPEC] * 3,
        out_specs=[VMEM_SPEC] * 5,
        scratch_shapes=[
            pltpu.VMEM((rows, width), jnp.bfloat16),
            pltpu.VMEM((late_depth, cols), jnp.bfloat16),
            pltpu.VMEM((rows, late_depth), jnp.bfloat16),
            pltpu.VMEM((rows, late_depth), jnp.bfloat16),
            pltpu.SemaphoreType.DMA((len(blocks.counts) + blocks.n_late + 2,)),
        ],
        compiler_params=pltpu.CompilerParams(vmem_limit_bytes=24 * MIB),
        name="project_late_attend",
    )(*tables, *blocks.operands, inputs, partner, halo, *sums)


def attend_own(tables, query, keys, values, weights, halo):
    rows, width = query.shape
    return pl.pallas_call(
        own_kernel,
        out_shape=jax.ShapeDtypeStruct((rows, width), jnp.bfloat16),
        in_specs=[SMEM_SPEC] * 3 + [VMEM_SPEC] * 5,
        out_specs=VMEM_SPEC,
        scratch_shapes=[pltpu.VMEM((rows + REACH, width), jnp.bfloat16)] * 2,
        compiler_params=pltpu.CompilerParams(vmem_limit_bytes=20 * MIB),
        name="attend_own",
    )(*tables, query, keys, values, weights, halo)


def gather_neighbours(half):
    size = half.shape[0]

    def along(name, block, hops):
        with jax.named_scope(name):
            return lax.ppermute(
                block, "dp", [(2 * a + s, 2 * b + s) for a, b in hops for s in range(2)]
            )

    def across(name, block, places):
        with jax.named_scope(name):
            return lax.ppermute(
                block, "dp", [(2 * a + s, 2 * a + 1 - s) for a in places for s in range(2)]
            )

    line, ends, middles = range(4), (0, 3), (1, 2)
    outward = [(1, 0), (2, 3)]
    between = [(1, 2), (2, 1)]
    near = along("near", half, outward + [(0, 1), (3, 2)])
    mid = along("mid", half, between)
    half_across = across("half_across", half, line)
    mid_far = along("mid_far", near, between)
    near_across = across("near_across", after(near, half_across, mid), line)
    end_mid = along("end_mid", mid, outward)
    mid_across = across("mid_across", after(mid, near_across, mid_far), middles)
    end_mid_across = across("end_mid_across", after(end_mid, near_across), ends)
    end_far = along("end_far", after(mid_far, end_mid), outward)
    mid_far_across = across("mid_far_across", after(mid_far, mid_across, end_far), middles)
    end_far_across = across("end_far_across", after(end_far, end_mid_across), ends)

    def find():
        index = lax.axis_index("dp")
        place, side = index // 2, index % 2
        is_end = jnp.where((place == 0) | (place == 3), 1, 0)
        second = jnp.where(is_end == 1, place ^ 2, 3 - place)
        third = jnp.where(is_end == 1, 3 - place, place ^ 2)
        spots = (place, place ^ 1, second, third)
        found = [((2 * spot + (side ^ n)) * size, is_end) for spot in spots for n in range(2)]
        return found, third * 2 * size

    blocks = [
        (half,),
        (half_across,),
        (near,),
        (near_across,),
        (mid, end_mid),
        (mid_across, end_mid_across),
        (mid_far, end_far),
        (mid_far_across, end_far_across),
    ]
    marks = (
        (near_across, mid_far, end_mid),
        (mid_across, end_mid_across, end_far),
        (mid_far_across, end_far_across),
    )
    return Blocks(blocks, 2, find), marks


def local(frames, w_qkv, utt_start, stretch_utt, left_stretches):
    inputs = frames[0]
    depth = inputs.shape[1]
    members = lax.axis_size("tm")
    core = lax.axis_index("tm") % 2

    inner = w_qkv.shape[1] // 3
    width = inner // 2
    thirds = [w_qkv[:, i * inner : (i + 1) * inner] for i in range(3)]
    half = jnp.concatenate(
        [jnp.where(core == 0, third[:, :width], third[:, width:]) for third in thirds], axis=1
    )

    tail = take_tail(after(inputs, half))
    with jax.named_scope("partner"):
        partner = lax.ppermute(inputs, "tm", [(i, i ^ 1) for i in range(members)])
    if lax.axis_size("dp") == 8:
        blocks, marks = gather_neighbours(half)
    else:
        weights = lax.all_gather(half, "dp", axis=0, tiled=True)
        late_first = depth - depth // GROUPS
        found = [(0, 0), (late_first, 0)], late_first
        parts = [(weights[:late_first],), (weights[late_first:],)]
        blocks, marks = Blocks(parts, 1, lambda: found), ((half,),) * 3

    with jax.named_scope("halo"):
        halo = lax.ppermute(
            after(tail, *marks[0]), "tm", [(i, i + 2) for i in range(1, members - 2, 2)]
        )

    tables = (utt_start, stretch_utt, left_stretches)
    sums = project_early(blocks, inputs, partner)
    with jax.named_scope("halo_first"):
        halo_first = lax.ppermute(
            after(halo, *marks[2], *sums), "tm", [(i + 1, i) for i in range(0, members, 2)]
        )
    partner_out, query, keys, values, weights = project_late_attend(
        tables, blocks, inputs, partner, halo, sums
    )
    with jax.named_scope("swap"):
        other = lax.ppermute(partner_out, "tm", [(i, i ^ 1) for i in range(members)])
    own_out = attend_own(tables, query, keys, values, weights, halo_first)
    left = jnp.where(core == 0, own_out, other)
    right = jnp.where(core == 0, other, own_out)
    return jnp.concatenate([left, right], axis=1)[None]


def solution(mesh):
    return jax.shard_map(
        local,
        mesh=mesh,
        in_specs=(P("dp", "tm", None), P("dp", None), P("dp", None), P("dp", None), P("dp", None)),
        out_specs=P("dp", "tm", None),
        check_vma=False,
    )
```

```python
import functools
import math

import jax
import jax.numpy as jnp
from jax import lax
from jax.experimental import pallas as pl
from jax.experimental.pallas import tpu as pltpu
from jax.sharding import PartitionSpec as P

HEAD_DIM = 96
STRETCH = 256
LEFT = 2
LANES = 128
GROUPS = 4
EXP_SCALE = HEAD_DIM**-0.5 * math.log2(math.e)
REACH = LEFT * STRETCH
MIB = 1024 * 1024


def dot(a, b, dims=((1,), (0,))):
    return lax.dot_general(a, b, (dims, ((), ())), preferred_element_type=jnp.float32)


def head_window(head):
    first = head * HEAD_DIM // LANES * LANES
    last = -(-(head + 1) * HEAD_DIM // LANES) * LANES
    return first, last


def start_all(sems, pairs):
    copies = []
    for i, (*source, target) in enumerate(pairs):
        if len(source) == 1:
            copy = pltpu.make_async_copy(source[0], target, sems.at[i])
            copy.start()
        else:
            for n, choice in enumerate(source[0]):
                copy = pltpu.make_async_copy(choice, target, sems.at[i])
                pl.when(source[1] == n)(copy.start)
        copies.append(copy)
    return copies


class Blocks:
    def __init__(self, blocks, n_late, find):
        self.operands = [operand for block in blocks for operand in block]
        self.counts = [len(block) for block in blocks]
        self.rows = [block[0].shape[0] for block in blocks]
        self.n_late = n_late
        self.early_operands = self.operands[: sum(self.counts[:-n_late])]
        self.find = find

    def copies(self, refs, found, members, target, first=0, columns=slice(None)):
        pairs = []
        for i in members:
            at = sum(self.counts[:i])
            choices = [ref.at[:, columns] for ref in refs[at : at + self.counts[i]]]
            row, which = found[i]
            goal = target.at[pl.ds(pl.multiple_of(row - first, self.rows[i]), self.rows[i])]
            pairs.append((choices[0], goal) if len(choices) == 1 else (choices, which, goal))
        return pairs


def early_kernel(blocks, *refs):
    n = len(blocks.early_operands)
    own_ref, partner_ref, own_sum, partner_sum, w_s, own_s, partner_s, sems = refs[n:]
    found, late_first = blocks.find()
    depth = w_s.shape[0]
    first = jnp.where(late_first == 0, own_ref.shape[1] - depth, 0)
    members = range(len(found) - blocks.n_late)
    pairs = blocks.copies(refs, found, members, w_s, first)
    columns = pl.ds(pl.multiple_of(first, LANES), depth)
    pairs.append((own_ref.at[:, columns], own_s))
    pairs.append((partner_ref.at[:, columns], partner_s))
    for copy in start_all(sems, pairs):
        copy.wait()
    width = w_s.shape[1] // 3
    for x_s, out in ((own_s, own_sum), (partner_s, partner_sum)):
        for third in range(3):
            cols = slice(third * width, (third + 1) * width)
            out[:, cols] = dot(x_s[...], w_s[:, cols])


def late_kernel(blocks, start_ref, owner_ref, left_ref, *refs):
    n = len(blocks.operands)
    own_ref, partner_ref, halo_ref, own_sum, partner_sum = refs[n : n + 5]
    out_ref, q_out, k_out, v_out, kv_out, w_s, own_s, partner_s, sems = refs[n + 5 :]
    depth = w_s.shape[0]
    width = w_s.shape[1] // 3
    rows = own_s.shape[0]
    core = lax.axis_index("tm") % 2
    found, late_first = blocks.find()
    everything = range(len(found))
    pairs = blocks.copies(refs, found, everything[-blocks.n_late :], w_s, late_first)
    columns = pl.ds(pl.multiple_of(late_first, LANES), depth)
    pairs.append((partner_ref.at[:, columns], partner_s))
    pairs.append((own_ref.at[:, columns], own_s))
    n_first = len(pairs)
    pairs += blocks.copies(refs, found, everything, kv_out, 0, slice(width, 3 * width))
    copies = start_all(sems, pairs)
    for copy in copies[:n_first]:
        copy.wait()
    for x_s, acc, place in ((partner_s, partner_sum, 1 - core), (own_s, own_sum, core)):
        row = pl.multiple_of(place * rows, STRETCH)
        for third, (dst, skip) in enumerate(((q_out, 0), (k_out, REACH), (v_out, REACH))):
            cols = slice(third * width, (third + 1) * width)
            value = (acc[:, cols] + dot(x_s[...], w_s[:, cols])).astype(jnp.bfloat16)
            dst[pl.ds(pl.multiple_of(row + skip, STRETCH), rows), :] = value
    for copy in copies[n_first:]:
        copy.wait()

    @pl.when(core == 1)
    def _():
        k_out[:REACH, :] = dot(halo_ref[...], kv_out[:, :width]).astype(jnp.bfloat16)
        v_out[:REACH, :] = dot(halo_ref[...], kv_out[:, width:]).astype(jnp.bfloat16)

    chunks = rows // STRETCH

    def block_of(i):
        return jnp.where(i < chunks, (1 - core) * chunks + i, i - chunks + LEFT)

    count = jnp.where(core == 0, 2 * chunks - LEFT, chunks)
    attend(start_ref, owner_ref, left_ref, q_out, k_out, v_out, 0, count, block_of, out_ref)


def own_kernel(
    start_ref, owner_ref, left_ref, q_ref, k_ref, v_ref, kv_ref, halo_ref, done_ref, out_ref, k_s, v_s
):
    rows, width = out_ref.shape
    core = lax.axis_index("tm") % 2
    own = pl.multiple_of(core * rows + REACH, STRETCH)
    k_s[REACH:, :] = k_ref[pl.ds(own, rows), :]
    v_s[REACH:, :] = v_ref[pl.ds(own, rows), :]

    @pl.when(core == 0)
    def _():
        k_s[:REACH, :] = dot(halo_ref[...], kv_ref[:, :width]).astype(jnp.bfloat16)
        v_s[:REACH, :] = dot(halo_ref[...], kv_ref[:, width:]).astype(jnp.bfloat16)

    @pl.when(core == 1)
    def _():
        k_s[:REACH, :] = k_ref[rows : rows + REACH, :]
        v_s[:REACH, :] = v_ref[rows : rows + REACH, :]

    chunks = rows // STRETCH
    base = core * chunks
    count = jnp.where(core == 0, LEFT, chunks)

    def block_of(i):
        return base + i

    attend(start_ref, owner_ref, left_ref, q_ref, k_s, v_s, base, count, block_of, out_ref)

    @pl.when(core == 0)
    def _():
        out_ref[REACH:, :] = done_ref[rows : 2 * rows - REACH, :]


def attend(start_ref, owner_ref, left_ref, q_s, k_s, v_s, k_base, count, block_of, out_ref):
    width = out_ref.shape[1]
    chunks = q_s.shape[0] // STRETCH
    pair = lax.axis_index("tm") // 2
    lane = lax.broadcasted_iota(jnp.int32, (1, width), 1)
    heads = width // HEAD_DIM

    def attend_block(chunk, start, lowest, q_row, k_row, span, out_ref, out_row):
        first_key = (chunk + 1) * STRETCH - span
        key_frame = first_key + lax.broadcasted_iota(jnp.int32, (1, STRETCH), 1)
        bias = jnp.where(key_frame >= lowest, 0.0, -jnp.inf).astype(jnp.float32)
        frame = chunk * STRETCH + lax.broadcasted_iota(jnp.int32, (STRETCH, 1), 0)
        live = frame >= start
        windows = [head_window(head) for head in range(heads)]
        insides = [
            ((lane >= head * HEAD_DIM) & (lane < (head + 1) * HEAD_DIM))[:, first:last]
            for head, (first, last) in enumerate(windows)
        ]
        tiles = [jnp.zeros((STRETCH, LANES), jnp.float32) for _ in range(width // LANES)]

        def score(head):
            first, last = windows[head]
            q = q_s[pl.ds(q_row, STRETCH), first:last]
            q = jnp.where(insides[head], q, jnp.zeros_like(q))
            return dot(q, k_s[pl.ds(k_row, span), first:last], ((1,), (1,)))

        def weigh(scores):
            scores = [scores[:, at : at + STRETCH] for at in range(0, span, STRETCH)]
            scores[0] = scores[0] + bias
            top = functools.reduce(jnp.maximum, scores)
            top = jnp.max(top, axis=-1, keepdims=True)
            expo = [jnp.exp2((part - top) * EXP_SCALE) for part in scores]
            total = jnp.sum(functools.reduce(jnp.add, expo), axis=-1, keepdims=True)
            share = 1.0 / total
            return jnp.concatenate([(part * share).astype(jnp.bfloat16) for part in expo], axis=1)

        def mix(head, probs):
            first, last = windows[head]
            mixed = dot(probs, v_s[pl.ds(k_row, span), first:last])
            for tile in range(first // LANES, last // LANES):
                at = tile * LANES - first
                tiles[tile] = jnp.where(
                    insides[head][:, at : at + LANES], mixed[:, at : at + LANES], tiles[tile]
                )

        scores = score(0)
        probs = None
        for head in range(heads):
            following = score(head + 1) if head + 1 < heads else None
            weighed = weigh(scores)
            if probs is not None:
                mix(head - 1, probs)
            scores, probs = following, weighed
        mix(heads - 1, probs)
        for tile, value in enumerate(tiles):
            value = jnp.where(live, value, 0.0).astype(jnp.bfloat16)
            out_ref[pl.ds(out_row, STRETCH), tile * LANES : (tile + 1) * LANES] = value

    @pl.loop(0, count)
    def _(i):
        block = block_of(i)
        out_row = pl.multiple_of(i * STRETCH, STRETCH)
        q_row = pl.multiple_of(block * STRETCH, STRETCH)
        chunk = pair * chunks + block
        left = left_ref[0, chunk]
        start = start_ref[0, owner_ref[0, chunk]]
        lowest = jnp.maximum((chunk - left) * STRETCH, start)
        for back in range(LEFT + 1):

            @pl.when(left == back)
            def _():
                k_row = pl.multiple_of((block - k_base + LEFT - back) * STRETCH, STRETCH)
                span = (back + 1) * STRETCH
                attend_block(chunk, start, lowest, q_row, k_row, span, out_ref, out_row)


def after(value, *others):
    return lax.optimization_barrier((value, *others))[0]


SMEM_SPEC = pl.BlockSpec(memory_space=pltpu.SMEM)
VMEM_SPEC = pl.BlockSpec(memory_space=pltpu.VMEM)
ANY_SPEC = pl.BlockSpec(memory_space=pl.ANY)


def project_early(blocks, inputs, partner):
    rows, depth = inputs.shape
    depth -= depth // GROUPS
    cols = blocks.operands[0].shape[1]
    n_copies = len(blocks.counts) - blocks.n_late + 2
    return pl.pallas_call(
        functools.partial(early_kernel, blocks),
        out_shape=[jax.ShapeDtypeStruct((rows, cols), jnp.float32)] * 2,
        in_specs=[ANY_SPEC] * (len(blocks.early_operands) + 2),
        out_specs=[VMEM_SPEC] * 2,
        scratch_shapes=[
            pltpu.VMEM((depth, cols), jnp.bfloat16),
            pltpu.VMEM((rows, depth), jnp.bfloat16),
            pltpu.VMEM((rows, depth), jnp.bfloat16),
            pltpu.SemaphoreType.DMA((n_copies,)),
        ],
        compiler_params=pltpu.CompilerParams(vmem_limit_bytes=24 * MIB),
        cost_estimate=pl.CostEstimate(flops=0, bytes_accessed=0, transcendentals=0),
        name="project_early",
    )(*blocks.early_operands, inputs, partner)


def tail_kernel(x_ref, out_ref, sems):
    rows = out_ref.shape[0]
    for copy in start_all(sems, [(x_ref.at[x_ref.shape[0] - rows :, :], out_ref)]):
        copy.wait()


def take_tail(x):
    return pl.pallas_call(
        tail_kernel,
        out_shape=jax.ShapeDtypeStruct((REACH, x.shape[1]), x.dtype),
        in_specs=[ANY_SPEC],
        out_specs=VMEM_SPEC,
        scratch_shapes=[pltpu.SemaphoreType.DMA((1,))],
        compiler_params=pltpu.CompilerParams(vmem_limit_bytes=4 * MIB),
        name="take_tail",
    )(x)


def project_late_attend(tables, blocks, inputs, partner, halo, sums):
    rows, depth = inputs.shape
    late_depth = depth // GROUPS
    cols = blocks.operands[0].shape[1]
    width = cols // 3
    keys = jax.ShapeDtypeStruct((2 * rows + REACH, width), jnp.bfloat16)
    return pl.pallas_call(
        functools.partial(late_kernel, blocks),
        out_shape=[
            jax.ShapeDtypeStruct((2 * rows - REACH, width), jnp.bfloat16),
            jax.ShapeDtypeStruct((2 * rows, width), jnp.bfloat16),
            keys,
            keys,
            jax.ShapeDtypeStruct((depth, 2 * width), jnp.bfloat16),
        ],
        in_specs=[SMEM_SPEC] * 3 + [ANY_SPEC] * (len(blocks.operands) + 2) + [VMEM_SPEC] * 3,
        out_specs=[VMEM_SPEC] * 5,
        scratch_shapes=[
            pltpu.VMEM((late_depth, cols), jnp.bfloat16),
            pltpu.VMEM((rows, late_depth), jnp.bfloat16),
            pltpu.VMEM((rows, late_depth), jnp.bfloat16),
            pltpu.SemaphoreType.DMA((len(blocks.counts) + blocks.n_late + 2,)),
        ],
        compiler_params=pltpu.CompilerParams(vmem_limit_bytes=24 * MIB),
        name="project_late_attend",
    )(*tables, *blocks.operands, inputs, partner, halo, *sums)


def attend_own(tables, queries, keys, values, weights, halo, done):
    rows, width = queries.shape
    rows //= 2
    return pl.pallas_call(
        own_kernel,
        out_shape=jax.ShapeDtypeStruct((rows, width), jnp.bfloat16),
        in_specs=[SMEM_SPEC] * 3 + [VMEM_SPEC] * 6,
        out_specs=VMEM_SPEC,
        scratch_shapes=[pltpu.VMEM((rows + REACH, width), jnp.bfloat16)] * 2,
        compiler_params=pltpu.CompilerParams(vmem_limit_bytes=20 * MIB),
        name="attend_own",
    )(*tables, queries, keys, values, weights, halo, done)


def gather_neighbours(half, tail):
    size = half.shape[0]

    def along(name, block, hops):
        with jax.named_scope(name):
            return lax.ppermute(
                block, "dp", [(2 * a + s, 2 * b + s) for a, b in hops for s in range(2)]
            )

    def across(name, block, places):
        with jax.named_scope(name):
            return lax.ppermute(
                block, "dp", [(2 * a + s, 2 * a + 1 - s) for a in places for s in range(2)]
            )

    line, ends, middles = range(4), (0, 3), (1, 2)
    outward = [(1, 0), (2, 3)]
    between = [(1, 2), (2, 1)]
    near = along("near", half, outward + [(0, 1), (3, 2)])
    mid = along("mid", after(half, tail), between)
    half_across = across("half_across", half, line)
    mid_far = along("mid_far", near, between)
    near_across = across("near_across", after(near, half_across, mid), line)
    end_mid = along("end_mid", mid, outward)
    mid_across = across("mid_across", after(mid, near_across, mid_far), middles)
    end_mid_across = across("end_mid_across", after(end_mid, near_across), ends)
    end_far = along("end_far", after(mid_far, end_mid), outward)
    mid_far_across = across("mid_far_across", after(mid_far, mid_across, end_far), middles)
    end_far_across = across("end_far_across", after(end_far, near_across), ends)

    def find():
        index = lax.axis_index("dp")
        place, side = index // 2, index % 2
        is_end = jnp.where((place == 0) | (place == 3), 1, 0)
        second = jnp.where(is_end == 1, place ^ 2, 3 - place)
        third = jnp.where(is_end == 1, 3 - place, place ^ 2)
        spots = (place, place ^ 1, second, third)
        found = [((2 * spot + (side ^ n)) * size, is_end) for spot in spots for n in range(2)]
        return found, third * 2 * size

    blocks = [
        (half,),
        (half_across,),
        (near,),
        (near_across,),
        (mid, end_mid),
        (mid_across, end_mid_across),
        (mid_far, end_far),
        (mid_far_across, end_far_across),
    ]
    marks = (
        (near_across, mid_far, end_mid),
        (mid_across, end_mid_across, end_far),
        (mid_far_across, end_far_across),
    )
    return Blocks(blocks, 2, find), marks


def local(frames, w_qkv, utt_start, stretch_utt, left_stretches):
    inputs = frames[0]
    depth = inputs.shape[1]
    members = lax.axis_size("tm")
    core = lax.axis_index("tm") % 2

    inner = w_qkv.shape[1] // 3
    width = inner // 2
    thirds = [w_qkv[:, i * inner : (i + 1) * inner] for i in range(3)]
    half = jnp.concatenate(
        [jnp.where(core == 0, third[:, :width], third[:, width:]) for third in thirds], axis=1
    )

    tail = take_tail(after(inputs, half))
    with jax.named_scope("partner"):
        partner = lax.ppermute(inputs, "tm", [(i, i ^ 1) for i in range(members)])
    if lax.axis_size("dp") == 8:
        blocks, marks = gather_neighbours(half, tail)
    else:
        weights = lax.all_gather(half, "dp", axis=0, tiled=True)
        late_first = depth - depth // GROUPS
        found = [(0, 0), (late_first, 0)], late_first
        parts = [(weights[:late_first],), (weights[late_first:],)]
        blocks, marks = Blocks(parts, 1, lambda: found), ((half,),) * 3

    with jax.named_scope("halo"):
        halo = lax.ppermute(
            after(tail, *marks[0]), "tm", [(i, i + 2) for i in range(1, members - 2, 2)]
        )

    tables = (utt_start, stretch_utt, left_stretches)
    sums = project_early(blocks, inputs, partner)
    with jax.named_scope("halo_first"):
        halo_first = lax.ppermute(
            after(halo, *marks[2], *sums), "tm", [(i + 1, i) for i in range(0, members, 2)]
        )
    attended, queries, keys, values, weights = project_late_attend(
        tables, blocks, inputs, partner, halo, sums
    )
    with jax.named_scope("swap"):
        other = lax.ppermute(attended, "tm", [(i, i ^ 1) for i in range(members)])
    own_out = attend_own(tables, queries, keys, values, weights, halo_first, attended)
    other = other[: inputs.shape[0]]
    left = jnp.where(core == 0, own_out, other)
    right = jnp.where(core == 0, other, own_out)
    return jnp.concatenate([left, right], axis=1)[None]


def solution(mesh):
    return jax.shard_map(
        local,
        mesh=mesh,
        in_specs=(P("dp", "tm", None), P("dp", None), P("dp", None), P("dp", None), P("dp", None)),
        out_specs=P("dp", "tm", None),
        check_vma=False,
    )
```

```python
import functools
import math

import jax
import jax.numpy as jnp
from jax import lax
from jax.experimental import pallas as pl
from jax.experimental.pallas import tpu as pltpu
from jax.sharding import PartitionSpec as P

HEAD_DIM = 96
STRETCH = 256
LEFT = 2
LANES = 128
GROUPS = 4
EXP_SCALE = HEAD_DIM**-0.5 * math.log2(math.e)
REACH = LEFT * STRETCH
MIB = 1024 * 1024


def dot(a, b, dims=((1,), (0,))):
    return lax.dot_general(a, b, (dims, ((), ())), preferred_element_type=jnp.float32)


def head_window(head):
    first = head * HEAD_DIM // LANES * LANES
    last = -(-(head + 1) * HEAD_DIM // LANES) * LANES
    return first, last


def start_all(sems, pairs):
    copies = []
    for i, (*source, target) in enumerate(pairs):
        if len(source) == 1:
            copy = pltpu.make_async_copy(source[0], target, sems.at[i])
            copy.start()
        else:
            for n, choice in enumerate(source[0]):
                copy = pltpu.make_async_copy(choice, target, sems.at[i])
                pl.when(source[1] == n)(copy.start)
        copies.append(copy)
    return copies


class Blocks:
    def __init__(self, blocks, n_late, find):
        self.operands = [operand for block in blocks for operand in block]
        self.counts = [len(block) for block in blocks]
        self.rows = [block[0].shape[0] for block in blocks]
        self.n_late = n_late
        self.early_operands = self.operands[: sum(self.counts[:-n_late])]
        self.find = find

    def copies(self, refs, found, members, target, first=0, columns=slice(None)):
        pairs = []
        for i in members:
            at = sum(self.counts[:i])
            choices = [ref.at[:, columns] for ref in refs[at : at + self.counts[i]]]
            row, which = found[i]
            goal = target.at[pl.ds(pl.multiple_of(row - first, self.rows[i]), self.rows[i])]
            pairs.append((choices[0], goal) if len(choices) == 1 else (choices, which, goal))
        return pairs


def early_kernel(blocks, *refs):
    n = len(blocks.early_operands)
    own_ref, partner_ref, own_sum, partner_sum, w_s, own_s, partner_s, sems = refs[n:]
    found, late_first = blocks.find()
    depth = w_s.shape[0]
    first = jnp.where(late_first == 0, own_ref.shape[1] - depth, 0)
    members = range(len(found) - blocks.n_late)
    pairs = blocks.copies(refs, found, members, w_s, first)
    columns = pl.ds(pl.multiple_of(first, LANES), depth)
    pairs.append((own_ref.at[:, columns], own_s))
    pairs.append((partner_ref.at[:, columns], partner_s))
    for copy in start_all(sems, pairs):
        copy.wait()
    width = w_s.shape[1] // 3
    for x_s, out in ((own_s, own_sum), (partner_s, partner_sum)):
        for third in range(3):
            cols = slice(third * width, (third + 1) * width)
            out[:, cols] = dot(x_s[...], w_s[:, cols])


def late_kernel(blocks, table_ref, *refs):
    n = len(blocks.operands)
    own_ref, partner_ref, halo_ref, own_sum, partner_sum = refs[n : n + 5]
    out_ref, q_own, k_out, v_out, kv_out, q_partner, w_s, own_s, partner_s, sems = refs[n + 5 :]
    depth = w_s.shape[0]
    width = w_s.shape[1] // 3
    rows = own_s.shape[0]
    core = lax.axis_index("tm") % 2
    found, late_first = blocks.find()
    everything = range(len(found))
    pairs = blocks.copies(refs, found, everything[-blocks.n_late :], w_s, late_first)
    columns = pl.ds(pl.multiple_of(late_first, LANES), depth)
    pairs.append((partner_ref.at[:, columns], partner_s))
    pairs.append((own_ref.at[:, columns], own_s))
    n_first = len(pairs)
    pairs += blocks.copies(refs, found, everything, kv_out, 0, slice(width, 3 * width))
    copies = start_all(sems, pairs)
    for copy in copies[:n_first]:
        copy.wait()
    for x_s, acc, query, place in (
        (partner_s, partner_sum, q_partner, 1 - core),
        (own_s, own_sum, q_own, core),
    ):
        row = pl.multiple_of(place * rows + REACH, STRETCH)
        for third, dst in enumerate((query, k_out, v_out)):
            cols = slice(third * width, (third + 1) * width)
            value = (acc[:, cols] + dot(x_s[...], w_s[:, cols])).astype(jnp.bfloat16)
            if third == 0:
                dst[...] = value
            else:
                dst[pl.ds(row, rows), :] = value
    for copy in copies[n_first:]:
        copy.wait()

    @pl.when(core == 1)
    def _():
        k_out[:REACH, :] = dot(halo_ref[...], kv_out[:, :width]).astype(jnp.bfloat16)
        v_out[:REACH, :] = dot(halo_ref[...], kv_out[:, width:]).astype(jnp.bfloat16)

    first = pl.multiple_of((1 - core) * rows, STRETCH)
    attend(table_ref, 1 - core, q_partner, 0, k_out, v_out, first, out_ref)


def own_kernel(
    table_ref, q_ref, k_ref, v_ref, kv_ref, halo_ref, out_ref, k_s, v_s
):
    rows, width = out_ref.shape
    core = lax.axis_index("tm") % 2
    own = pl.multiple_of(core * rows + REACH, STRETCH)
    k_s[REACH:, :] = k_ref[pl.ds(own, rows), :]
    v_s[REACH:, :] = v_ref[pl.ds(own, rows), :]

    @pl.when(core == 0)
    def _():
        k_s[:REACH, :] = dot(halo_ref[...], kv_ref[:, :width]).astype(jnp.bfloat16)
        v_s[:REACH, :] = dot(halo_ref[...], kv_ref[:, width:]).astype(jnp.bfloat16)

    @pl.when(core == 1)
    def _():
        k_s[:REACH, :] = k_ref[rows : rows + REACH, :]
        v_s[:REACH, :] = v_ref[rows : rows + REACH, :]

    attend(table_ref, core, q_ref, 0, k_s, v_s, 0, out_ref)


def attend(table_ref, place, q_s, q_first, k_s, v_s, k_first, out_ref):
    rows, width = out_ref.shape
    chunks = rows // STRETCH
    pair = lax.axis_index("tm") // 2
    lane = lax.broadcasted_iota(jnp.int32, (1, width), 1)
    heads = width // HEAD_DIM
    ones = jnp.ones((2 * LANES, LANES), jnp.bfloat16)

    def attend_block(chunk, start, lowest, q_row, k_row, span, out_ref, out_row):
        first_key = (chunk + 1) * STRETCH - span
        key_frame = first_key + lax.broadcasted_iota(jnp.int32, (1, STRETCH), 1)
        bias = jnp.where(key_frame >= lowest, 0.0, -jnp.inf).astype(jnp.float32)
        frame = chunk * STRETCH + lax.broadcasted_iota(jnp.int32, (STRETCH, 1), 0)
        live = frame >= start
        windows = [head_window(head) for head in range(heads)]
        insides = [
            ((lane >= head * HEAD_DIM) & (lane < (head + 1) * HEAD_DIM))[:, first:last]
            for head, (first, last) in enumerate(windows)
        ]
        tiles = [jnp.zeros((STRETCH, LANES), jnp.float32) for _ in range(width // LANES)]

        def score(head):
            first, last = windows[head]
            q = q_s[pl.ds(q_row, STRETCH), first:last]
            q = jnp.where(insides[head], q, jnp.zeros_like(q))
            return dot(q, k_s[pl.ds(k_row, span), first:last], ((1,), (1,)))

        def weigh(scores):
            scores = [scores[:, at : at + STRETCH] for at in range(0, span, STRETCH)]
            scores[0] = scores[0] + bias
            top = functools.reduce(jnp.maximum, scores)
            top = jnp.max(top, axis=-1, keepdims=True)
            expo = [jnp.exp2((part - top) * EXP_SCALE) for part in scores]
            total = functools.reduce(jnp.add, expo)
            total = functools.reduce(
                jnp.add, [total[:, at : at + LANES] for at in range(0, STRETCH, LANES)]
            )
            high = total.astype(jnp.bfloat16)
            low = (total - high.astype(jnp.float32)).astype(jnp.bfloat16)
            share = 1.0 / dot(jnp.concatenate([high, low], axis=1), ones)
            share = jnp.concatenate([share] * (STRETCH // LANES), axis=1)
            return jnp.concatenate([(part * share).astype(jnp.bfloat16) for part in expo], axis=1)

        def mix(head, probs):
            first, last = windows[head]
            mixed = dot(probs, v_s[pl.ds(k_row, span), first:last])
            for tile in range(first // LANES, last // LANES):
                at = tile * LANES - first
                tiles[tile] = jnp.where(
                    insides[head][:, at : at + LANES], mixed[:, at : at + LANES], tiles[tile]
                )

        scores = score(0)
        probs = None
        for head in range(heads):
            following = score(head + 1) if head + 1 < heads else None
            weighed = weigh(scores)
            if probs is not None:
                mix(head - 1, probs)
            scores, probs = following, weighed
        mix(heads - 1, probs)
        for tile, value in enumerate(tiles):
            value = jnp.where(live, value, 0.0).astype(jnp.bfloat16)
            out_ref[pl.ds(out_row, STRETCH), tile * LANES : (tile + 1) * LANES] = value

    @pl.loop(0, chunks)
    def _(i):
        row = pl.multiple_of(i * STRETCH, STRETCH)
        chunk = (pair * 2 + place) * chunks + i
        left = table_ref[2, chunk]
        start = table_ref[0, table_ref[1, chunk]]
        lowest = jnp.maximum((chunk - left) * STRETCH, start)
        for back in range(LEFT + 1):

            @pl.when(left == back)
            def _():
                q_row = pl.multiple_of(q_first + row, STRETCH)
                k_row = pl.multiple_of(k_first + row + (LEFT - back) * STRETCH, STRETCH)
                attend_block(chunk, start, lowest, q_row, k_row, (back + 1) * STRETCH, out_ref, row)


def after(value, *others):
    return lax.optimization_barrier((value, *others))[0]


SMEM_SPEC = pl.BlockSpec(memory_space=pltpu.SMEM)
VMEM_SPEC = pl.BlockSpec(memory_space=pltpu.VMEM)
ANY_SPEC = pl.BlockSpec(memory_space=pl.ANY)


def project_early(blocks, inputs, partner):
    rows, depth = inputs.shape
    depth -= depth // GROUPS
    cols = blocks.operands[0].shape[1]
    n_copies = len(blocks.counts) - blocks.n_late + 2
    return pl.pallas_call(
        functools.partial(early_kernel, blocks),
        out_shape=[jax.ShapeDtypeStruct((rows, cols), jnp.float32)] * 2,
        in_specs=[ANY_SPEC] * (len(blocks.early_operands) + 2),
        out_specs=[VMEM_SPEC] * 2,
        scratch_shapes=[
            pltpu.VMEM((depth, cols), jnp.bfloat16),
            pltpu.VMEM((rows, depth), jnp.bfloat16),
            pltpu.VMEM((rows, depth), jnp.bfloat16),
            pltpu.SemaphoreType.DMA((n_copies,)),
        ],
        compiler_params=pltpu.CompilerParams(vmem_limit_bytes=24 * MIB),
        cost_estimate=pl.CostEstimate(flops=0, bytes_accessed=0, transcendentals=0),
        name="project_early",
    )(*blocks.early_operands, inputs, partner)


def tail_kernel(x_ref, out_ref, sems):
    rows = out_ref.shape[0]
    for copy in start_all(sems, [(x_ref.at[x_ref.shape[0] - rows :, :], out_ref)]):
        copy.wait()


def take_tail(x):
    return pl.pallas_call(
        tail_kernel,
        out_shape=jax.ShapeDtypeStruct((REACH, x.shape[1]), x.dtype),
        in_specs=[ANY_SPEC],
        out_specs=VMEM_SPEC,
        scratch_shapes=[pltpu.SemaphoreType.DMA((1,))],
        compiler_params=pltpu.CompilerParams(vmem_limit_bytes=4 * MIB),
        name="take_tail",
    )(x)


def project_late_attend(table, blocks, inputs, partner, halo, sums):
    rows, depth = inputs.shape
    late_depth = depth // GROUPS
    cols = blocks.operands[0].shape[1]
    width = cols // 3
    keys = jax.ShapeDtypeStruct((2 * rows + REACH, width), jnp.bfloat16)
    queries = jax.ShapeDtypeStruct((rows, width), jnp.bfloat16)
    return pl.pallas_call(
        functools.partial(late_kernel, blocks),
        out_shape=[
            queries,
            queries,
            keys,
            keys,
            jax.ShapeDtypeStruct((depth, 2 * width), jnp.bfloat16),
        ],
        in_specs=[SMEM_SPEC] + [ANY_SPEC] * (len(blocks.operands) + 2) + [VMEM_SPEC] * 3,
        out_specs=[VMEM_SPEC] * 5,
        scratch_shapes=[
            pltpu.VMEM((rows, width), jnp.bfloat16),
            pltpu.VMEM((late_depth, cols), jnp.bfloat16),
            pltpu.VMEM((rows, late_depth), jnp.bfloat16),
            pltpu.VMEM((rows, late_depth), jnp.bfloat16),
            pltpu.SemaphoreType.DMA((len(blocks.counts) + blocks.n_late + 2,)),
        ],
        compiler_params=pltpu.CompilerParams(vmem_limit_bytes=24 * MIB),
        name="project_late_attend",
    )(table, *blocks.operands, inputs, partner, halo, *sums)


def attend_own(table, query, keys, values, weights, halo):
    rows, width = query.shape
    return pl.pallas_call(
        own_kernel,
        out_shape=jax.ShapeDtypeStruct((rows, width), jnp.bfloat16),
        in_specs=[SMEM_SPEC] + [VMEM_SPEC] * 5,
        out_specs=VMEM_SPEC,
        scratch_shapes=[pltpu.VMEM((rows + REACH, width), jnp.bfloat16)] * 2,
        compiler_params=pltpu.CompilerParams(vmem_limit_bytes=20 * MIB),
        name="attend_own",
    )(table, query, keys, values, weights, halo)


def gather_neighbours(half):
    size = half.shape[0]

    def along(name, block, hops):
        with jax.named_scope(name):
            return lax.ppermute(
                block, "dp", [(2 * a + s, 2 * b + s) for a, b in hops for s in range(2)]
            )

    def across(name, block, places):
        with jax.named_scope(name):
            return lax.ppermute(
                block, "dp", [(2 * a + s, 2 * a + 1 - s) for a in places for s in range(2)]
            )

    line, ends, middles = range(4), (0, 3), (1, 2)
    outward = [(1, 0), (2, 3)]
    between = [(1, 2), (2, 1)]
    near = along("near", half, outward + [(0, 1), (3, 2)])
    mid = along("mid", half, between)
    half_across = across("half_across", half, line)
    mid_far = along("mid_far", near, between)
    near_across = across("near_across", after(near, half_across, mid), line)
    end_mid = along("end_mid", mid, outward)
    mid_across = across("mid_across", after(mid, near_across, mid_far), middles)
    end_mid_across = across("end_mid_across", after(end_mid, near_across), ends)
    end_far = along("end_far", after(mid_far, end_mid), outward)
    mid_far_across = across("mid_far_across", after(mid_far, mid_across, end_far), middles)
    end_far_across = across("end_far_across", after(end_far, end_mid_across), ends)

    def find():
        index = lax.axis_index("dp")
        place, side = index // 2, index % 2
        is_end = jnp.where((place == 0) | (place == 3), 1, 0)
        second = jnp.where(is_end == 1, place ^ 2, 3 - place)
        third = jnp.where(is_end == 1, 3 - place, place ^ 2)
        spots = (place, place ^ 1, second, third)
        found = [((2 * spot + (side ^ n)) * size, is_end) for spot in spots for n in range(2)]
        return found, third * 2 * size

    blocks = [
        (half,),
        (half_across,),
        (near,),
        (near_across,),
        (mid, end_mid),
        (mid_across, end_mid_across),
        (mid_far, end_far),
        (mid_far_across, end_far_across),
    ]
    marks = (
        (near_across, mid_far, end_mid),
        (mid_across, end_mid_across, end_far),
        (mid_far_across, end_far_across),
    )
    return Blocks(blocks, 2, find), marks


def local(frames, w_qkv, utt_start, stretch_utt, left_stretches):
    inputs = frames[0]
    depth = inputs.shape[1]
    members = lax.axis_size("tm")
    core = lax.axis_index("tm") % 2

    inner = w_qkv.shape[1] // 3
    width = inner // 2
    thirds = [w_qkv[:, i * inner : (i + 1) * inner] for i in range(3)]
    half = jnp.concatenate(
        [jnp.where(core == 0, third[:, :width], third[:, width:]) for third in thirds], axis=1
    )

    starts = jnp.pad(utt_start, ((0, 0), (0, stretch_utt.shape[1] - utt_start.shape[1])))
    table = jnp.concatenate([starts, stretch_utt, left_stretches], axis=0)
    half = after(half, table)
    tail = take_tail(after(inputs, half))
    with jax.named_scope("partner"):
        partner = lax.ppermute(inputs, "tm", [(i, i ^ 1) for i in range(members)])
    if lax.axis_size("dp") == 8:
        blocks, marks = gather_neighbours(half)
    else:
        weights = lax.all_gather(half, "dp", axis=0, tiled=True)
        late_first = depth - depth // GROUPS
        found = [(0, 0), (late_first, 0)], late_first
        parts = [(weights[:late_first],), (weights[late_first:],)]
        blocks, marks = Blocks(parts, 1, lambda: found), ((half,),) * 3

    with jax.named_scope("halo"):
        halo = lax.ppermute(
            after(tail, *marks[0]), "tm", [(i, i + 2) for i in range(1, members - 2, 2)]
        )

    sums = project_early(blocks, inputs, partner)
    with jax.named_scope("halo_first"):
        halo_first = lax.ppermute(
            after(halo, *marks[2], *sums), "tm", [(i + 1, i) for i in range(0, members, 2)]
        )
    partner_out, query, keys, values, weights = project_late_attend(
        table, blocks, inputs, partner, halo, sums
    )
    with jax.named_scope("swap"):
        other = lax.ppermute(partner_out, "tm", [(i, i ^ 1) for i in range(members)])
    own_out = attend_own(table, query, keys, values, weights, halo_first)
    left = jnp.where(core == 0, own_out, other)
    right = jnp.where(core == 0, other, own_out)
    return jnp.concatenate([left, right], axis=1)[None]


def solution(mesh):
    return jax.shard_map(
        local,
        mesh=mesh,
        in_specs=(P("dp", "tm", None), P("dp", None), P("dp", None), P("dp", None), P("dp", None)),
        out_specs=P("dp", "tm", None),
        check_vma=False,
    )
```

```python
import functools
import math

import jax
import jax.numpy as jnp
from jax import lax
from jax.experimental import pallas as pl
from jax.experimental.pallas import tpu as pltpu
from jax.sharding import PartitionSpec as P

HEAD_DIM = 96
STRETCH = 256
LEFT = 2
LANES = 128
GROUPS = 4
EXP_SCALE = HEAD_DIM**-0.5 * math.log2(math.e)
REACH = LEFT * STRETCH
MIB = 1024 * 1024


def dot(a, b, dims=((1,), (0,))):
    return lax.dot_general(a, b, (dims, ((), ())), preferred_element_type=jnp.float32)


def head_window(head):
    first = head * HEAD_DIM // LANES * LANES
    last = -(-(head + 1) * HEAD_DIM // LANES) * LANES
    return first, last


def start_all(sems, pairs):
    copies = []
    for i, (*source, target) in enumerate(pairs):
        if len(source) == 1:
            copy = pltpu.make_async_copy(source[0], target, sems.at[i])
            copy.start()
        else:
            for n, choice in enumerate(source[0]):
                copy = pltpu.make_async_copy(choice, target, sems.at[i])
                pl.when(source[1] == n)(copy.start)
        copies.append(copy)
    return copies


class Blocks:
    def __init__(self, blocks, n_late, find):
        self.operands = [operand for block in blocks for operand in block]
        self.counts = [len(block) for block in blocks]
        self.rows = [block[0].shape[0] for block in blocks]
        self.n_late = n_late
        self.early_operands = self.operands[: sum(self.counts[:-n_late])]
        self.find = find

    def copies(self, refs, found, members, target, first=0, columns=slice(None)):
        pairs = []
        for i in members:
            at = sum(self.counts[:i])
            choices = [ref.at[:, columns] for ref in refs[at : at + self.counts[i]]]
            row, which = found[i]
            goal = target.at[pl.ds(pl.multiple_of(row - first, self.rows[i]), self.rows[i])]
            pairs.append((choices[0], goal) if len(choices) == 1 else (choices, which, goal))
        return pairs


def early_kernel(blocks, *refs):
    n = len(blocks.early_operands)
    own_ref, partner_ref, own_sum, partner_sum, w_s, own_s, partner_s, sems = refs[n:]
    found, late_first = blocks.find()
    depth = w_s.shape[0]
    first = jnp.where(late_first == 0, own_ref.shape[1] - depth, 0)
    members = range(len(found) - blocks.n_late)
    pairs = blocks.copies(refs, found, members, w_s, first)
    columns = pl.ds(pl.multiple_of(first, LANES), depth)
    pairs.append((own_ref.at[:, columns], own_s))
    pairs.append((partner_ref.at[:, columns], partner_s))
    for copy in start_all(sems, pairs):
        copy.wait()
    width = w_s.shape[1] // 3
    for x_s, out in ((own_s, own_sum), (partner_s, partner_sum)):
        for third in range(3):
            cols = slice(third * width, (third + 1) * width)
            out[:, cols] = dot(x_s[...], w_s[:, cols])


def late_kernel(blocks, start_ref, owner_ref, left_ref, *refs):
    n = len(blocks.operands)
    own_ref, partner_ref, halo_ref, own_sum, partner_sum = refs[n : n + 5]
    out_ref, q_own, k_out, v_out, kv_out, q_partner, w_s, own_s, partner_s, sems = refs[n + 5 :]
    depth = w_s.shape[0]
    width = w_s.shape[1] // 3
    rows = own_s.shape[0]
    core = lax.axis_index("tm") % 2
    found, late_first = blocks.find()
    everything = range(len(found))
    pairs = blocks.copies(refs, found, everything[-blocks.n_late :], w_s, late_first)
    columns = pl.ds(pl.multiple_of(late_first, LANES), depth)
    pairs.append((partner_ref.at[:, columns], partner_s))
    pairs.append((own_ref.at[:, columns], own_s))
    n_first = len(pairs)
    pairs += blocks.copies(refs, found, everything, kv_out, 0, slice(width, 3 * width))
    copies = start_all(sems, pairs)
    for copy in copies[:n_first]:
        copy.wait()
    for x_s, acc, query, place in (
        (partner_s, partner_sum, q_partner, 1 - core),
        (own_s, own_sum, q_own, core),
    ):
        row = pl.multiple_of(place * rows + REACH, STRETCH)
        for third, dst in enumerate((query, k_out, v_out)):
            cols = slice(third * width, (third + 1) * width)
            value = (acc[:, cols] + dot(x_s[...], w_s[:, cols])).astype(jnp.bfloat16)
            if third == 0:
                dst[...] = value
            else:
                dst[pl.ds(row, rows), :] = value
    for copy in copies[n_first:]:
        copy.wait()

    @pl.when(core == 1)
    def _():
        k_out[:REACH, :] = dot(halo_ref[...], kv_out[:, :width]).astype(jnp.bfloat16)
        v_out[:REACH, :] = dot(halo_ref[...], kv_out[:, width:]).astype(jnp.bfloat16)

    first = pl.multiple_of((1 - core) * rows, STRETCH)
    attend(start_ref, owner_ref, left_ref, 1 - core, q_partner, 0, k_out, v_out, first, out_ref)


def own_kernel(
    start_ref, owner_ref, left_ref, q_ref, k_ref, v_ref, kv_ref, halo_ref, out_ref, k_s, v_s
):
    rows, width = out_ref.shape
    core = lax.axis_index("tm") % 2
    own = pl.multiple_of(core * rows + REACH, STRETCH)
    k_s[REACH:, :] = k_ref[pl.ds(own, rows), :]
    v_s[REACH:, :] = v_ref[pl.ds(own, rows), :]

    @pl.when(core == 0)
    def _():
        k_s[:REACH, :] = dot(halo_ref[...], kv_ref[:, :width]).astype(jnp.bfloat16)
        v_s[:REACH, :] = dot(halo_ref[...], kv_ref[:, width:]).astype(jnp.bfloat16)

    @pl.when(core == 1)
    def _():
        k_s[:REACH, :] = k_ref[rows : rows + REACH, :]
        v_s[:REACH, :] = v_ref[rows : rows + REACH, :]

    attend(start_ref, owner_ref, left_ref, core, q_ref, 0, k_s, v_s, 0, out_ref)


def attend(start_ref, owner_ref, left_ref, place, q_s, q_first, k_s, v_s, k_first, out_ref):
    rows, width = out_ref.shape
    chunks = rows // STRETCH
    pair = lax.axis_index("tm") // 2
    lane = lax.broadcasted_iota(jnp.int32, (1, width), 1)
    heads = width // HEAD_DIM

    def attend_block(chunk, start, lowest, q_row, k_row, span, out_ref, out_row):
        first_key = (chunk + 1) * STRETCH - span
        key_frame = first_key + lax.broadcasted_iota(jnp.int32, (1, STRETCH), 1)
        bias = jnp.where(key_frame >= lowest, 0.0, -jnp.inf).astype(jnp.float32)
        frame = chunk * STRETCH + lax.broadcasted_iota(jnp.int32, (STRETCH, 1), 0)
        live = frame >= start
        windows = [head_window(head) for head in range(heads)]
        insides = [
            ((lane >= head * HEAD_DIM) & (lane < (head + 1) * HEAD_DIM))[:, first:last]
            for head, (first, last) in enumerate(windows)
        ]
        tiles = [jnp.zeros((STRETCH, LANES), jnp.float32) for _ in range(width // LANES)]

        def score(head):
            first, last = windows[head]
            q = q_s[pl.ds(q_row, STRETCH), first:last]
            q = jnp.where(insides[head], q, jnp.zeros_like(q))
            return dot(q, k_s[pl.ds(k_row, span), first:last], ((1,), (1,)))

        def weigh(scores):
            scores = [scores[:, at : at + STRETCH] for at in range(0, span, STRETCH)]
            scores[0] = scores[0] + bias
            top = functools.reduce(jnp.maximum, scores)
            top = jnp.max(top, axis=-1, keepdims=True)
            expo = [jnp.exp2((part - top) * EXP_SCALE) for part in scores]
            total = jnp.sum(functools.reduce(jnp.add, expo), axis=-1, keepdims=True)
            share = 1.0 / total
            return jnp.concatenate([(part * share).astype(jnp.bfloat16) for part in expo], axis=1)

        def mix(head, probs):
            first, last = windows[head]
            mixed = dot(probs, v_s[pl.ds(k_row, span), first:last])
            for tile in range(first // LANES, last // LANES):
                at = tile * LANES - first
                tiles[tile] = jnp.where(
                    insides[head][:, at : at + LANES], mixed[:, at : at + LANES], tiles[tile]
                )

        scores = score(0)
        probs = None
        for head in range(heads):
            following = score(head + 1) if head + 1 < heads else None
            weighed = weigh(scores)
            if probs is not None:
                mix(head - 1, probs)
            scores, probs = following, weighed
        mix(heads - 1, probs)
        for tile, value in enumerate(tiles):
            value = jnp.where(live, value, 0.0).astype(jnp.bfloat16)
            out_ref[pl.ds(out_row, STRETCH), tile * LANES : (tile + 1) * LANES] = value

    @pl.loop(0, chunks)
    def _(i):
        row = pl.multiple_of(i * STRETCH, STRETCH)
        chunk = (pair * 2 + place) * chunks + i
        left = left_ref[0, chunk]
        start = start_ref[0, owner_ref[0, chunk]]
        lowest = jnp.maximum((chunk - left) * STRETCH, start)
        for back in range(LEFT + 1):

            @pl.when(left == back)
            def _():
                q_row = pl.multiple_of(q_first + row, STRETCH)
                k_row = pl.multiple_of(k_first + row + (LEFT - back) * STRETCH, STRETCH)
                attend_block(chunk, start, lowest, q_row, k_row, (back + 1) * STRETCH, out_ref, row)


def after(value, *others):
    return lax.optimization_barrier((value, *others))[0]


SMEM_SPEC = pl.BlockSpec(memory_space=pltpu.SMEM)
VMEM_SPEC = pl.BlockSpec(memory_space=pltpu.VMEM)
ANY_SPEC = pl.BlockSpec(memory_space=pl.ANY)


def project_early(blocks, inputs, partner):
    rows, depth = inputs.shape
    depth -= depth // GROUPS
    cols = blocks.operands[0].shape[1]
    n_copies = len(blocks.counts) - blocks.n_late + 2
    return pl.pallas_call(
        functools.partial(early_kernel, blocks),
        out_shape=[jax.ShapeDtypeStruct((rows, cols), jnp.float32)] * 2,
        in_specs=[ANY_SPEC] * (len(blocks.early_operands) + 2),
        out_specs=[VMEM_SPEC] * 2,
        scratch_shapes=[
            pltpu.VMEM((depth, cols), jnp.bfloat16),
            pltpu.VMEM((rows, depth), jnp.bfloat16),
            pltpu.VMEM((rows, depth), jnp.bfloat16),
            pltpu.SemaphoreType.DMA((n_copies,)),
        ],
        compiler_params=pltpu.CompilerParams(vmem_limit_bytes=24 * MIB),
        cost_estimate=pl.CostEstimate(flops=0, bytes_accessed=0, transcendentals=0),
        name="project_early",
    )(*blocks.early_operands, inputs, partner)


def tail_kernel(x_ref, out_ref, sems):
    rows = out_ref.shape[0]
    for copy in start_all(sems, [(x_ref.at[x_ref.shape[0] - rows :, :], out_ref)]):
        copy.wait()


def take_tail(x):
    return pl.pallas_call(
        tail_kernel,
        out_shape=jax.ShapeDtypeStruct((REACH, x.shape[1]), x.dtype),
        in_specs=[ANY_SPEC],
        out_specs=VMEM_SPEC,
        scratch_shapes=[pltpu.SemaphoreType.DMA((1,))],
        compiler_params=pltpu.CompilerParams(vmem_limit_bytes=4 * MIB),
        name="take_tail",
    )(x)


def project_late_attend(tables, blocks, inputs, partner, halo, sums):
    rows, depth = inputs.shape
    late_depth = depth // GROUPS
    cols = blocks.operands[0].shape[1]
    width = cols // 3
    keys = jax.ShapeDtypeStruct((2 * rows + REACH, width), jnp.bfloat16)
    queries = jax.ShapeDtypeStruct((rows, width), jnp.bfloat16)
    return pl.pallas_call(
        functools.partial(late_kernel, blocks),
        out_shape=[
            queries,
            queries,
            keys,
            keys,
            jax.ShapeDtypeStruct((depth, 2 * width), jnp.bfloat16),
        ],
        in_specs=[SMEM_SPEC] * 3 + [ANY_SPEC] * (len(blocks.operands) + 2) + [VMEM_SPEC] * 3,
        out_specs=[VMEM_SPEC] * 5,
        scratch_shapes=[
            pltpu.VMEM((rows, width), jnp.bfloat16),
            pltpu.VMEM((late_depth, cols), jnp.bfloat16),
            pltpu.VMEM((rows, late_depth), jnp.bfloat16),
            pltpu.VMEM((rows, late_depth), jnp.bfloat16),
            pltpu.SemaphoreType.DMA((len(blocks.counts) + blocks.n_late + 2,)),
        ],
        compiler_params=pltpu.CompilerParams(vmem_limit_bytes=24 * MIB),
        name="project_late_attend",
    )(*tables, *blocks.operands, inputs, partner, halo, *sums)


def attend_own(tables, query, keys, values, weights, halo):
    rows, width = query.shape
    return pl.pallas_call(
        own_kernel,
        out_shape=jax.ShapeDtypeStruct((rows, width), jnp.bfloat16),
        in_specs=[SMEM_SPEC] * 3 + [VMEM_SPEC] * 5,
        out_specs=VMEM_SPEC,
        scratch_shapes=[pltpu.VMEM((rows + REACH, width), jnp.bfloat16)] * 2,
        compiler_params=pltpu.CompilerParams(vmem_limit_bytes=20 * MIB),
        name="attend_own",
    )(*tables, query, keys, values, weights, halo)


def at_end():
    place = lax.axis_index("dp") // 2
    return jnp.where((place == 0) | (place == 3), 1, 0)


def choose_kernel(between_ref, end_ref, out_ref, sems):
    for copy in start_all(sems, [((between_ref, end_ref), at_end(), out_ref)]):
        copy.wait()


def choose(between, end):
    return pl.pallas_call(
        choose_kernel,
        out_shape=jax.ShapeDtypeStruct(end.shape, end.dtype),
        in_specs=[ANY_SPEC] * 2,
        out_specs=VMEM_SPEC,
        scratch_shapes=[pltpu.SemaphoreType.DMA((1,))],
        compiler_params=pltpu.CompilerParams(vmem_limit_bytes=2 * MIB),
        name="choose",
    )(between, end)


def gather_neighbours(half):
    size = half.shape[0]

    def along(name, block, hops):
        with jax.named_scope(name):
            return lax.ppermute(
                block, "dp", [(2 * a + s, 2 * b + s) for a, b in hops for s in range(2)]
            )

    def across(name, block, places):
        with jax.named_scope(name):
            return lax.ppermute(
                block, "dp", [(2 * a + s, 2 * a + 1 - s) for a in places for s in range(2)]
            )

    line = range(4)
    outward = [(1, 0), (2, 3)]
    between = [(1, 2), (2, 1)]
    near = along("near", half, outward + [(0, 1), (3, 2)])
    mid = along("mid", half, between)
    half_across = across("half_across", half, line)
    mid_far = along("mid_far", near, between)
    near_across = across("near_across", after(near, half_across, mid), line)
    end_mid = along("end_mid", mid, outward)
    end_far = along("end_far", after(mid_far, end_mid), outward)
    second = choose(mid, end_mid)
    second_across = across("second_across", after(second, near_across), line)
    third = choose(mid_far, end_far)
    third_across = across("third_across", after(third, second_across), line)

    def find():
        index = lax.axis_index("dp")
        place, side = index // 2, index % 2
        is_end = at_end()
        second = jnp.where(is_end == 1, place ^ 2, 3 - place)
        third = jnp.where(is_end == 1, 3 - place, place ^ 2)
        spots = (place, place ^ 1, second, third)
        found = [((2 * spot + (side ^ n)) * size, is_end) for spot in spots for n in range(2)]
        return found, third * 2 * size

    blocks = [
        (half,),
        (half_across,),
        (near,),
        (near_across,),
        (second,),
        (second_across,),
        (third,),
        (third_across,),
    ]
    marks = (near_across, mid_far, end_mid), (second_across, end_far), (third_across,)
    return Blocks(blocks, 2, find), marks


def local(frames, w_qkv, utt_start, stretch_utt, left_stretches):
    inputs = frames[0]
    depth = inputs.shape[1]
    members = lax.axis_size("tm")
    core = lax.axis_index("tm") % 2

    inner = w_qkv.shape[1] // 3
    width = inner // 2
    thirds = [w_qkv[:, i * inner : (i + 1) * inner] for i in range(3)]
    half = jnp.concatenate(
        [jnp.where(core == 0, third[:, :width], third[:, width:]) for third in thirds], axis=1
    )

    tail = take_tail(after(inputs, half))
    with jax.named_scope("partner"):
        partner = lax.ppermute(inputs, "tm", [(i, i ^ 1) for i in range(members)])
    if lax.axis_size("dp") == 8:
        blocks, marks = gather_neighbours(half)
    else:
        weights = lax.all_gather(half, "dp", axis=0, tiled=True)
        late_first = depth - depth // GROUPS
        found = [(0, 0), (late_first, 0)], late_first
        parts = [(weights[:late_first],), (weights[late_first:],)]
        blocks, marks = Blocks(parts, 1, lambda: found), ((half,),) * 3

    with jax.named_scope("halo"):
        halo = lax.ppermute(
            after(tail, *marks[0]), "tm", [(i, i + 2) for i in range(1, members - 2, 2)]
        )

    tables = (utt_start, stretch_utt, left_stretches)
    sums = project_early(blocks, inputs, partner)
    with jax.named_scope("halo_first"):
        halo_first = lax.ppermute(
            after(halo, *marks[2], *sums), "tm", [(i + 1, i) for i in range(0, members, 2)]
        )
    partner_out, query, keys, values, weights = project_late_attend(
        tables, blocks, inputs, partner, halo, sums
    )
    with jax.named_scope("swap"):
        other = lax.ppermute(partner_out, "tm", [(i, i ^ 1) for i in range(members)])
    own_out = attend_own(tables, query, keys, values, weights, halo_first)
    left = jnp.where(core == 0, own_out, other)
    right = jnp.where(core == 0, other, own_out)
    return jnp.concatenate([left, right], axis=1)[None]


def solution(mesh):
    return jax.shard_map(
        local,
        mesh=mesh,
        in_specs=(P("dp", "tm", None), P("dp", None), P("dp", None), P("dp", None), P("dp", None)),
        out_specs=P("dp", "tm", None),
        check_vma=False,
    )
```

```python
import functools
import math

import jax
import jax.numpy as jnp
from jax import lax
from jax.experimental import pallas as pl
from jax.experimental.pallas import tpu as pltpu
from jax.sharding import PartitionSpec as P

HEAD_DIM = 96
STRETCH = 256
LEFT = 2
LANES = 128
GROUPS = 4
EXP_SCALE = HEAD_DIM**-0.5 * math.log2(math.e)
REACH = LEFT * STRETCH
MIB = 1024 * 1024


def dot(a, b, dims=((1,), (0,))):
    return lax.dot_general(a, b, (dims, ((), ())), preferred_element_type=jnp.float32)


def head_window(head):
    first = head * HEAD_DIM // LANES * LANES
    last = -(-(head + 1) * HEAD_DIM // LANES) * LANES
    return first, last


def start_all(sems, pairs):
    copies = []
    for i, (*source, target) in enumerate(pairs):
        if len(source) == 1:
            copy = pltpu.make_async_copy(source[0], target, sems.at[i])
            copy.start()
        else:
            for n, choice in enumerate(source[0]):
                copy = pltpu.make_async_copy(choice, target, sems.at[i])
                pl.when(source[1] == n)(copy.start)
        copies.append(copy)
    return copies


class Blocks:
    def __init__(self, blocks, n_late, find):
        self.operands = [operand for block in blocks for operand in block]
        self.counts = [len(block) for block in blocks]
        self.rows = [block[0].shape[0] for block in blocks]
        self.n_late = n_late
        self.early_operands = self.operands[: sum(self.counts[:-n_late])]
        self.find = find

    def copies(self, refs, found, members, target, first=0, columns=slice(None)):
        pairs = []
        for i in members:
            at = sum(self.counts[:i])
            choices = [ref.at[:, columns] for ref in refs[at : at + self.counts[i]]]
            row, which = found[i]
            goal = target.at[pl.ds(pl.multiple_of(row - first, self.rows[i]), self.rows[i])]
            pairs.append((choices[0], goal) if len(choices) == 1 else (choices, which, goal))
        return pairs


def early_kernel(blocks, *refs):
    n = len(blocks.early_operands)
    own_ref, partner_ref, own_sum, partner_sum, w_s, own_s, partner_s, sems = refs[n:]
    found, late_first = blocks.find()
    depth = w_s.shape[0]
    first = jnp.where(late_first == 0, own_ref.shape[1] - depth, 0)
    members = range(len(found) - blocks.n_late)
    pairs = blocks.copies(refs, found, members, w_s, first)
    columns = pl.ds(pl.multiple_of(first, LANES), depth)
    pairs.append((own_ref.at[:, columns], own_s))
    pairs.append((partner_ref.at[:, columns], partner_s))
    for copy in start_all(sems, pairs):
        copy.wait()
    width = w_s.shape[1] // 3
    for x_s, out in ((own_s, own_sum), (partner_s, partner_sum)):
        for third in range(3):
            cols = slice(third * width, (third + 1) * width)
            out[:, cols] = dot(x_s[...], w_s[:, cols])


def late_kernel(blocks, start_ref, owner_ref, left_ref, *refs):
    n = len(blocks.operands)
    own_ref, partner_ref, halo_ref, own_sum, partner_sum = refs[n : n + 5]
    out_ref, q_out, k_out, v_out, kv_out, w_s, own_s, partner_s, sems = refs[n + 5 :]
    depth = w_s.shape[0]
    width = w_s.shape[1] // 3
    rows = own_s.shape[0]
    core = lax.axis_index("tm") % 2
    found, late_first = blocks.find()
    everything = range(len(found))
    pairs = blocks.copies(refs, found, everything[-blocks.n_late :], w_s, late_first)
    columns = pl.ds(pl.multiple_of(late_first, LANES), depth)
    pairs.append((partner_ref.at[:, columns], partner_s))
    pairs.append((own_ref.at[:, columns], own_s))
    n_first = len(pairs)
    pairs += blocks.copies(refs, found, everything, kv_out, 0, slice(width, 3 * width))
    copies = start_all(sems, pairs)
    for copy in copies[:n_first]:
        copy.wait()
    for x_s, acc, place in ((partner_s, partner_sum, 1 - core), (own_s, own_sum, core)):
        row = pl.multiple_of(place * rows, STRETCH)
        for third, (dst, skip) in enumerate(((q_out, 0), (k_out, REACH), (v_out, REACH))):
            cols = slice(third * width, (third + 1) * width)
            value = (acc[:, cols] + dot(x_s[...], w_s[:, cols])).astype(jnp.bfloat16)
            dst[pl.ds(pl.multiple_of(row + skip, STRETCH), rows), :] = value
    for copy in copies[n_first:]:
        copy.wait()

    @pl.when(core == 1)
    def _():
        k_out[:REACH, :] = dot(halo_ref[...], kv_out[:, :width]).astype(jnp.bfloat16)
        v_out[:REACH, :] = dot(halo_ref[...], kv_out[:, width:]).astype(jnp.bfloat16)

    chunks = rows // STRETCH

    def block_of(i):
        return jnp.where(i < chunks, (1 - core) * chunks + i, i - chunks + LEFT)

    count = jnp.where(core == 0, 2 * chunks - LEFT, chunks)
    attend(start_ref, owner_ref, left_ref, q_out, k_out, v_out, 0, count, block_of, out_ref)


def own_kernel(
    start_ref, owner_ref, left_ref, q_ref, k_ref, v_ref, kv_ref, halo_ref, done_ref, out_ref, k_s, v_s
):
    rows, width = out_ref.shape
    core = lax.axis_index("tm") % 2
    own = pl.multiple_of(core * rows + REACH, STRETCH)
    k_s[REACH:, :] = k_ref[pl.ds(own, rows), :]
    v_s[REACH:, :] = v_ref[pl.ds(own, rows), :]

    @pl.when(core == 0)
    def _():
        k_s[:REACH, :] = dot(halo_ref[...], kv_ref[:, :width]).astype(jnp.bfloat16)
        v_s[:REACH, :] = dot(halo_ref[...], kv_ref[:, width:]).astype(jnp.bfloat16)

    @pl.when(core == 1)
    def _():
        k_s[:REACH, :] = k_ref[rows : rows + REACH, :]
        v_s[:REACH, :] = v_ref[rows : rows + REACH, :]

    chunks = rows // STRETCH
    base = core * chunks
    count = jnp.where(core == 0, LEFT, chunks)

    def block_of(i):
        return base + i

    attend(start_ref, owner_ref, left_ref, q_ref, k_s, v_s, base, count, block_of, out_ref)

    @pl.when(core == 0)
    def _():
        out_ref[REACH:, :] = done_ref[rows : 2 * rows - REACH, :]


def attend(start_ref, owner_ref, left_ref, q_s, k_s, v_s, k_base, count, block_of, out_ref):
    width = out_ref.shape[1]
    chunks = q_s.shape[0] // STRETCH
    pair = lax.axis_index("tm") // 2
    lane = lax.broadcasted_iota(jnp.int32, (1, width), 1)
    heads = width // HEAD_DIM

    def attend_block(chunk, start, lowest, q_row, k_row, span, out_ref, out_row):
        first_key = (chunk + 1) * STRETCH - span
        key_frame = first_key + lax.broadcasted_iota(jnp.int32, (1, STRETCH), 1)
        bias = jnp.where(key_frame >= lowest, 0.0, -jnp.inf).astype(jnp.float32)
        frame = chunk * STRETCH + lax.broadcasted_iota(jnp.int32, (STRETCH, 1), 0)
        live = frame >= start
        windows = [head_window(head) for head in range(heads)]
        insides = [
            ((lane >= head * HEAD_DIM) & (lane < (head + 1) * HEAD_DIM))[:, first:last]
            for head, (first, last) in enumerate(windows)
        ]
        tiles = [jnp.zeros((STRETCH, LANES), jnp.float32) for _ in range(width // LANES)]

        def score(head):
            first, last = windows[head]
            q = q_s[pl.ds(q_row, STRETCH), first:last]
            q = jnp.where(insides[head], q, jnp.zeros_like(q))
            return dot(q, k_s[pl.ds(k_row, span), first:last], ((1,), (1,)))

        def weigh(scores):
            scores = [scores[:, at : at + STRETCH] for at in range(0, span, STRETCH)]
            scores[0] = scores[0] + bias
            top = functools.reduce(jnp.maximum, scores)
            top = jnp.max(top, axis=-1, keepdims=True)
            expo = [jnp.exp2((part - top) * EXP_SCALE) for part in scores]
            total = jnp.sum(functools.reduce(jnp.add, expo), axis=-1, keepdims=True)
            share = 1.0 / total
            return jnp.concatenate([(part * share).astype(jnp.bfloat16) for part in expo], axis=1)

        def mix(head, probs):
            first, last = windows[head]
            mixed = dot(probs, v_s[pl.ds(k_row, span), first:last])
            for tile in range(first // LANES, last // LANES):
                at = tile * LANES - first
                tiles[tile] = jnp.where(
                    insides[head][:, at : at + LANES], mixed[:, at : at + LANES], tiles[tile]
                )

        scores = score(0)
        probs = None
        for head in range(heads):
            following = score(head + 1) if head + 1 < heads else None
            weighed = weigh(scores)
            if probs is not None:
                mix(head - 1, probs)
            scores, probs = following, weighed
        mix(heads - 1, probs)
        for tile, value in enumerate(tiles):
            value = jnp.where(live, value, 0.0).astype(jnp.bfloat16)
            out_ref[pl.ds(out_row, STRETCH), tile * LANES : (tile + 1) * LANES] = value

    @pl.loop(0, count)
    def _(i):
        block = block_of(i)
        out_row = pl.multiple_of(i * STRETCH, STRETCH)
        q_row = pl.multiple_of(block * STRETCH, STRETCH)
        chunk = pair * chunks + block
        left = left_ref[0, chunk]
        start = start_ref[0, owner_ref[0, chunk]]
        lowest = jnp.maximum((chunk - left) * STRETCH, start)
        for back in range(LEFT + 1):

            @pl.when(left == back)
            def _():
                k_row = pl.multiple_of((block - k_base + LEFT - back) * STRETCH, STRETCH)
                span = (back + 1) * STRETCH
                attend_block(chunk, start, lowest, q_row, k_row, span, out_ref, out_row)


def after(value, *others):
    return lax.optimization_barrier((value, *others))[0]


SMEM_SPEC = pl.BlockSpec(memory_space=pltpu.SMEM)
VMEM_SPEC = pl.BlockSpec(memory_space=pltpu.VMEM)
ANY_SPEC = pl.BlockSpec(memory_space=pl.ANY)


def half_kernel(w_ref, out_ref, sems):
    width = out_ref.shape[1] // 3
    core = lax.axis_index("tm") % 2
    pairs = []
    for third in range(3):
        at = pl.multiple_of((2 * third + core) * width, LANES)
        pairs.append((w_ref.at[:, pl.ds(at, width)], out_ref.at[:, third * width : (third + 1) * width]))
    for copy in start_all(sems, pairs):
        copy.wait()


def take_half(w):
    return pl.pallas_call(
        half_kernel,
        out_shape=jax.ShapeDtypeStruct((w.shape[0], w.shape[1] // 2), w.dtype),
        in_specs=[pl.BlockSpec(memory_space=pltpu.HBM)],
        out_specs=VMEM_SPEC,
        scratch_shapes=[pltpu.SemaphoreType.DMA((3,))],
        compiler_params=pltpu.CompilerParams(vmem_limit_bytes=4 * MIB),
        name="take_half",
    )(w)


def join_kernel(own_ref, other_ref, out_ref, sems):
    rows, width = own_ref.shape
    core = lax.axis_index("tm") % 2
    own_at = pl.multiple_of(core * width, LANES)
    other_at = pl.multiple_of((1 - core) * width, LANES)
    pairs = [
        (own_ref, out_ref.at[:, pl.ds(own_at, width)]),
        (other_ref.at[:rows, :], out_ref.at[:, pl.ds(other_at, width)]),
    ]
    for copy in start_all(sems, pairs):
        copy.wait()


def join(own, other):
    rows, width = own.shape
    return pl.pallas_call(
        join_kernel,
        out_shape=jax.ShapeDtypeStruct((rows, 2 * width), own.dtype),
        in_specs=[ANY_SPEC] * 2,
        out_specs=ANY_SPEC,
        scratch_shapes=[pltpu.SemaphoreType.DMA((2,))],
        compiler_params=pltpu.CompilerParams(vmem_limit_bytes=4 * MIB),
        name="join",
    )(own, other)


def project_early(blocks, inputs, partner):
    rows, depth = inputs.shape
    depth -= depth // GROUPS
    cols = blocks.operands[0].shape[1]
    n_copies = len(blocks.counts) - blocks.n_late + 2
    return pl.pallas_call(
        functools.partial(early_kernel, blocks),
        out_shape=[jax.ShapeDtypeStruct((rows, cols), jnp.float32)] * 2,
        in_specs=[ANY_SPEC] * (len(blocks.early_operands) + 2),
        out_specs=[VMEM_SPEC] * 2,
        scratch_shapes=[
            pltpu.VMEM((depth, cols), jnp.bfloat16),
            pltpu.VMEM((rows, depth), jnp.bfloat16),
            pltpu.VMEM((rows, depth), jnp.bfloat16),
            pltpu.SemaphoreType.DMA((n_copies,)),
        ],
        compiler_params=pltpu.CompilerParams(vmem_limit_bytes=24 * MIB),
        cost_estimate=pl.CostEstimate(flops=0, bytes_accessed=0, transcendentals=0),
        name="project_early",
    )(*blocks.early_operands, inputs, partner)


def tail_kernel(x_ref, out_ref, sems):
    rows = out_ref.shape[0]
    for copy in start_all(sems, [(x_ref.at[x_ref.shape[0] - rows :, :], out_ref)]):
        copy.wait()


def take_tail(x):
    return pl.pallas_call(
        tail_kernel,
        out_shape=jax.ShapeDtypeStruct((REACH, x.shape[1]), x.dtype),
        in_specs=[ANY_SPEC],
        out_specs=VMEM_SPEC,
        scratch_shapes=[pltpu.SemaphoreType.DMA((1,))],
        compiler_params=pltpu.CompilerParams(vmem_limit_bytes=4 * MIB),
        name="take_tail",
    )(x)


def project_late_attend(tables, blocks, inputs, partner, halo, sums):
    rows, depth = inputs.shape
    late_depth = depth // GROUPS
    cols = blocks.operands[0].shape[1]
    width = cols // 3
    keys = jax.ShapeDtypeStruct((2 * rows + REACH, width), jnp.bfloat16)
    return pl.pallas_call(
        functools.partial(late_kernel, blocks),
        out_shape=[
            jax.ShapeDtypeStruct((2 * rows - REACH, width), jnp.bfloat16),
            jax.ShapeDtypeStruct((2 * rows, width), jnp.bfloat16),
            keys,
            keys,
            jax.ShapeDtypeStruct((depth, 2 * width), jnp.bfloat16),
        ],
        in_specs=[SMEM_SPEC] * 3 + [ANY_SPEC] * (len(blocks.operands) + 2) + [VMEM_SPEC] * 3,
        out_specs=[VMEM_SPEC] * 5,
        scratch_shapes=[
            pltpu.VMEM((late_depth, cols), jnp.bfloat16),
            pltpu.VMEM((rows, late_depth), jnp.bfloat16),
            pltpu.VMEM((rows, late_depth), jnp.bfloat16),
            pltpu.SemaphoreType.DMA((len(blocks.counts) + blocks.n_late + 2,)),
        ],
        compiler_params=pltpu.CompilerParams(vmem_limit_bytes=24 * MIB),
        name="project_late_attend",
    )(*tables, *blocks.operands, inputs, partner, halo, *sums)


def attend_own(tables, queries, keys, values, weights, halo, done):
    rows, width = queries.shape
    rows //= 2
    return pl.pallas_call(
        own_kernel,
        out_shape=jax.ShapeDtypeStruct((rows, width), jnp.bfloat16),
        in_specs=[SMEM_SPEC] * 3 + [VMEM_SPEC] * 6,
        out_specs=VMEM_SPEC,
        scratch_shapes=[pltpu.VMEM((rows + REACH, width), jnp.bfloat16)] * 2,
        compiler_params=pltpu.CompilerParams(vmem_limit_bytes=20 * MIB),
        name="attend_own",
    )(*tables, queries, keys, values, weights, halo, done)


def at_end():
    place = lax.axis_index("dp") // 2
    return jnp.where((place == 0) | (place == 3), 1, 0)


def choose_kernel(between_ref, end_ref, out_ref, sems):
    for copy in start_all(sems, [((between_ref, end_ref), at_end(), out_ref)]):
        copy.wait()


def choose(between, end):
    return pl.pallas_call(
        choose_kernel,
        out_shape=jax.ShapeDtypeStruct(end.shape, end.dtype),
        in_specs=[ANY_SPEC] * 2,
        out_specs=VMEM_SPEC,
        scratch_shapes=[pltpu.SemaphoreType.DMA((1,))],
        compiler_params=pltpu.CompilerParams(vmem_limit_bytes=2 * MIB),
        name="choose",
    )(between, end)


def gather_neighbours(half):
    size = half.shape[0]

    def along(name, block, hops):
        with jax.named_scope(name):
            return lax.ppermute(
                block, "dp", [(2 * a + s, 2 * b + s) for a, b in hops for s in range(2)]
            )

    def across(name, block, places):
        with jax.named_scope(name):
            return lax.ppermute(
                block, "dp", [(2 * a + s, 2 * a + 1 - s) for a in places for s in range(2)]
            )

    line = range(4)
    outward = [(1, 0), (2, 3)]
    between = [(1, 2), (2, 1)]
    near = along("near", half, outward + [(0, 1), (3, 2)])
    mid = along("mid", half, between)
    half_across = across("half_across", half, line)
    mid_far = along("mid_far", near, between)
    near_across = across("near_across", after(near, half_across, mid), line)
    end_mid = along("end_mid", mid, outward)
    end_far = along("end_far", after(mid_far, end_mid), outward)
    second = choose(mid, end_mid)
    second_across = across("second_across", after(second, near_across), line)
    third = choose(mid_far, end_far)
    third_across = across("third_across", after(third, second_across), line)

    def find():
        index = lax.axis_index("dp")
        place, side = index // 2, index % 2
        is_end = at_end()
        second = jnp.where(is_end == 1, place ^ 2, 3 - place)
        third = jnp.where(is_end == 1, 3 - place, place ^ 2)
        spots = (place, place ^ 1, second, third)
        found = [((2 * spot + (side ^ n)) * size, is_end) for spot in spots for n in range(2)]
        return found, third * 2 * size

    blocks = [
        (half,),
        (half_across,),
        (near,),
        (near_across,),
        (second,),
        (second_across,),
        (third,),
        (third_across,),
    ]
    marks = (near_across, mid_far, end_mid), (second_across, end_far), (third_across,)
    return Blocks(blocks, 2, find), marks


def local(frames, w_qkv, utt_start, stretch_utt, left_stretches):
    inputs = frames[0]
    depth = inputs.shape[1]
    members = lax.axis_size("tm")

    half = take_half(w_qkv)

    tail = take_tail(after(inputs, half))
    with jax.named_scope("partner"):
        partner = lax.ppermute(inputs, "tm", [(i, i ^ 1) for i in range(members)])
    if lax.axis_size("dp") == 8:
        blocks, marks = gather_neighbours(half)
    else:
        weights = lax.all_gather(half, "dp", axis=0, tiled=True)
        late_first = depth - depth // GROUPS
        found = [(0, 0), (late_first, 0)], late_first
        parts = [(weights[:late_first],), (weights[late_first:],)]
        blocks, marks = Blocks(parts, 1, lambda: found), ((half,),) * 3

    with jax.named_scope("halo"):
        halo = lax.ppermute(
            after(tail, *marks[0]), "tm", [(i, i + 2) for i in range(1, members - 2, 2)]
        )

    tables = (utt_start, stretch_utt, left_stretches)
    sums = project_early(blocks, inputs, partner)
    with jax.named_scope("halo_first"):
        halo_first = lax.ppermute(
            after(halo, *marks[2], *sums), "tm", [(i + 1, i) for i in range(0, members, 2)]
        )
    attended, queries, keys, values, weights = project_late_attend(
        tables, blocks, inputs, partner, halo, sums
    )
    with jax.named_scope("swap"):
        other = lax.ppermute(attended, "tm", [(i, i ^ 1) for i in range(members)])
    own_out = attend_own(tables, queries, keys, values, weights, halo_first, attended)
    return join(own_out, other)[None]


def solution(mesh):
    return jax.shard_map(
        local,
        mesh=mesh,
        in_specs=(P("dp", "tm", None), P("dp", None), P("dp", None), P("dp", None), P("dp", None)),
        out_specs=P("dp", "tm", None),
        check_vma=False,
    )
```

```python
import functools
import math

import jax
import jax.numpy as jnp
from jax import lax
from jax.experimental import pallas as pl
from jax.experimental.pallas import tpu as pltpu
from jax.sharding import PartitionSpec as P

HEAD_DIM = 96
STRETCH = 256
LEFT = 2
LANES = 128
GROUPS = 4
EXP_SCALE = HEAD_DIM**-0.5 * math.log2(math.e)
REACH = LEFT * STRETCH
MIB = 1024 * 1024


def dot(a, b, dims=((1,), (0,))):
    return lax.dot_general(a, b, (dims, ((), ())), preferred_element_type=jnp.float32)


def head_window(head):
    first = head * HEAD_DIM // LANES * LANES
    last = -(-(head + 1) * HEAD_DIM // LANES) * LANES
    return first, last


def start_all(sems, pairs):
    copies = []
    for i, (*source, target) in enumerate(pairs):
        if len(source) == 1:
            copy = pltpu.make_async_copy(source[0], target, sems.at[i])
            copy.start()
        else:
            for n, choice in enumerate(source[0]):
                copy = pltpu.make_async_copy(choice, target, sems.at[i])
                pl.when(source[1] == n)(copy.start)
        copies.append(copy)
    return copies


class Blocks:
    def __init__(self, blocks, n_late, find):
        self.operands = [operand for block in blocks for operand in block]
        self.counts = [len(block) for block in blocks]
        self.rows = [block[0].shape[0] for block in blocks]
        self.n_late = n_late
        self.early_operands = self.operands[: sum(self.counts[:-n_late])]
        self.find = find

    def copies(self, refs, found, members, target, first=0, columns=slice(None)):
        pairs = []
        for i in members:
            at = sum(self.counts[:i])
            choices = [ref.at[:, columns] for ref in refs[at : at + self.counts[i]]]
            row, which = found[i]
            goal = target.at[pl.ds(pl.multiple_of(row - first, self.rows[i]), self.rows[i])]
            pairs.append((choices[0], goal) if len(choices) == 1 else (choices, which, goal))
        return pairs


def early_kernel(blocks, *refs):
    n = len(blocks.early_operands)
    own_ref, partner_ref, own_sum, partner_sum, w_s, own_s, partner_s, sems = refs[n:]
    found, late_first = blocks.find()
    depth = w_s.shape[0]
    first = jnp.where(late_first == 0, own_ref.shape[1] - depth, 0)
    members = range(len(found) - blocks.n_late)
    pairs = blocks.copies(refs, found, members, w_s, first)
    columns = pl.ds(pl.multiple_of(first, LANES), depth)
    pairs.append((own_ref.at[:, columns], own_s))
    pairs.append((partner_ref.at[:, columns], partner_s))
    for copy in start_all(sems, pairs):
        copy.wait()
    width = w_s.shape[1] // 3
    for x_s, out in ((own_s, own_sum), (partner_s, partner_sum)):
        for third in range(3):
            cols = slice(third * width, (third + 1) * width)
            out[:, cols] = dot(x_s[...], w_s[:, cols])


def project_halo(halo_refs, kv_ref, k_ref, v_ref):
    width = k_ref.shape[1]
    for i, frames_ref in enumerate(halo_refs):
        at = slice(i * STRETCH, (i + 1) * STRETCH)
        k_ref[at, :] = dot(frames_ref[...], kv_ref[:, :width]).astype(jnp.bfloat16)
        v_ref[at, :] = dot(frames_ref[...], kv_ref[:, width:]).astype(jnp.bfloat16)


def late_kernel(blocks, start_ref, owner_ref, left_ref, *refs):
    n = len(blocks.operands)
    own_ref, partner_ref = refs[n : n + 2]
    halo_refs = refs[n + 2 : n + 2 + LEFT]
    own_sum, partner_sum, out_ref, q_out, k_out, v_out, kv_out, *scratch = refs[n + 2 + LEFT :]
    w_s, own_s, partner_s, sems = scratch
    depth = w_s.shape[0]
    width = w_s.shape[1] // 3
    rows = own_s.shape[0]
    core = lax.axis_index("tm") % 2
    found, late_first = blocks.find()
    everything = range(len(found))
    pairs = blocks.copies(refs, found, everything[-blocks.n_late :], w_s, late_first)
    columns = pl.ds(pl.multiple_of(late_first, LANES), depth)
    pairs.append((partner_ref.at[:, columns], partner_s))
    pairs.append((own_ref.at[:, columns], own_s))
    n_first = len(pairs)
    pairs += blocks.copies(refs, found, everything, kv_out, 0, slice(width, 3 * width))
    copies = start_all(sems, pairs)
    for copy in copies[:n_first]:
        copy.wait()
    for x_s, acc, place in ((partner_s, partner_sum, 1 - core), (own_s, own_sum, core)):
        row = pl.multiple_of(place * rows, STRETCH)
        for third, (dst, skip) in enumerate(((q_out, 0), (k_out, REACH), (v_out, REACH))):
            cols = slice(third * width, (third + 1) * width)
            value = (acc[:, cols] + dot(x_s[...], w_s[:, cols])).astype(jnp.bfloat16)
            dst[pl.ds(pl.multiple_of(row + skip, STRETCH), rows), :] = value
    for copy in copies[n_first:]:
        copy.wait()

    @pl.when(core == 1)
    def _():
        project_halo(halo_refs, kv_out, k_out, v_out)

    chunks = rows // STRETCH

    def block_of(i):
        return jnp.where(i < chunks, (1 - core) * chunks + i, i - chunks + LEFT)

    count = jnp.where(core == 0, 2 * chunks - LEFT, chunks)
    attend(start_ref, owner_ref, left_ref, q_out, k_out, v_out, 0, count, block_of, out_ref)


def own_kernel(start_ref, owner_ref, left_ref, q_ref, k_ref, v_ref, kv_ref, *refs):
    *halo_refs, done_ref, out_ref, k_s, v_s = refs
    rows, width = out_ref.shape
    core = lax.axis_index("tm") % 2
    own = pl.multiple_of(core * rows + REACH, STRETCH)
    k_s[REACH:, :] = k_ref[pl.ds(own, rows), :]
    v_s[REACH:, :] = v_ref[pl.ds(own, rows), :]

    @pl.when(core == 0)
    def _():
        project_halo(halo_refs, kv_ref, k_s, v_s)

    @pl.when(core == 1)
    def _():
        k_s[:REACH, :] = k_ref[rows : rows + REACH, :]
        v_s[:REACH, :] = v_ref[rows : rows + REACH, :]

    chunks = rows // STRETCH
    base = core * chunks
    count = jnp.where(core == 0, LEFT, chunks)

    def block_of(i):
        return base + i

    attend(start_ref, owner_ref, left_ref, q_ref, k_s, v_s, base, count, block_of, out_ref)

    @pl.when(core == 0)
    def _():
        out_ref[REACH:, :] = done_ref[rows : 2 * rows - REACH, :]


def attend(start_ref, owner_ref, left_ref, q_s, k_s, v_s, k_base, count, block_of, out_ref):
    width = out_ref.shape[1]
    chunks = q_s.shape[0] // STRETCH
    pair = lax.axis_index("tm") // 2
    lane = lax.broadcasted_iota(jnp.int32, (1, width), 1)
    heads = width // HEAD_DIM

    def attend_block(chunk, start, lowest, q_row, k_row, span, out_ref, out_row):
        first_key = (chunk + 1) * STRETCH - span
        key_frame = first_key + lax.broadcasted_iota(jnp.int32, (1, STRETCH), 1)
        bias = jnp.where(key_frame >= lowest, 0.0, -jnp.inf).astype(jnp.float32)
        frame = chunk * STRETCH + lax.broadcasted_iota(jnp.int32, (STRETCH, 1), 0)
        live = frame >= start
        windows = [head_window(head) for head in range(heads)]
        insides = [
            ((lane >= head * HEAD_DIM) & (lane < (head + 1) * HEAD_DIM))[:, first:last]
            for head, (first, last) in enumerate(windows)
        ]
        tiles = [jnp.zeros((STRETCH, LANES), jnp.float32) for _ in range(width // LANES)]

        def score(head):
            first, last = windows[head]
            q = q_s[pl.ds(q_row, STRETCH), first:last]
            q = jnp.where(insides[head], q, jnp.zeros_like(q))
            return dot(q, k_s[pl.ds(k_row, span), first:last], ((1,), (1,)))

        def weigh(scores):
            scores = [scores[:, at : at + STRETCH] for at in range(0, span, STRETCH)]
            scores[0] = scores[0] + bias
            top = functools.reduce(jnp.maximum, scores)
            top = jnp.max(top, axis=-1, keepdims=True)
            expo = [jnp.exp2((part - top) * EXP_SCALE) for part in scores]
            total = jnp.sum(functools.reduce(jnp.add, expo), axis=-1, keepdims=True)
            share = 1.0 / total
            return jnp.concatenate([(part * share).astype(jnp.bfloat16) for part in expo], axis=1)

        def mix(head, probs):
            first, last = windows[head]
            mixed = dot(probs, v_s[pl.ds(k_row, span), first:last])
            for tile in range(first // LANES, last // LANES):
                at = tile * LANES - first
                tiles[tile] = jnp.where(
                    insides[head][:, at : at + LANES], mixed[:, at : at + LANES], tiles[tile]
                )

        scores = score(0)
        probs = None
        for head in range(heads):
            following = score(head + 1) if head + 1 < heads else None
            weighed = weigh(scores)
            if probs is not None:
                mix(head - 1, probs)
            scores, probs = following, weighed
        mix(heads - 1, probs)
        for tile, value in enumerate(tiles):
            value = jnp.where(live, value, 0.0).astype(jnp.bfloat16)
            out_ref[pl.ds(out_row, STRETCH), tile * LANES : (tile + 1) * LANES] = value

    @pl.loop(0, count)
    def _(i):
        block = block_of(i)
        out_row = pl.multiple_of(i * STRETCH, STRETCH)
        q_row = pl.multiple_of(block * STRETCH, STRETCH)
        chunk = pair * chunks + block
        left = left_ref[0, chunk]
        start = start_ref[0, owner_ref[0, chunk]]
        lowest = jnp.maximum((chunk - left) * STRETCH, start)
        for back in range(LEFT + 1):

            @pl.when(left == back)
            def _():
                k_row = pl.multiple_of((block - k_base + LEFT - back) * STRETCH, STRETCH)
                span = (back + 1) * STRETCH
                attend_block(chunk, start, lowest, q_row, k_row, span, out_ref, out_row)


def after(value, *others):
    return lax.optimization_barrier((value, *others))[0]


SMEM_SPEC = pl.BlockSpec(memory_space=pltpu.SMEM)
VMEM_SPEC = pl.BlockSpec(memory_space=pltpu.VMEM)
ANY_SPEC = pl.BlockSpec(memory_space=pl.ANY)


def half_kernel(w_ref, out_ref, sems):
    width = out_ref.shape[1] // 3
    core = lax.axis_index("tm") % 2
    pairs = []
    for third in range(3):
        at = pl.multiple_of((2 * third + core) * width, LANES)
        pairs.append((w_ref.at[:, pl.ds(at, width)], out_ref.at[:, third * width : (third + 1) * width]))
    for copy in start_all(sems, pairs):
        copy.wait()


def take_half(w):
    return pl.pallas_call(
        half_kernel,
        out_shape=jax.ShapeDtypeStruct((w.shape[0], w.shape[1] // 2), w.dtype),
        in_specs=[pl.BlockSpec(memory_space=pltpu.HBM)],
        out_specs=VMEM_SPEC,
        scratch_shapes=[pltpu.SemaphoreType.DMA((3,))],
        compiler_params=pltpu.CompilerParams(vmem_limit_bytes=4 * MIB),
        name="take_half",
    )(w)


def join_kernel(own_ref, other_ref, out_ref, sems):
    rows, width = own_ref.shape
    core = lax.axis_index("tm") % 2
    own_at = pl.multiple_of(core * width, LANES)
    other_at = pl.multiple_of((1 - core) * width, LANES)
    pairs = [
        (own_ref, out_ref.at[:, pl.ds(own_at, width)]),
        (other_ref.at[:rows, :], out_ref.at[:, pl.ds(other_at, width)]),
    ]
    for copy in start_all(sems, pairs):
        copy.wait()


def join(own, other):
    rows, width = own.shape
    return pl.pallas_call(
        join_kernel,
        out_shape=jax.ShapeDtypeStruct((rows, 2 * width), own.dtype),
        in_specs=[ANY_SPEC] * 2,
        out_specs=ANY_SPEC,
        scratch_shapes=[pltpu.SemaphoreType.DMA((2,))],
        compiler_params=pltpu.CompilerParams(vmem_limit_bytes=4 * MIB),
        name="join",
    )(own, other)


def project_early(blocks, inputs, partner):
    rows, depth = inputs.shape
    depth -= depth // GROUPS
    cols = blocks.operands[0].shape[1]
    n_copies = len(blocks.counts) - blocks.n_late + 2
    return pl.pallas_call(
        functools.partial(early_kernel, blocks),
        out_shape=[jax.ShapeDtypeStruct((rows, cols), jnp.float32)] * 2,
        in_specs=[ANY_SPEC] * (len(blocks.early_operands) + 2),
        out_specs=[VMEM_SPEC] * 2,
        scratch_shapes=[
            pltpu.VMEM((depth, cols), jnp.bfloat16),
            pltpu.VMEM((rows, depth), jnp.bfloat16),
            pltpu.VMEM((rows, depth), jnp.bfloat16),
            pltpu.SemaphoreType.DMA((n_copies,)),
        ],
        compiler_params=pltpu.CompilerParams(vmem_limit_bytes=24 * MIB),
        cost_estimate=pl.CostEstimate(flops=0, bytes_accessed=0, transcendentals=0),
        name="project_early",
    )(*blocks.early_operands, inputs, partner)


def tail_kernel(x_ref, *refs):
    *outs, sems = refs
    first = x_ref.shape[0] - len(outs) * STRETCH
    pairs = [
        (x_ref.at[first + i * STRETCH : first + (i + 1) * STRETCH, :], out)
        for i, out in enumerate(outs)
    ]
    for copy in start_all(sems, pairs):
        copy.wait()


def take_tail(x):
    return pl.pallas_call(
        tail_kernel,
        out_shape=[jax.ShapeDtypeStruct((STRETCH, x.shape[1]), x.dtype)] * LEFT,
        in_specs=[ANY_SPEC],
        out_specs=[VMEM_SPEC] * LEFT,
        scratch_shapes=[pltpu.SemaphoreType.DMA((LEFT,))],
        compiler_params=pltpu.CompilerParams(vmem_limit_bytes=4 * MIB),
        name="take_tail",
    )(x)


def project_late_attend(tables, blocks, inputs, partner, halo, sums):
    rows, depth = inputs.shape
    late_depth = depth // GROUPS
    cols = blocks.operands[0].shape[1]
    width = cols // 3
    keys = jax.ShapeDtypeStruct((2 * rows + REACH, width), jnp.bfloat16)
    return pl.pallas_call(
        functools.partial(late_kernel, blocks),
        out_shape=[
            jax.ShapeDtypeStruct((2 * rows - REACH, width), jnp.bfloat16),
            jax.ShapeDtypeStruct((2 * rows, width), jnp.bfloat16),
            keys,
            keys,
            jax.ShapeDtypeStruct((depth, 2 * width), jnp.bfloat16),
        ],
        in_specs=[SMEM_SPEC] * 3 + [ANY_SPEC] * (len(blocks.operands) + 2) + [VMEM_SPEC] * (LEFT + 2),
        out_specs=[VMEM_SPEC] * 5,
        scratch_shapes=[
            pltpu.VMEM((late_depth, cols), jnp.bfloat16),
            pltpu.VMEM((rows, late_depth), jnp.bfloat16),
            pltpu.VMEM((rows, late_depth), jnp.bfloat16),
            pltpu.SemaphoreType.DMA((len(blocks.counts) + blocks.n_late + 2,)),
        ],
        compiler_params=pltpu.CompilerParams(vmem_limit_bytes=24 * MIB),
        name="project_late_attend",
    )(*tables, *blocks.operands, inputs, partner, *halo, *sums)


def attend_own(tables, queries, keys, values, weights, halo, done):
    rows, width = queries.shape
    rows //= 2
    return pl.pallas_call(
        own_kernel,
        out_shape=jax.ShapeDtypeStruct((rows, width), jnp.bfloat16),
        in_specs=[SMEM_SPEC] * 3 + [VMEM_SPEC] * (LEFT + 5),
        out_specs=VMEM_SPEC,
        scratch_shapes=[pltpu.VMEM((rows + REACH, width), jnp.bfloat16)] * 2,
        compiler_params=pltpu.CompilerParams(vmem_limit_bytes=20 * MIB),
        name="attend_own",
    )(*tables, queries, keys, values, weights, *halo, done)


def at_end():
    place = lax.axis_index("dp") // 2
    return jnp.where((place == 0) | (place == 3), 1, 0)


def choose_kernel(between_ref, end_ref, out_ref, sems):
    for copy in start_all(sems, [((between_ref, end_ref), at_end(), out_ref)]):
        copy.wait()


def choose(between, end):
    return pl.pallas_call(
        choose_kernel,
        out_shape=jax.ShapeDtypeStruct(end.shape, end.dtype),
        in_specs=[ANY_SPEC] * 2,
        out_specs=VMEM_SPEC,
        scratch_shapes=[pltpu.SemaphoreType.DMA((1,))],
        compiler_params=pltpu.CompilerParams(vmem_limit_bytes=2 * MIB),
        name="choose",
    )(between, end)


def gather_neighbours(half):
    size = half.shape[0]

    def along(name, block, hops):
        with jax.named_scope(name):
            return lax.ppermute(
                block, "dp", [(2 * a + s, 2 * b + s) for a, b in hops for s in range(2)]
            )

    def across(name, block, places):
        with jax.named_scope(name):
            return lax.ppermute(
                block, "dp", [(2 * a + s, 2 * a + 1 - s) for a in places for s in range(2)]
            )

    line = range(4)
    outward = [(1, 0), (2, 3)]
    between = [(1, 2), (2, 1)]
    near = along("near", half, outward + [(0, 1), (3, 2)])
    mid = along("mid", half, between)
    half_across = across("half_across", half, line)
    mid_far = along("mid_far", near, between)
    near_across = across("near_across", after(near, half_across, mid), line)
    end_mid = along("end_mid", mid, outward)
    end_far = along("end_far", after(mid_far, end_mid), outward)
    second = choose(mid, end_mid)
    second_across = across("second_across", after(second, near_across), line)
    third = choose(mid_far, end_far)
    third_across = across("third_across", after(third, second_across), line)

    def find():
        index = lax.axis_index("dp")
        place, side = index // 2, index % 2
        is_end = at_end()
        second = jnp.where(is_end == 1, place ^ 2, 3 - place)
        third = jnp.where(is_end == 1, 3 - place, place ^ 2)
        spots = (place, place ^ 1, second, third)
        found = [((2 * spot + (side ^ n)) * size, is_end) for spot in spots for n in range(2)]
        return found, third * 2 * size

    blocks = [
        (half,),
        (half_across,),
        (near,),
        (near_across,),
        (second,),
        (second_across,),
        (third,),
        (third_across,),
    ]
    marks = (near_across, mid_far, end_mid), (second_across, end_far), (third_across,)
    return Blocks(blocks, 2, find), marks


def local(frames, w_qkv, utt_start, stretch_utt, left_stretches):
    inputs = frames[0]
    depth = inputs.shape[1]
    members = lax.axis_size("tm")

    half = take_half(w_qkv)

    tail = take_tail(after(inputs, half))
    with jax.named_scope("partner"):
        partner = lax.ppermute(inputs, "tm", [(i, i ^ 1) for i in range(members)])
    if lax.axis_size("dp") == 8:
        blocks, marks = gather_neighbours(half)
    else:
        weights = lax.all_gather(half, "dp", axis=0, tiled=True)
        late_first = depth - depth // GROUPS
        found = [(0, 0), (late_first, 0)], late_first
        parts = [(weights[:late_first],), (weights[late_first:],)]
        blocks, marks = Blocks(parts, 1, lambda: found), ((half,),) * 3

    with jax.named_scope("halo"):
        onward = [(i, i + 2) for i in range(1, members - 2, 2)]
        halo = [lax.ppermute(after(x, *mark), "tm", onward) for x, mark in zip(tail, marks)]

    tables = (utt_start, stretch_utt, left_stretches)
    sums = project_early(blocks, inputs, partner)
    with jax.named_scope("halo_first"):
        back = [(i + 1, i) for i in range(0, members, 2)]
        halo_first = [lax.ppermute(after(halo[0], *sums), "tm", back), lax.ppermute(after(halo[1], *marks[2], *sums), "tm", back)]
    attended, queries, keys, values, weights = project_late_attend(
        tables, blocks, inputs, partner, halo, sums
    )
    with jax.named_scope("swap"):
        other = lax.ppermute(attended, "tm", [(i, i ^ 1) for i in range(members)])
    own_out = attend_own(tables, queries, keys, values, weights, halo_first, attended)
    return join(own_out, other)[None]


def solution(mesh):
    return jax.shard_map(
        local,
        mesh=mesh,
        in_specs=(P("dp", "tm", None), P("dp", None), P("dp", None), P("dp", None), P("dp", None)),
        out_specs=P("dp", "tm", None),
        check_vma=False,
    )
```

```python
import functools
import math

import jax
import jax.numpy as jnp
from jax import lax
from jax.experimental import pallas as pl
from jax.experimental.pallas import tpu as pltpu
from jax.sharding import PartitionSpec as P

HEAD_DIM = 96
STRETCH = 256
LEFT = 2
LANES = 128
GROUPS = 4
EXP_SCALE = HEAD_DIM**-0.5 * math.log2(math.e)
REACH = LEFT * STRETCH
MIB = 1024 * 1024


def dot(a, b, dims=((1,), (0,))):
    return lax.dot_general(a, b, (dims, ((), ())), preferred_element_type=jnp.float32)


def head_window(head):
    first = head * HEAD_DIM // LANES * LANES
    last = -(-(head + 1) * HEAD_DIM // LANES) * LANES
    return first, last


def start_all(sems, pairs):
    copies = []
    for i, (*source, target) in enumerate(pairs):
        if len(source) == 1:
            copy = pltpu.make_async_copy(source[0], target, sems.at[i])
            copy.start()
        else:
            for n, choice in enumerate(source[0]):
                copy = pltpu.make_async_copy(choice, target, sems.at[i])
                pl.when(source[1] == n)(copy.start)
        copies.append(copy)
    return copies


class Blocks:
    def __init__(self, blocks, n_late, find):
        self.operands = [operand for block in blocks for operand in block]
        self.counts = [len(block) for block in blocks]
        self.rows = [block[0].shape[0] for block in blocks]
        self.n_late = n_late
        self.early_operands = self.operands[: sum(self.counts[:-n_late])]
        self.find = find

    def copies(self, refs, found, members, target, first=0, columns=slice(None)):
        pairs = []
        for i in members:
            at = sum(self.counts[:i])
            choices = [ref.at[:, columns] for ref in refs[at : at + self.counts[i]]]
            row, which = found[i]
            goal = target.at[pl.ds(pl.multiple_of(row - first, self.rows[i]), self.rows[i])]
            pairs.append((choices[0], goal) if len(choices) == 1 else (choices, which, goal))
        return pairs


def early_kernel(blocks, *refs):
    n = len(blocks.early_operands)
    own_ref, partner_ref, own_sum, partner_sum, w_s, own_s, partner_s, sems = refs[n:]
    found, late_first = blocks.find()
    depth = w_s.shape[0]
    first = jnp.where(late_first == 0, own_ref.shape[1] - depth, 0)
    members = range(len(found) - blocks.n_late)
    pairs = blocks.copies(refs, found, members, w_s, first)
    columns = pl.ds(pl.multiple_of(first, LANES), depth)
    pairs.append((own_ref.at[:, columns], own_s))
    pairs.append((partner_ref.at[:, columns], partner_s))
    for copy in start_all(sems, pairs):
        copy.wait()
    width = w_s.shape[1] // 3
    for x_s, out in ((own_s, own_sum), (partner_s, partner_sum)):
        for third in range(3):
            cols = slice(third * width, (third + 1) * width)
            out[:, cols] = dot(x_s[...], w_s[:, cols])


def project_halo(halo_refs, kv_ref, k_ref, v_ref):
    width = k_ref.shape[1]
    for i, frames_ref in enumerate(halo_refs):
        at = slice(i * STRETCH, (i + 1) * STRETCH)
        k_ref[at, :] = dot(frames_ref[...], kv_ref[:, :width]).astype(jnp.bfloat16)
        v_ref[at, :] = dot(frames_ref[...], kv_ref[:, width:]).astype(jnp.bfloat16)


def late_kernel(blocks, start_ref, owner_ref, left_ref, *refs):
    n = len(blocks.operands)
    own_ref, partner_ref = refs[n : n + 2]
    halo_refs = refs[n + 2 : n + 2 + LEFT]
    own_sum, partner_sum, out_ref, q_out, k_out, v_out, kv_out, *scratch = refs[n + 2 + LEFT :]
    w_s, own_s, partner_s, sems = scratch
    depth = w_s.shape[0]
    width = w_s.shape[1] // 3
    rows = own_s.shape[0]
    core = lax.axis_index("tm") % 2
    found, late_first = blocks.find()
    everything = range(len(found))
    pairs = blocks.copies(refs, found, everything[-blocks.n_late :], w_s, late_first)
    columns = pl.ds(pl.multiple_of(late_first, LANES), depth)
    pairs.append((partner_ref.at[:, columns], partner_s))
    pairs.append((own_ref.at[:, columns], own_s))
    n_first = len(pairs)
    pairs += blocks.copies(refs, found, everything, kv_out, 0, slice(width, 3 * width))
    copies = start_all(sems, pairs)
    for copy in copies[:n_first]:
        copy.wait()
    for x_s, acc, place in ((partner_s, partner_sum, 1 - core), (own_s, own_sum, core)):
        row = pl.multiple_of(place * rows, STRETCH)
        for third, (dst, skip) in enumerate(((q_out, 0), (k_out, REACH), (v_out, REACH))):
            cols = slice(third * width, (third + 1) * width)
            value = (acc[:, cols] + dot(x_s[...], w_s[:, cols])).astype(jnp.bfloat16)
            dst[pl.ds(pl.multiple_of(row + skip, STRETCH), rows), :] = value
    for copy in copies[n_first:]:
        copy.wait()

    @pl.when(core == 1)
    def _():
        project_halo(halo_refs, kv_out, k_out, v_out)

    chunks = rows // STRETCH

    def block_of(i):
        return jnp.where(i < chunks, (1 - core) * chunks + i, i - chunks + LEFT)

    count = jnp.where(core == 0, 2 * chunks - LEFT, chunks)
    attend(start_ref, owner_ref, left_ref, q_out, k_out, v_out, 0, count, block_of, out_ref)


def own_kernel(start_ref, owner_ref, left_ref, q_ref, k_ref, v_ref, kv_ref, *refs):
    *halo_refs, done_ref, out_ref, k_s, v_s = refs
    rows, width = out_ref.shape
    core = lax.axis_index("tm") % 2
    own = pl.multiple_of(core * rows + REACH, STRETCH)
    k_s[REACH:, :] = k_ref[pl.ds(own, rows), :]
    v_s[REACH:, :] = v_ref[pl.ds(own, rows), :]

    @pl.when(core == 0)
    def _():
        project_halo(halo_refs, kv_ref, k_s, v_s)

    @pl.when(core == 1)
    def _():
        k_s[:REACH, :] = k_ref[rows : rows + REACH, :]
        v_s[:REACH, :] = v_ref[rows : rows + REACH, :]

    chunks = rows // STRETCH
    base = core * chunks
    count = jnp.where(core == 0, LEFT, chunks)

    def block_of(i):
        return base + i

    attend(start_ref, owner_ref, left_ref, q_ref, k_s, v_s, base, count, block_of, out_ref)

    @pl.when(core == 0)
    def _():
        out_ref[REACH:, :] = done_ref[rows : 2 * rows - REACH, :]


def attend(start_ref, owner_ref, left_ref, q_s, k_s, v_s, k_base, count, block_of, out_ref):
    width = out_ref.shape[1]
    chunks = q_s.shape[0] // STRETCH
    pair = lax.axis_index("tm") // 2
    lane = lax.broadcasted_iota(jnp.int32, (1, width), 1)
    heads = width // HEAD_DIM

    def attend_block(chunk, start, lowest, q_row, k_row, span, out_ref, out_row):
        first_key = (chunk + 1) * STRETCH - span
        key_frame = first_key + lax.broadcasted_iota(jnp.int32, (1, STRETCH), 1)
        bias = jnp.where(key_frame >= lowest, 0.0, -jnp.inf).astype(jnp.float32)
        frame = chunk * STRETCH + lax.broadcasted_iota(jnp.int32, (STRETCH, 1), 0)
        live = frame >= start
        windows = [head_window(head) for head in range(heads)]
        insides = [
            ((lane >= head * HEAD_DIM) & (lane < (head + 1) * HEAD_DIM))[:, first:last]
            for head, (first, last) in enumerate(windows)
        ]
        tiles = [jnp.zeros((STRETCH, LANES), jnp.float32) for _ in range(width // LANES)]

        def score(head):
            first, last = windows[head]
            q = q_s[pl.ds(q_row, STRETCH), first:last]
            q = jnp.where(insides[head], q, jnp.zeros_like(q))
            return dot(q, k_s[pl.ds(k_row, span), first:last], ((1,), (1,)))

        def weigh(scores):
            scores = [scores[:, at : at + STRETCH] for at in range(0, span, STRETCH)]
            scores[0] = scores[0] + bias
            top = functools.reduce(jnp.maximum, scores)
            top = jnp.max(top, axis=-1, keepdims=True)
            expo = [jnp.exp2((part - top) * EXP_SCALE) for part in scores]
            total = jnp.sum(functools.reduce(jnp.add, expo), axis=-1, keepdims=True)
            share = 1.0 / total
            return jnp.concatenate([(part * share).astype(jnp.bfloat16) for part in expo], axis=1)

        def mix(head, probs):
            first, last = windows[head]
            mixed = dot(probs, v_s[pl.ds(k_row, span), first:last])
            for tile in range(first // LANES, last // LANES):
                at = tile * LANES - first
                tiles[tile] = jnp.where(
                    insides[head][:, at : at + LANES], mixed[:, at : at + LANES], tiles[tile]
                )

        scores = score(0)
        probs = None
        for head in range(heads):
            following = score(head + 1) if head + 1 < heads else None
            weighed = weigh(scores)
            if probs is not None:
                mix(head - 1, probs)
            scores, probs = following, weighed
        mix(heads - 1, probs)
        for tile, value in enumerate(tiles):
            value = jnp.where(live, value, 0.0).astype(jnp.bfloat16)
            out_ref[pl.ds(out_row, STRETCH), tile * LANES : (tile + 1) * LANES] = value

    @pl.loop(0, count)
    def _(i):
        block = block_of(i)
        out_row = pl.multiple_of(i * STRETCH, STRETCH)
        q_row = pl.multiple_of(block * STRETCH, STRETCH)
        chunk = pair * chunks + block
        left = left_ref[0, chunk]
        start = start_ref[0, owner_ref[0, chunk]]
        lowest = jnp.maximum((chunk - left) * STRETCH, start)
        for back in range(LEFT + 1):

            @pl.when(left == back)
            def _():
                k_row = pl.multiple_of((block - k_base + LEFT - back) * STRETCH, STRETCH)
                span = (back + 1) * STRETCH
                attend_block(chunk, start, lowest, q_row, k_row, span, out_ref, out_row)


def after(value, *others):
    return lax.optimization_barrier((value, *others))[0]


SMEM_SPEC = pl.BlockSpec(memory_space=pltpu.SMEM)
VMEM_SPEC = pl.BlockSpec(memory_space=pltpu.VMEM)
ANY_SPEC = pl.BlockSpec(memory_space=pl.ANY)


def half_kernel(w_ref, out_ref, sems):
    width = out_ref.shape[1] // 3
    core = lax.axis_index("tm") % 2
    pairs = []
    for third in range(3):
        at = pl.multiple_of((2 * third + core) * width, LANES)
        pairs.append((w_ref.at[:, pl.ds(at, width)], out_ref.at[:, third * width : (third + 1) * width]))
    for copy in start_all(sems, pairs):
        copy.wait()


def take_half(w):
    return pl.pallas_call(
        half_kernel,
        out_shape=jax.ShapeDtypeStruct((w.shape[0], w.shape[1] // 2), w.dtype),
        in_specs=[pl.BlockSpec(memory_space=pltpu.HBM)],
        out_specs=VMEM_SPEC,
        scratch_shapes=[pltpu.SemaphoreType.DMA((3,))],
        compiler_params=pltpu.CompilerParams(vmem_limit_bytes=4 * MIB),
        name="take_half",
    )(w)


def join_kernel(own_ref, other_ref, out_ref, sems):
    rows, width = own_ref.shape
    core = lax.axis_index("tm") % 2
    own_at = pl.multiple_of(core * width, LANES)
    other_at = pl.multiple_of((1 - core) * width, LANES)
    pairs = [
        (own_ref, out_ref.at[:, pl.ds(own_at, width)]),
        (other_ref.at[:rows, :], out_ref.at[:, pl.ds(other_at, width)]),
    ]
    for copy in start_all(sems, pairs):
        copy.wait()


def join(own, other):
    rows, width = own.shape
    return pl.pallas_call(
        join_kernel,
        out_shape=jax.ShapeDtypeStruct((rows, 2 * width), own.dtype),
        in_specs=[ANY_SPEC] * 2,
        out_specs=ANY_SPEC,
        scratch_shapes=[pltpu.SemaphoreType.DMA((2,))],
        compiler_params=pltpu.CompilerParams(vmem_limit_bytes=4 * MIB),
        name="join",
    )(own, other)


def project_early(blocks, inputs, partner):
    rows, depth = inputs.shape
    depth -= depth // GROUPS
    cols = blocks.operands[0].shape[1]
    n_copies = len(blocks.counts) - blocks.n_late + 2
    return pl.pallas_call(
        functools.partial(early_kernel, blocks),
        out_shape=[jax.ShapeDtypeStruct((rows, cols), jnp.float32)] * 2,
        in_specs=[ANY_SPEC] * (len(blocks.early_operands) + 2),
        out_specs=[VMEM_SPEC] * 2,
        scratch_shapes=[
            pltpu.VMEM((depth, cols), jnp.bfloat16),
            pltpu.VMEM((rows, depth), jnp.bfloat16),
            pltpu.VMEM((rows, depth), jnp.bfloat16),
            pltpu.SemaphoreType.DMA((n_copies,)),
        ],
        compiler_params=pltpu.CompilerParams(vmem_limit_bytes=24 * MIB),
        cost_estimate=pl.CostEstimate(flops=0, bytes_accessed=0, transcendentals=0),
        name="project_early",
    )(*blocks.early_operands, inputs, partner)


def tail_kernel(x_ref, *refs):
    *outs, sems = refs
    first = x_ref.shape[0] - len(outs) * STRETCH
    pairs = [
        (x_ref.at[first + i * STRETCH : first + (i + 1) * STRETCH, :], out)
        for i, out in enumerate(outs)
    ]
    for copy in start_all(sems, pairs):
        copy.wait()


def take_tail(x):
    return pl.pallas_call(
        tail_kernel,
        out_shape=[jax.ShapeDtypeStruct((STRETCH, x.shape[1]), x.dtype)] * LEFT,
        in_specs=[ANY_SPEC],
        out_specs=[VMEM_SPEC] * LEFT,
        scratch_shapes=[pltpu.SemaphoreType.DMA((LEFT,))],
        compiler_params=pltpu.CompilerParams(vmem_limit_bytes=4 * MIB),
        name="take_tail",
    )(x)


def project_late_attend(tables, blocks, inputs, partner, halo, sums):
    rows, depth = inputs.shape
    late_depth = depth // GROUPS
    cols = blocks.operands[0].shape[1]
    width = cols // 3
    keys = jax.ShapeDtypeStruct((2 * rows + REACH, width), jnp.bfloat16)
    return pl.pallas_call(
        functools.partial(late_kernel, blocks),
        out_shape=[
            jax.ShapeDtypeStruct((2 * rows - REACH, width), jnp.bfloat16),
            jax.ShapeDtypeStruct((2 * rows, width), jnp.bfloat16),
            keys,
            keys,
            jax.ShapeDtypeStruct((depth, 2 * width), jnp.bfloat16),
        ],
        in_specs=[SMEM_SPEC] * 3 + [ANY_SPEC] * (len(blocks.operands) + 2) + [VMEM_SPEC] * (LEFT + 2),
        out_specs=[VMEM_SPEC] * 5,
        scratch_shapes=[
            pltpu.VMEM((late_depth, cols), jnp.bfloat16),
            pltpu.VMEM((rows, late_depth), jnp.bfloat16),
            pltpu.VMEM((rows, late_depth), jnp.bfloat16),
            pltpu.SemaphoreType.DMA((len(blocks.counts) + blocks.n_late + 2,)),
        ],
        compiler_params=pltpu.CompilerParams(vmem_limit_bytes=24 * MIB),
        name="project_late_attend",
    )(*tables, *blocks.operands, inputs, partner, *halo, *sums)


def attend_own(tables, queries, keys, values, weights, halo, done):
    rows, width = queries.shape
    rows //= 2
    return pl.pallas_call(
        own_kernel,
        out_shape=jax.ShapeDtypeStruct((rows, width), jnp.bfloat16),
        in_specs=[SMEM_SPEC] * 3 + [VMEM_SPEC] * (LEFT + 5),
        out_specs=VMEM_SPEC,
        scratch_shapes=[pltpu.VMEM((rows + REACH, width), jnp.bfloat16)] * 2,
        compiler_params=pltpu.CompilerParams(vmem_limit_bytes=20 * MIB),
        name="attend_own",
    )(*tables, queries, keys, values, weights, *halo, done)


def at_end():
    place = lax.axis_index("dp") // 2
    return jnp.where((place == 0) | (place == 3), 1, 0)


def choose_kernel(between_ref, end_ref, out_ref, sems):
    for copy in start_all(sems, [((between_ref, end_ref), at_end(), out_ref)]):
        copy.wait()


def choose(between, end):
    return pl.pallas_call(
        choose_kernel,
        out_shape=jax.ShapeDtypeStruct(end.shape, end.dtype),
        in_specs=[ANY_SPEC] * 2,
        out_specs=VMEM_SPEC,
        scratch_shapes=[pltpu.SemaphoreType.DMA((1,))],
        compiler_params=pltpu.CompilerParams(vmem_limit_bytes=2 * MIB),
        name="choose",
    )(between, end)


def gather_neighbours(half):
    size = half.shape[0]

    def along(name, block, hops):
        with jax.named_scope(name):
            return lax.ppermute(
                block, "dp", [(2 * a + s, 2 * b + s) for a, b in hops for s in range(2)]
            )

    def across(name, block, places):
        with jax.named_scope(name):
            return lax.ppermute(
                block, "dp", [(2 * a + s, 2 * a + 1 - s) for a in places for s in range(2)]
            )

    line = range(4)
    outward = [(1, 0), (2, 3)]
    between = [(1, 2), (2, 1)]
    near = along("near", half, outward + [(0, 1), (3, 2)])
    mid = along("mid", half, between)
    half_across = across("half_across", half, line)
    mid_far = along("mid_far", near, between)
    near_across = across("near_across", after(near, half_across, mid), line)
    end_mid = along("end_mid", mid, outward)
    end_far = along("end_far", after(mid_far, end_mid), outward)
    second = choose(mid, end_mid)
    second_across = across("second_across", after(second, near_across), line)
    third = choose(mid_far, end_far)
    third_across = across("third_across", after(third, second_across), line)

    def find():
        index = lax.axis_index("dp")
        place, side = index // 2, index % 2
        is_end = at_end()
        second = jnp.where(is_end == 1, place ^ 2, 3 - place)
        third = jnp.where(is_end == 1, 3 - place, place ^ 2)
        spots = (place, place ^ 1, second, third)
        found = [((2 * spot + (side ^ n)) * size, is_end) for spot in spots for n in range(2)]
        return found, third * 2 * size

    blocks = [
        (half,),
        (half_across,),
        (near,),
        (near_across,),
        (second,),
        (second_across,),
        (third,),
        (third_across,),
    ]
    marks = (near_across, mid_far, end_mid), (second_across, end_far), (third_across,)
    return Blocks(blocks, 2, find), marks


def local(frames, w_qkv, utt_start, stretch_utt, left_stretches):
    inputs = frames[0]
    depth = inputs.shape[1]
    members = lax.axis_size("tm")

    half = take_half(w_qkv)

    tail = take_tail(after(inputs, half))
    with jax.named_scope("partner"):
        partner = lax.ppermute(inputs, "tm", [(i, i ^ 1) for i in range(members)])
    if lax.axis_size("dp") == 8:
        blocks, marks = gather_neighbours(half)
    else:
        weights = lax.all_gather(half, "dp", axis=0, tiled=True)
        late_first = depth - depth // GROUPS
        found = [(0, 0), (late_first, 0)], late_first
        parts = [(weights[:late_first],), (weights[late_first:],)]
        blocks, marks = Blocks(parts, 1, lambda: found), ((half,),) * 3

    with jax.named_scope("halo"):
        onward = [(i, i + 2) for i in range(1, members - 2, 2)]
        halo = [lax.ppermute(after(x, *mark), "tm", onward) for x, mark in zip(tail, marks)]

    tables = (utt_start, stretch_utt, left_stretches)
    sums = project_early(blocks, inputs, partner)
    with jax.named_scope("halo_first"):
        back = [(i + 1, i) for i in range(0, members, 2)]
        halo_first = [lax.ppermute(after(x, *sums), "tm", back) for x in halo]
    attended, queries, keys, values, weights = project_late_attend(
        tables, blocks, inputs, partner, halo, sums
    )
    with jax.named_scope("swap"):
        other = lax.ppermute(attended, "tm", [(i, i ^ 1) for i in range(members)])
    own_out = attend_own(tables, queries, keys, values, weights, halo_first, attended)
    return join(own_out, other)[None]


def solution(mesh):
    return jax.shard_map(
        local,
        mesh=mesh,
        in_specs=(P("dp", "tm", None), P("dp", None), P("dp", None), P("dp", None), P("dp", None)),
        out_specs=P("dp", "tm", None),
        check_vma=False,
    )
```

```python
import functools
import math

import jax
import jax.numpy as jnp
from jax import lax
from jax.experimental import pallas as pl
from jax.experimental.pallas import tpu as pltpu
from jax.sharding import PartitionSpec as P

HEAD_DIM = 96
STRETCH = 256
LEFT = 2
LANES = 128
GROUPS = 4
EXP_SCALE = HEAD_DIM**-0.5 * math.log2(math.e)
REACH = LEFT * STRETCH
MIB = 1024 * 1024


def dot(a, b, dims=((1,), (0,))):
    return lax.dot_general(a, b, (dims, ((), ())), preferred_element_type=jnp.float32)


def head_window(head):
    first = head * HEAD_DIM // LANES * LANES
    last = -(-(head + 1) * HEAD_DIM // LANES) * LANES
    return first, last


def start_all(sems, pairs):
    copies = []
    for i, (*source, target) in enumerate(pairs):
        if len(source) == 1:
            copy = pltpu.make_async_copy(source[0], target, sems.at[i])
            copy.start()
        else:
            for n, choice in enumerate(source[0]):
                copy = pltpu.make_async_copy(choice, target, sems.at[i])
                pl.when(source[1] == n)(copy.start)
        copies.append(copy)
    return copies


class Blocks:
    def __init__(self, blocks, n_late, find):
        self.operands = [operand for block in blocks for operand in block]
        self.counts = [len(block) for block in blocks]
        self.rows = [block[0].shape[0] for block in blocks]
        self.n_late = n_late
        self.early_operands = self.operands[: sum(self.counts[:-n_late])]
        self.find = find

    def copies(self, refs, found, members, target, first=0, columns=slice(None)):
        pairs = []
        for i in members:
            at = sum(self.counts[:i])
            choices = [ref.at[:, columns] for ref in refs[at : at + self.counts[i]]]
            row, which = found[i]
            goal = target.at[pl.ds(pl.multiple_of(row - first, self.rows[i]), self.rows[i])]
            pairs.append((choices[0], goal) if len(choices) == 1 else (choices, which, goal))
        return pairs


def early_kernel(blocks, *refs):
    n = len(blocks.early_operands)
    own_ref, partner_ref, own_sum, partner_sum, w_s, own_s, partner_s, sems = refs[n:]
    found, late_first = blocks.find()
    depth = w_s.shape[0]
    first = jnp.where(late_first == 0, own_ref.shape[1] - depth, 0)
    members = range(len(found) - blocks.n_late)
    pairs = blocks.copies(refs, found, members, w_s, first)
    columns = pl.ds(pl.multiple_of(first, LANES), depth)
    pairs.append((own_ref.at[:, columns], own_s))
    pairs.append((partner_ref.at[:, columns], partner_s))
    *first_copies, last_copy = start_all(sems, pairs)
    for copy in first_copies:
        copy.wait()
    own_sum[...] = dot(own_s[...], w_s[...])
    last_copy.wait()
    partner_sum[...] = dot(partner_s[...], w_s[...])


def project_halo(halo_refs, kv_ref, k_ref, v_ref):
    width = k_ref.shape[1]
    for i, frames_ref in enumerate(halo_refs):
        at = slice(i * STRETCH, (i + 1) * STRETCH)
        both = dot(frames_ref[...], kv_ref[...]).astype(jnp.bfloat16)
        k_ref[at, :] = both[:, :width]
        v_ref[at, :] = both[:, width:]


def late_kernel(blocks, start_ref, owner_ref, left_ref, *refs):
    n = len(blocks.operands)
    own_ref, partner_ref = refs[n : n + 2]
    halo_refs = refs[n + 2 : n + 2 + LEFT]
    own_sum, partner_sum, out_ref, q_out, k_out, v_out, kv_out, *scratch = refs[n + 2 + LEFT :]
    w_s, own_s, partner_s, sems = scratch
    depth = w_s.shape[0]
    width = w_s.shape[1] // 3
    rows = own_s.shape[0]
    core = lax.axis_index("tm") % 2
    found, late_first = blocks.find()
    everything = range(len(found))
    pairs = blocks.copies(refs, found, everything[-blocks.n_late :], w_s, late_first)
    columns = pl.ds(pl.multiple_of(late_first, LANES), depth)
    pairs.append((partner_ref.at[:, columns], partner_s))
    pairs.append((own_ref.at[:, columns], own_s))
    n_first = len(pairs)
    pairs += blocks.copies(refs, found, everything, kv_out, 0, slice(width, 3 * width))
    copies = start_all(sems, pairs)
    for copy in copies[: n_first - 1]:
        copy.wait()
    for x_s, acc, place in ((partner_s, partner_sum, 1 - core), (own_s, own_sum, core)):
        if x_s is own_s:
            copies[n_first - 1].wait()
        row = pl.multiple_of(place * rows, STRETCH)
        value = (acc[...] + dot(x_s[...], w_s[...])).astype(jnp.bfloat16)
        for third, (dst, skip) in enumerate(((q_out, 0), (k_out, REACH), (v_out, REACH))):
            part = value[:, third * width : (third + 1) * width]
            dst[pl.ds(pl.multiple_of(row + skip, STRETCH), rows), :] = part
    for copy in copies[n_first:]:
        copy.wait()

    @pl.when(core == 1)
    def _():
        project_halo(halo_refs, kv_out, k_out, v_out)

    chunks = rows // STRETCH

    def block_of(i):
        return jnp.where(i < chunks, (1 - core) * chunks + i, i - chunks + LEFT)

    count = jnp.where(core == 0, 2 * chunks - LEFT, chunks)
    attend(start_ref, owner_ref, left_ref, q_out, k_out, v_out, 0, count, block_of, out_ref)


def own_kernel(start_ref, owner_ref, left_ref, q_ref, k_ref, v_ref, kv_ref, *refs):
    *halo_refs, done_ref, out_ref, k_s, v_s = refs
    rows, width = out_ref.shape
    core = lax.axis_index("tm") % 2
    own = pl.multiple_of(core * rows + REACH, STRETCH)
    k_s[REACH:, :] = k_ref[pl.ds(own, rows), :]
    v_s[REACH:, :] = v_ref[pl.ds(own, rows), :]

    @pl.when(core == 0)
    def _():
        project_halo(halo_refs, kv_ref, k_s, v_s)

    @pl.when(core == 1)
    def _():
        k_s[:REACH, :] = k_ref[rows : rows + REACH, :]
        v_s[:REACH, :] = v_ref[rows : rows + REACH, :]

    chunks = rows // STRETCH
    base = core * chunks
    count = jnp.where(core == 0, LEFT, chunks)

    def block_of(i):
        return base + i

    attend(start_ref, owner_ref, left_ref, q_ref, k_s, v_s, base, count, block_of, out_ref)

    @pl.when(core == 0)
    def _():
        out_ref[REACH:, :] = done_ref[rows : 2 * rows - REACH, :]


def attend(start_ref, owner_ref, left_ref, q_s, k_s, v_s, k_base, count, block_of, out_ref):
    width = out_ref.shape[1]
    chunks = q_s.shape[0] // STRETCH
    pair = lax.axis_index("tm") // 2
    lane = lax.broadcasted_iota(jnp.int32, (1, width), 1)
    heads = width // HEAD_DIM

    def attend_block(chunk, start, lowest, q_row, k_row, span, out_ref, out_row):
        first_key = (chunk + 1) * STRETCH - span
        key_frame = first_key + lax.broadcasted_iota(jnp.int32, (1, STRETCH), 1)
        bias = jnp.where(key_frame >= lowest, 0.0, -jnp.inf).astype(jnp.float32)
        frame = chunk * STRETCH + lax.broadcasted_iota(jnp.int32, (STRETCH, 1), 0)
        live = frame >= start
        windows = [head_window(head) for head in range(heads)]
        insides = [
            ((lane >= head * HEAD_DIM) & (lane < (head + 1) * HEAD_DIM))[:, first:last]
            for head, (first, last) in enumerate(windows)
        ]
        tiles = [jnp.zeros((STRETCH, LANES), jnp.float32) for _ in range(width // LANES)]

        def score(head):
            first, last = windows[head]
            q = q_s[pl.ds(q_row, STRETCH), first:last]
            q = jnp.where(insides[head], q, jnp.zeros_like(q))
            return dot(q, k_s[pl.ds(k_row, span), first:last], ((1,), (1,)))

        def weigh(scores):
            scores = [scores[:, at : at + STRETCH] for at in range(0, span, STRETCH)]
            scores[0] = scores[0] + bias
            top = functools.reduce(jnp.maximum, scores)
            top = jnp.max(top, axis=-1, keepdims=True)
            expo = [jnp.exp2((part - top) * EXP_SCALE) for part in scores]
            total = jnp.sum(functools.reduce(jnp.add, expo), axis=-1, keepdims=True)
            share = 1.0 / total
            return jnp.concatenate([(part * share).astype(jnp.bfloat16) for part in expo], axis=1)

        def mix(head, probs):
            first, last = windows[head]
            mixed = dot(probs, v_s[pl.ds(k_row, span), first:last])
            for tile in range(first // LANES, last // LANES):
                at = tile * LANES - first
                tiles[tile] = jnp.where(
                    insides[head][:, at : at + LANES], mixed[:, at : at + LANES], tiles[tile]
                )

        scores = score(0)
        probs = None
        for head in range(heads):
            following = score(head + 1) if head + 1 < heads else None
            weighed = weigh(scores)
            if probs is not None:
                mix(head - 1, probs)
            scores, probs = following, weighed
        mix(heads - 1, probs)
        for tile, value in enumerate(tiles):
            value = jnp.where(live, value, 0.0).astype(jnp.bfloat16)
            out_ref[pl.ds(out_row, STRETCH), tile * LANES : (tile + 1) * LANES] = value

    @pl.loop(0, count)
    def _(i):
        block = block_of(i)
        out_row = pl.multiple_of(i * STRETCH, STRETCH)
        q_row = pl.multiple_of(block * STRETCH, STRETCH)
        chunk = pair * chunks + block
        left = left_ref[0, chunk]
        start = start_ref[0, owner_ref[0, chunk]]
        lowest = jnp.maximum((chunk - left) * STRETCH, start)
        for back in range(LEFT + 1):

            @pl.when(left == back)
            def _():
                k_row = pl.multiple_of((block - k_base + LEFT - back) * STRETCH, STRETCH)
                span = (back + 1) * STRETCH
                attend_block(chunk, start, lowest, q_row, k_row, span, out_ref, out_row)


def after(value, *others):
    return lax.optimization_barrier((value, *others))[0]


SMEM_SPEC = pl.BlockSpec(memory_space=pltpu.SMEM)
VMEM_SPEC = pl.BlockSpec(memory_space=pltpu.VMEM)
ANY_SPEC = pl.BlockSpec(memory_space=pl.ANY)


def half_kernel(w_ref, out_ref, sems):
    width = out_ref.shape[1] // 3
    core = lax.axis_index("tm") % 2
    pairs = []
    for third in range(3):
        at = pl.multiple_of((2 * third + core) * width, LANES)
        pairs.append((w_ref.at[:, pl.ds(at, width)], out_ref.at[:, third * width : (third + 1) * width]))
    for copy in start_all(sems, pairs):
        copy.wait()


def take_half(w):
    return pl.pallas_call(
        half_kernel,
        out_shape=jax.ShapeDtypeStruct((w.shape[0], w.shape[1] // 2), w.dtype),
        in_specs=[pl.BlockSpec(memory_space=pltpu.HBM)],
        out_specs=VMEM_SPEC,
        scratch_shapes=[pltpu.SemaphoreType.DMA((3,))],
        compiler_params=pltpu.CompilerParams(vmem_limit_bytes=4 * MIB),
        name="take_half",
    )(w)


def join_kernel(own_ref, other_ref, out_ref, sems):
    rows, width = own_ref.shape
    core = lax.axis_index("tm") % 2
    own_at = pl.multiple_of(core * width, LANES)
    other_at = pl.multiple_of((1 - core) * width, LANES)
    pairs = [
        (own_ref, out_ref.at[:, pl.ds(own_at, width)]),
        (other_ref.at[:rows, :], out_ref.at[:, pl.ds(other_at, width)]),
    ]
    for copy in start_all(sems, pairs):
        copy.wait()


def join(own, other):
    rows, width = own.shape
    return pl.pallas_call(
        join_kernel,
        out_shape=jax.ShapeDtypeStruct((rows, 2 * width), own.dtype),
        in_specs=[ANY_SPEC] * 2,
        out_specs=ANY_SPEC,
        scratch_shapes=[pltpu.SemaphoreType.DMA((2,))],
        compiler_params=pltpu.CompilerParams(vmem_limit_bytes=4 * MIB),
        name="join",
    )(own, other)


def project_early(blocks, inputs, partner):
    rows, depth = inputs.shape
    depth -= depth // GROUPS
    cols = blocks.operands[0].shape[1]
    n_copies = len(blocks.counts) - blocks.n_late + 2
    return pl.pallas_call(
        functools.partial(early_kernel, blocks),
        out_shape=[jax.ShapeDtypeStruct((rows, cols), jnp.float32)] * 2,
        in_specs=[ANY_SPEC] * (len(blocks.early_operands) + 2),
        out_specs=[VMEM_SPEC] * 2,
        scratch_shapes=[
            pltpu.VMEM((depth, cols), jnp.bfloat16),
            pltpu.VMEM((rows, depth), jnp.bfloat16),
            pltpu.VMEM((rows, depth), jnp.bfloat16),
            pltpu.SemaphoreType.DMA((n_copies,)),
        ],
        compiler_params=pltpu.CompilerParams(vmem_limit_bytes=24 * MIB),
        cost_estimate=pl.CostEstimate(flops=0, bytes_accessed=0, transcendentals=0),
        name="project_early",
    )(*blocks.early_operands, inputs, partner)


def tail_kernel(x_ref, *refs):
    *outs, sems = refs
    first = x_ref.shape[0] - len(outs) * STRETCH
    pairs = [
        (x_ref.at[first + i * STRETCH : first + (i + 1) * STRETCH, :], out)
        for i, out in enumerate(outs)
    ]
    for copy in start_all(sems, pairs):
        copy.wait()


def take_tail(x):
    return pl.pallas_call(
        tail_kernel,
        out_shape=[jax.ShapeDtypeStruct((STRETCH, x.shape[1]), x.dtype)] * LEFT,
        in_specs=[ANY_SPEC],
        out_specs=[VMEM_SPEC] * LEFT,
        scratch_shapes=[pltpu.SemaphoreType.DMA((LEFT,))],
        compiler_params=pltpu.CompilerParams(vmem_limit_bytes=4 * MIB),
        name="take_tail",
    )(x)


def project_late_attend(tables, blocks, inputs, partner, halo, sums):
    rows, depth = inputs.shape
    late_depth = depth // GROUPS
    cols = blocks.operands[0].shape[1]
    width = cols // 3
    keys = jax.ShapeDtypeStruct((2 * rows + REACH, width), jnp.bfloat16)
    return pl.pallas_call(
        functools.partial(late_kernel, blocks),
        out_shape=[
            jax.ShapeDtypeStruct((2 * rows - REACH, width), jnp.bfloat16),
            jax.ShapeDtypeStruct((2 * rows, width), jnp.bfloat16),
            keys,
            keys,
            jax.ShapeDtypeStruct((depth, 2 * width), jnp.bfloat16),
        ],
        in_specs=[SMEM_SPEC] * 3 + [ANY_SPEC] * (len(blocks.operands) + 2) + [VMEM_SPEC] * (LEFT + 2),
        out_specs=[VMEM_SPEC] * 5,
        scratch_shapes=[
            pltpu.VMEM((late_depth, cols), jnp.bfloat16),
            pltpu.VMEM((rows, late_depth), jnp.bfloat16),
            pltpu.VMEM((rows, late_depth), jnp.bfloat16),
            pltpu.SemaphoreType.DMA((len(blocks.counts) + blocks.n_late + 2,)),
        ],
        compiler_params=pltpu.CompilerParams(vmem_limit_bytes=24 * MIB),
        name="project_late_attend",
    )(*tables, *blocks.operands, inputs, partner, *halo, *sums)


def attend_own(tables, queries, keys, values, weights, halo, done):
    rows, width = queries.shape
    rows //= 2
    return pl.pallas_call(
        own_kernel,
        out_shape=jax.ShapeDtypeStruct((rows, width), jnp.bfloat16),
        in_specs=[SMEM_SPEC] * 3 + [VMEM_SPEC] * (LEFT + 5),
        out_specs=VMEM_SPEC,
        scratch_shapes=[pltpu.VMEM((rows + REACH, width), jnp.bfloat16)] * 2,
        compiler_params=pltpu.CompilerParams(vmem_limit_bytes=20 * MIB),
        name="attend_own",
    )(*tables, queries, keys, values, weights, *halo, done)


def at_end():
    place = lax.axis_index("dp") // 2
    return jnp.where((place == 0) | (place == 3), 1, 0)


def choose_kernel(between_ref, end_ref, out_ref, sems):
    for copy in start_all(sems, [((between_ref, end_ref), at_end(), out_ref)]):
        copy.wait()


def choose(between, end):
    return pl.pallas_call(
        choose_kernel,
        out_shape=jax.ShapeDtypeStruct(end.shape, end.dtype),
        in_specs=[ANY_SPEC] * 2,
        out_specs=VMEM_SPEC,
        scratch_shapes=[pltpu.SemaphoreType.DMA((1,))],
        compiler_params=pltpu.CompilerParams(vmem_limit_bytes=2 * MIB),
        name="choose",
    )(between, end)


def gather_neighbours(half):
    size = half.shape[0]

    def along(name, block, hops):
        with jax.named_scope(name):
            return lax.ppermute(
                block, "dp", [(2 * a + s, 2 * b + s) for a, b in hops for s in range(2)]
            )

    def across(name, block, places):
        with jax.named_scope(name):
            return lax.ppermute(
                block, "dp", [(2 * a + s, 2 * a + 1 - s) for a in places for s in range(2)]
            )

    line = range(4)
    outward = [(1, 0), (2, 3)]
    between = [(1, 2), (2, 1)]
    near = along("near", half, outward + [(0, 1), (3, 2)])
    mid = along("mid", half, between)
    half_across = across("half_across", half, line)
    mid_far = along("mid_far", near, between)
    near_across = across("near_across", after(near, half_across, mid), line)
    end_mid = along("end_mid", mid, outward)
    end_far = along("end_far", after(mid_far, end_mid), outward)
    second = choose(mid, end_mid)
    second_across = across("second_across", after(second, near_across), line)
    third = choose(mid_far, end_far)
    third_across = across("third_across", after(third, second_across), line)

    def find():
        index = lax.axis_index("dp")
        place, side = index // 2, index % 2
        is_end = at_end()
        second = jnp.where(is_end == 1, place ^ 2, 3 - place)
        third = jnp.where(is_end == 1, 3 - place, place ^ 2)
        spots = (place, place ^ 1, second, third)
        found = [((2 * spot + (side ^ n)) * size, is_end) for spot in spots for n in range(2)]
        return found, third * 2 * size

    blocks = [
        (half,),
        (half_across,),
        (near,),
        (near_across,),
        (second,),
        (second_across,),
        (third,),
        (third_across,),
    ]
    marks = (near_across, mid_far, end_mid), (second_across, end_far), (third_across,)
    return Blocks(blocks, 2, find), marks


def local(frames, w_qkv, utt_start, stretch_utt, left_stretches):
    inputs = frames[0]
    depth = inputs.shape[1]
    members = lax.axis_size("tm")

    half = take_half(w_qkv)

    tail = take_tail(after(inputs, half))
    with jax.named_scope("partner"):
        partner = lax.ppermute(inputs, "tm", [(i, i ^ 1) for i in range(members)])
    if lax.axis_size("dp") == 8:
        blocks, marks = gather_neighbours(half)
    else:
        weights = lax.all_gather(half, "dp", axis=0, tiled=True)
        late_first = depth - depth // GROUPS
        found = [(0, 0), (late_first, 0)], late_first
        parts = [(weights[:late_first],), (weights[late_first:],)]
        blocks, marks = Blocks(parts, 1, lambda: found), ((half,),) * 3

    with jax.named_scope("halo"):
        onward = [(i, i + 2) for i in range(1, members - 2, 2)]
        halo = [lax.ppermute(after(x, *mark), "tm", onward) for x, mark in zip(tail, marks)]

    tables = (utt_start, stretch_utt, left_stretches)
    sums = project_early(blocks, inputs, partner)
    with jax.named_scope("halo_first"):
        back = [(i + 1, i) for i in range(0, members, 2)]
        halo_first = [lax.ppermute(after(x, *sums), "tm", back) for x in halo]
    attended, queries, keys, values, weights = project_late_attend(
        tables, blocks, inputs, partner, halo, sums
    )
    with jax.named_scope("swap"):
        other = lax.ppermute(attended, "tm", [(i, i ^ 1) for i in range(members)])
    own_out = attend_own(tables, queries, keys, values, weights, halo_first, attended)
    return join(own_out, other)[None]


def solution(mesh):
    return jax.shard_map(
        local,
        mesh=mesh,
        in_specs=(P("dp", "tm", None), P("dp", None), P("dp", None), P("dp", None), P("dp", None)),
        out_specs=P("dp", "tm", None),
        check_vma=False,
    )
```

```python
import functools
import math

import jax
import jax.numpy as jnp
from jax import lax
from jax.experimental import pallas as pl
from jax.experimental.pallas import tpu as pltpu
from jax.sharding import PartitionSpec as P

HEAD_DIM = 96
STRETCH = 256
LEFT = 2
LANES = 128
GROUPS = 4
EXP_SCALE = HEAD_DIM**-0.5 * math.log2(math.e)
REACH = LEFT * STRETCH
MIB = 1024 * 1024


def dot(a, b, dims=((1,), (0,))):
    return lax.dot_general(a, b, (dims, ((), ())), preferred_element_type=jnp.float32)


def head_window(head):
    first = head * HEAD_DIM // LANES * LANES
    last = -(-(head + 1) * HEAD_DIM // LANES) * LANES
    return first, last


def start_all(sems, pairs):
    copies = []
    for i, (*source, target) in enumerate(pairs):
        if len(source) == 1:
            copy = pltpu.make_async_copy(source[0], target, sems.at[i])
            copy.start()
        else:
            for n, choice in enumerate(source[0]):
                copy = pltpu.make_async_copy(choice, target, sems.at[i])
                pl.when(source[1] == n)(copy.start)
        copies.append(copy)
    return copies


class Blocks:
    def __init__(self, blocks, steps, find):
        self.operands = list(blocks)
        self.rows = [block.shape[0] for block in blocks]
        self.steps = steps
        self.find = find

    def step_operands(self, step):
        return [self.operands[i] for i in self.steps[step]]

    def step_depth(self, step):
        return sum(self.rows[i] for i in self.steps[step])

    def copies(self, refs, found, members, target, first=0, columns=slice(None)):
        pairs = []
        for ref, i in zip(refs, members):
            rows = self.rows[i]
            goal = target.at[pl.ds(pl.multiple_of(found[i] - first, rows), rows)]
            pairs.append((ref.at[:, columns], goal))
        return pairs


def early_kernel(blocks, step, *refs):
    n = len(blocks.step_operands(step))
    own_ref, partner_ref, *sums = refs[n : n + 2 + 2 * min(step, 1)]
    own_out, partner_out, w_s, own_s, partner_s, sems = refs[n + 2 + len(sums) :]
    found, firsts = blocks.find()
    depth = w_s.shape[0]
    first = firsts[step]
    pairs = blocks.copies(refs, found, blocks.steps[step], w_s, first)
    columns = pl.ds(pl.multiple_of(first, LANES), depth)
    pairs.append((own_ref.at[:, columns], own_s))
    pairs.append((partner_ref.at[:, columns], partner_s))
    *first_copies, last_copy = start_all(sems, pairs)
    for copy in first_copies:
        copy.wait()
    own = dot(own_s[...], w_s[...])
    own_out[...] = own + sums[0][...] if sums else own
    last_copy.wait()
    partner = dot(partner_s[...], w_s[...])
    partner_out[...] = partner + sums[1][...] if sums else partner


def project_halo(halo_refs, kv_ref, k_ref, v_ref):
    width = k_ref.shape[1]
    for i, frames_ref in enumerate(halo_refs):
        at = slice(i * STRETCH, (i + 1) * STRETCH)
        both = dot(frames_ref[...], kv_ref[...]).astype(jnp.bfloat16)
        k_ref[at, :] = both[:, :width]
        v_ref[at, :] = both[:, width:]


def late_kernel(blocks, start_ref, owner_ref, left_ref, *refs):
    n = len(blocks.operands)
    own_ref, partner_ref = refs[n : n + 2]
    halo_refs = refs[n + 2 : n + 2 + LEFT]
    own_sum, partner_sum, out_ref, q_out, k_out, v_out, kv_out, *scratch = refs[n + 2 + LEFT :]
    w_s, own_s, partner_s, sems = scratch
    depth = w_s.shape[0]
    width = w_s.shape[1] // 3
    rows = own_s.shape[0]
    core = lax.axis_index("tm") % 2
    found, (*_, late_first) = blocks.find()
    everything = range(len(found))
    last = blocks.steps[-1]
    pairs = blocks.copies([refs[i] for i in last], found, last, w_s, late_first)
    columns = pl.ds(pl.multiple_of(late_first, LANES), depth)
    pairs.append((partner_ref.at[:, columns], partner_s))
    pairs.append((own_ref.at[:, columns], own_s))
    n_first = len(pairs)
    pairs += blocks.copies(refs, found, everything, kv_out, 0, slice(width, 3 * width))
    copies = start_all(sems, pairs)
    for copy in copies[: n_first - 1]:
        copy.wait()
    for x_s, acc, place in ((partner_s, partner_sum, 1 - core), (own_s, own_sum, core)):
        if x_s is own_s:
            copies[n_first - 1].wait()
        row = pl.multiple_of(place * rows, STRETCH)
        value = (acc[...] + dot(x_s[...], w_s[...])).astype(jnp.bfloat16)
        for third, (dst, skip) in enumerate(((q_out, 0), (k_out, REACH), (v_out, REACH))):
            part = value[:, third * width : (third + 1) * width]
            dst[pl.ds(pl.multiple_of(row + skip, STRETCH), rows), :] = part
    for copy in copies[n_first:]:
        copy.wait()

    @pl.when(core == 1)
    def _():
        project_halo(halo_refs, kv_out, k_out, v_out)

    chunks = rows // STRETCH

    def block_of(i):
        return jnp.where(i < chunks, (1 - core) * chunks + i, i - chunks + LEFT)

    count = jnp.where(core == 0, 2 * chunks - LEFT, chunks)
    attend(start_ref, owner_ref, left_ref, q_out, k_out, v_out, 0, count, block_of, out_ref)


def own_kernel(start_ref, owner_ref, left_ref, q_ref, k_ref, v_ref, kv_ref, *refs):
    *halo_refs, done_ref, out_ref, k_s, v_s = refs
    rows, width = out_ref.shape
    core = lax.axis_index("tm") % 2
    own = pl.multiple_of(core * rows + REACH, STRETCH)
    k_s[REACH:, :] = k_ref[pl.ds(own, rows), :]
    v_s[REACH:, :] = v_ref[pl.ds(own, rows), :]

    @pl.when(core == 0)
    def _():
        project_halo(halo_refs, kv_ref, k_s, v_s)

    @pl.when(core == 1)
    def _():
        k_s[:REACH, :] = k_ref[rows : rows + REACH, :]
        v_s[:REACH, :] = v_ref[rows : rows + REACH, :]

    chunks = rows // STRETCH
    base = core * chunks
    count = jnp.where(core == 0, LEFT, chunks)

    def block_of(i):
        return base + i

    attend(start_ref, owner_ref, left_ref, q_ref, k_s, v_s, base, count, block_of, out_ref)

    @pl.when(core == 0)
    def _():
        out_ref[REACH:, :] = done_ref[rows : 2 * rows - REACH, :]


def attend(start_ref, owner_ref, left_ref, q_s, k_s, v_s, k_base, count, block_of, out_ref):
    width = out_ref.shape[1]
    chunks = q_s.shape[0] // STRETCH
    pair = lax.axis_index("tm") // 2
    lane = lax.broadcasted_iota(jnp.int32, (1, width), 1)
    heads = width // HEAD_DIM

    def attend_block(chunk, start, lowest, q_row, k_row, span, out_ref, out_row):
        first_key = (chunk + 1) * STRETCH - span
        key_frame = first_key + lax.broadcasted_iota(jnp.int32, (1, STRETCH), 1)
        bias = jnp.where(key_frame >= lowest, 0.0, -jnp.inf).astype(jnp.float32)
        frame = chunk * STRETCH + lax.broadcasted_iota(jnp.int32, (STRETCH, 1), 0)
        live = frame >= start
        windows = [head_window(head) for head in range(heads)]
        insides = [
            ((lane >= head * HEAD_DIM) & (lane < (head + 1) * HEAD_DIM))[:, first:last]
            for head, (first, last) in enumerate(windows)
        ]
        tiles = [jnp.zeros((STRETCH, LANES), jnp.float32) for _ in range(width // LANES)]

        def score(head):
            first, last = windows[head]
            q = q_s[pl.ds(q_row, STRETCH), first:last]
            q = jnp.where(insides[head], q, jnp.zeros_like(q))
            return dot(q, k_s[pl.ds(k_row, span), first:last], ((1,), (1,)))

        def weigh(scores):
            scores = [scores[:, at : at + STRETCH] for at in range(0, span, STRETCH)]
            scores[0] = scores[0] + bias
            top = functools.reduce(jnp.maximum, scores)
            top = jnp.max(top, axis=-1, keepdims=True)
            expo = [jnp.exp2((part - top) * EXP_SCALE) for part in scores]
            total = jnp.sum(functools.reduce(jnp.add, expo), axis=-1, keepdims=True)
            share = 1.0 / total
            return jnp.concatenate([(part * share).astype(jnp.bfloat16) for part in expo], axis=1)

        def mix(head, probs):
            first, last = windows[head]
            mixed = dot(probs, v_s[pl.ds(k_row, span), first:last])
            for tile in range(first // LANES, last // LANES):
                at = tile * LANES - first
                tiles[tile] = jnp.where(
                    insides[head][:, at : at + LANES], mixed[:, at : at + LANES], tiles[tile]
                )

        scores = score(0)
        probs = None
        for head in range(heads):
            following = score(head + 1) if head + 1 < heads else None
            weighed = weigh(scores)
            if probs is not None:
                mix(head - 1, probs)
            scores, probs = following, weighed
        mix(heads - 1, probs)
        for tile, value in enumerate(tiles):
            value = jnp.where(live, value, 0.0).astype(jnp.bfloat16)
            out_ref[pl.ds(out_row, STRETCH), tile * LANES : (tile + 1) * LANES] = value

    @pl.loop(0, count)
    def _(i):
        block = block_of(i)
        out_row = pl.multiple_of(i * STRETCH, STRETCH)
        q_row = pl.multiple_of(block * STRETCH, STRETCH)
        chunk = pair * chunks + block
        left = left_ref[0, chunk]
        start = start_ref[0, owner_ref[0, chunk]]
        lowest = jnp.maximum((chunk - left) * STRETCH, start)
        for back in range(LEFT + 1):

            @pl.when(left == back)
            def _():
                k_row = pl.multiple_of((block - k_base + LEFT - back) * STRETCH, STRETCH)
                span = (back + 1) * STRETCH
                attend_block(chunk, start, lowest, q_row, k_row, span, out_ref, out_row)


def after(value, *others):
    return lax.optimization_barrier((value, *others))[0]


SMEM_SPEC = pl.BlockSpec(memory_space=pltpu.SMEM)
VMEM_SPEC = pl.BlockSpec(memory_space=pltpu.VMEM)
ANY_SPEC = pl.BlockSpec(memory_space=pl.ANY)


def half_kernel(w_ref, out_ref, sems):
    width = out_ref.shape[1] // 3
    core = lax.axis_index("tm") % 2
    pairs = []
    for third in range(3):
        at = pl.multiple_of((2 * third + core) * width, LANES)
        pairs.append((w_ref.at[:, pl.ds(at, width)], out_ref.at[:, third * width : (third + 1) * width]))
    for copy in start_all(sems, pairs):
        copy.wait()


def take_half(w):
    return pl.pallas_call(
        half_kernel,
        out_shape=jax.ShapeDtypeStruct((w.shape[0], w.shape[1] // 2), w.dtype),
        in_specs=[pl.BlockSpec(memory_space=pltpu.HBM)],
        out_specs=VMEM_SPEC,
        scratch_shapes=[pltpu.SemaphoreType.DMA((3,))],
        compiler_params=pltpu.CompilerParams(vmem_limit_bytes=4 * MIB),
        name="take_half",
    )(w)


def join_kernel(own_ref, other_ref, out_ref, sems):
    rows, width = own_ref.shape
    core = lax.axis_index("tm") % 2
    own_at = pl.multiple_of(core * width, LANES)
    other_at = pl.multiple_of((1 - core) * width, LANES)
    pairs = [
        (own_ref, out_ref.at[:, pl.ds(own_at, width)]),
        (other_ref.at[:rows, :], out_ref.at[:, pl.ds(other_at, width)]),
    ]
    for copy in start_all(sems, pairs):
        copy.wait()


def join(own, other):
    rows, width = own.shape
    return pl.pallas_call(
        join_kernel,
        out_shape=jax.ShapeDtypeStruct((rows, 2 * width), own.dtype),
        in_specs=[ANY_SPEC] * 2,
        out_specs=ANY_SPEC,
        scratch_shapes=[pltpu.SemaphoreType.DMA((2,))],
        compiler_params=pltpu.CompilerParams(vmem_limit_bytes=4 * MIB),
        name="join",
    )(own, other)


def project_early(blocks, step, inputs, partner, sums=()):
    rows = inputs.shape[0]
    depth = blocks.step_depth(step)
    operands = blocks.step_operands(step)
    cols = operands[0].shape[1]
    return pl.pallas_call(
        functools.partial(early_kernel, blocks, step),
        out_shape=[jax.ShapeDtypeStruct((rows, cols), jnp.float32)] * 2,
        in_specs=[ANY_SPEC] * (len(operands) + 2) + [VMEM_SPEC] * len(sums),
        out_specs=[VMEM_SPEC] * 2,
        scratch_shapes=[
            pltpu.VMEM((depth, cols), jnp.bfloat16),
            pltpu.VMEM((rows, depth), jnp.bfloat16),
            pltpu.VMEM((rows, depth), jnp.bfloat16),
            pltpu.SemaphoreType.DMA((len(operands) + 2,)),
        ],
        compiler_params=pltpu.CompilerParams(vmem_limit_bytes=20 * MIB),
        cost_estimate=pl.CostEstimate(flops=0, bytes_accessed=0, transcendentals=0),
        name="project_early",
    )(*operands, inputs, partner, *sums)


def tail_kernel(x_ref, *refs):
    *outs, sems = refs
    first = x_ref.shape[0] - len(outs) * STRETCH
    pairs = [
        (x_ref.at[first + i * STRETCH : first + (i + 1) * STRETCH, :], out)
        for i, out in enumerate(outs)
    ]
    for copy in start_all(sems, pairs):
        copy.wait()


def take_tail(x):
    return pl.pallas_call(
        tail_kernel,
        out_shape=[jax.ShapeDtypeStruct((STRETCH, x.shape[1]), x.dtype)] * LEFT,
        in_specs=[ANY_SPEC],
        out_specs=[VMEM_SPEC] * LEFT,
        scratch_shapes=[pltpu.SemaphoreType.DMA((LEFT,))],
        compiler_params=pltpu.CompilerParams(vmem_limit_bytes=4 * MIB),
        name="take_tail",
    )(x)


def project_late_attend(tables, blocks, inputs, partner, halo, sums):
    rows, depth = inputs.shape
    late_depth = blocks.step_depth(-1)
    cols = blocks.operands[0].shape[1]
    width = cols // 3
    keys = jax.ShapeDtypeStruct((2 * rows + REACH, width), jnp.bfloat16)
    return pl.pallas_call(
        functools.partial(late_kernel, blocks),
        out_shape=[
            jax.ShapeDtypeStruct((2 * rows - REACH, width), jnp.bfloat16),
            jax.ShapeDtypeStruct((2 * rows, width), jnp.bfloat16),
            keys,
            keys,
            jax.ShapeDtypeStruct((depth, 2 * width), jnp.bfloat16),
        ],
        in_specs=[SMEM_SPEC] * 3 + [ANY_SPEC] * (len(blocks.operands) + 2) + [VMEM_SPEC] * (LEFT + 2),
        out_specs=[VMEM_SPEC] * 5,
        scratch_shapes=[
            pltpu.VMEM((late_depth, cols), jnp.bfloat16),
            pltpu.VMEM((rows, late_depth), jnp.bfloat16),
            pltpu.VMEM((rows, late_depth), jnp.bfloat16),
            pltpu.SemaphoreType.DMA((len(blocks.operands) + len(blocks.steps[-1]) + 2,)),
        ],
        compiler_params=pltpu.CompilerParams(vmem_limit_bytes=24 * MIB),
        name="project_late_attend",
    )(*tables, *blocks.operands, inputs, partner, *halo, *sums)


def attend_own(tables, queries, keys, values, weights, halo, done):
    rows, width = queries.shape
    rows //= 2
    return pl.pallas_call(
        own_kernel,
        out_shape=jax.ShapeDtypeStruct((rows, width), jnp.bfloat16),
        in_specs=[SMEM_SPEC] * 3 + [VMEM_SPEC] * (LEFT + 5),
        out_specs=VMEM_SPEC,
        scratch_shapes=[pltpu.VMEM((rows + REACH, width), jnp.bfloat16)] * 2,
        compiler_params=pltpu.CompilerParams(vmem_limit_bytes=20 * MIB),
        name="attend_own",
    )(*tables, queries, keys, values, weights, *halo, done)


def at_end():
    place = lax.axis_index("dp") // 2
    return jnp.where((place == 0) | (place == 3), 1, 0)


def choose_kernel(between_ref, end_ref, out_ref, sems):
    for copy in start_all(sems, [((between_ref, end_ref), at_end(), out_ref)]):
        copy.wait()


def choose(between, end):
    return pl.pallas_call(
        choose_kernel,
        out_shape=jax.ShapeDtypeStruct(end.shape, end.dtype),
        in_specs=[ANY_SPEC] * 2,
        out_specs=VMEM_SPEC,
        scratch_shapes=[pltpu.SemaphoreType.DMA((1,))],
        compiler_params=pltpu.CompilerParams(vmem_limit_bytes=2 * MIB),
        name="choose",
    )(between, end)


def gather_neighbours(half):
    size = half.shape[0]

    def along(name, block, hops):
        with jax.named_scope(name):
            return lax.ppermute(
                block, "dp", [(2 * a + s, 2 * b + s) for a, b in hops for s in range(2)]
            )

    def across(name, block, places):
        with jax.named_scope(name):
            return lax.ppermute(
                block, "dp", [(2 * a + s, 2 * a + 1 - s) for a in places for s in range(2)]
            )

    line = range(4)
    outward = [(1, 0), (2, 3)]
    between = [(1, 2), (2, 1)]
    near = along("near", half, outward + [(0, 1), (3, 2)])
    mid = along("mid", half, between)
    half_across = across("half_across", half, line)
    mid_far = along("mid_far", near, between)
    near_across = across("near_across", after(near, half_across, mid), line)
    end_mid = along("end_mid", mid, outward)
    end_far = along("end_far", after(mid_far, end_mid), outward)
    second = choose(mid, end_mid)
    second_across = across("second_across", after(second, near_across), line)
    third = choose(mid_far, end_far)
    third_across = across("third_across", after(third, second_across), line)

    def find():
        index = lax.axis_index("dp")
        place, side = index // 2, index % 2
        is_end = at_end()
        second = jnp.where(is_end == 1, place ^ 2, 3 - place)
        third = jnp.where(is_end == 1, 3 - place, place ^ 2)
        spots = (place, place ^ 1, second, third)
        found = [(2 * spot + (side ^ n)) * size for spot in spots for n in range(2)]
        return found, [place // 2 * 4 * size, second * 2 * size, third * 2 * size]

    blocks = [
        half,
        half_across,
        near,
        near_across,
        second,
        second_across,
        third,
        third_across,
    ]
    marks = (near_across, mid_far, end_mid), (second_across, end_far), (third_across,)
    return Blocks(blocks, ((0, 1, 2, 3), (4, 5), (6, 7)), find), marks


def local(frames, w_qkv, utt_start, stretch_utt, left_stretches):
    inputs = frames[0]
    depth = inputs.shape[1]
    members = lax.axis_size("tm")

    half = take_half(w_qkv)

    tail = take_tail(after(inputs, half))
    with jax.named_scope("partner"):
        partner = lax.ppermute(inputs, "tm", [(i, i ^ 1) for i in range(members)])
    if lax.axis_size("dp") == 8:
        blocks, marks = gather_neighbours(half)
    else:
        weights = lax.all_gather(half, "dp", axis=0, tiled=True)
        firsts = [depth // GROUPS * i for i in (0, 2, 3)]
        parts = [weights[i:j] for i, j in zip(firsts, firsts[1:] + [depth])]
        blocks = Blocks(parts, ((0,), (1,), (2,)), lambda: (firsts, firsts))
        marks = ((half,),) * 3

    sums = project_early(blocks, 0, inputs, partner)
    marks = marks[0], (*marks[1], *sums)
    with jax.named_scope("halo"):
        onward = [(i, i + 2) for i in range(1, members - 2, 2)]
        halo = [lax.ppermute(after(x, *mark), "tm", onward) for x, mark in zip(tail, marks)]

    tables = (utt_start, stretch_utt, left_stretches)
    sums = project_early(blocks, 1, inputs, partner, sums)
    with jax.named_scope("halo_first"):
        back = [(i + 1, i) for i in range(0, members, 2)]
        halo_first = [lax.ppermute(after(x, *sums), "tm", back) for x in halo]
    attended, queries, keys, values, weights = project_late_attend(
        tables, blocks, inputs, partner, halo, sums
    )
    with jax.named_scope("swap"):
        other = lax.ppermute(attended, "tm", [(i, i ^ 1) for i in range(members)])
    own_out = attend_own(tables, queries, keys, values, weights, halo_first, attended)
    return join(own_out, other)[None]


def solution(mesh):
    return jax.shard_map(
        local,
        mesh=mesh,
        in_specs=(P("dp", "tm", None), P("dp", None), P("dp", None), P("dp", None), P("dp", None)),
        out_specs=P("dp", "tm", None),
        check_vma=False,
    )
```

```python
import functools
import math

import jax
import jax.numpy as jnp
from jax import lax
from jax.experimental import pallas as pl
from jax.experimental.pallas import tpu as pltpu
from jax.sharding import PartitionSpec as P

HEAD_DIM = 96
STRETCH = 256
LEFT = 2
LANES = 128
GROUPS = 4
EXP_SCALE = HEAD_DIM**-0.5 * math.log2(math.e)
REACH = LEFT * STRETCH
MIB = 1024 * 1024


def dot(a, b, dims=((1,), (0,))):
    return lax.dot_general(a, b, (dims, ((), ())), preferred_element_type=jnp.float32)


def head_window(head):
    first = head * HEAD_DIM // LANES * LANES
    last = -(-(head + 1) * HEAD_DIM // LANES) * LANES
    return first, last


def start_all(sems, pairs):
    copies = []
    for i, (*source, target) in enumerate(pairs):
        if len(source) == 1:
            copy = pltpu.make_async_copy(source[0], target, sems.at[i])
            copy.start()
        else:
            for n, choice in enumerate(source[0]):
                copy = pltpu.make_async_copy(choice, target, sems.at[i])
                pl.when(source[1] == n)(copy.start)
        copies.append(copy)
    return copies


class Blocks:
    def __init__(self, blocks, steps, find):
        self.operands = list(blocks)
        self.rows = [block.shape[0] for block in blocks]
        self.steps = steps
        self.find = find

    def step_operands(self, step):
        return [self.operands[i] for i in self.steps[step]]

    def step_depth(self, step):
        return sum(self.rows[i] for i in self.steps[step])

    def copies(self, refs, found, members, target, first=0, columns=slice(None)):
        pairs = []
        for ref, i in zip(refs, members):
            rows = self.rows[i]
            goal = target.at[pl.ds(pl.multiple_of(found[i] - first, rows), rows)]
            pairs.append((ref.at[:, columns], goal))
        return pairs


def early_kernel(blocks, step, *refs):
    n = len(blocks.step_operands(step))
    own_ref, partner_ref, *sums = refs[n : n + 2 + 2 * min(step, 1)]
    own_out, partner_out, w_s, own_s, partner_s, sems = refs[n + 2 + len(sums) :]
    found, firsts = blocks.find()
    depth = w_s.shape[0]
    first = firsts[step]
    pairs = blocks.copies(refs, found, blocks.steps[step], w_s, first)
    columns = pl.ds(pl.multiple_of(first, LANES), depth)
    pairs.append((own_ref.at[:, columns], own_s))
    pairs.append((partner_ref.at[:, columns], partner_s))
    *first_copies, last_copy = start_all(sems, pairs)
    for copy in first_copies:
        copy.wait()
    own = dot(own_s[...], w_s[...])
    own_out[...] = own + sums[0][...] if sums else own
    last_copy.wait()
    partner = dot(partner_s[...], w_s[...])
    partner_out[...] = partner + sums[1][...] if sums else partner


def project_halo(halo_refs, kv_ref, k_ref, v_ref):
    width = k_ref.shape[1]
    for i, frames_ref in enumerate(halo_refs):
        at = slice(i * STRETCH, (i + 1) * STRETCH)
        both = dot(frames_ref[...], kv_ref[...]).astype(jnp.bfloat16)
        k_ref[at, :] = both[:, :width]
        v_ref[at, :] = both[:, width:]


def late_kernel(blocks, start_ref, owner_ref, left_ref, *refs):
    n = len(blocks.operands)
    own_ref, partner_ref = refs[n : n + 2]
    halo_refs = refs[n + 2 : n + 2 + LEFT]
    own_sum, partner_sum, out_ref, q_out, k_out, v_out, kv_out, *scratch = refs[n + 2 + LEFT :]
    w_s, own_s, partner_s, sems = scratch
    depth = w_s.shape[0]
    width = w_s.shape[1] // 3
    rows = own_s.shape[0]
    core = lax.axis_index("tm") % 2
    found, (*_, late_first) = blocks.find()
    everything = range(len(found))
    last = blocks.steps[-1]
    pairs = blocks.copies([refs[i] for i in last], found, last, w_s, late_first)
    columns = pl.ds(pl.multiple_of(late_first, LANES), depth)
    pairs.append((partner_ref.at[:, columns], partner_s))
    pairs.append((own_ref.at[:, columns], own_s))
    n_first = len(pairs)
    pairs += blocks.copies(refs, found, everything, kv_out, 0, slice(width, 3 * width))
    copies = start_all(sems, pairs)
    for copy in copies[: n_first - 1]:
        copy.wait()
    for x_s, acc, place in ((partner_s, partner_sum, 1 - core), (own_s, own_sum, core)):
        if x_s is own_s:
            copies[n_first - 1].wait()
        row = pl.multiple_of(place * rows, STRETCH)
        value = (acc[...] + dot(x_s[...], w_s[...])).astype(jnp.bfloat16)
        for third, (dst, skip) in enumerate(((q_out, 0), (k_out, REACH), (v_out, REACH))):
            part = value[:, third * width : (third + 1) * width]
            dst[pl.ds(pl.multiple_of(row + skip, STRETCH), rows), :] = part
    for copy in copies[n_first:]:
        copy.wait()

    @pl.when(core == 1)
    def _():
        project_halo(halo_refs, kv_out, k_out, v_out)

    chunks = rows // STRETCH

    def block_of(i):
        return jnp.where(i < chunks, (1 - core) * chunks + i, i - chunks + LEFT)

    count = jnp.where(core == 0, 2 * chunks - LEFT, chunks)
    attend(start_ref, owner_ref, left_ref, q_out, k_out, v_out, 0, count, block_of, out_ref)


def own_kernel(start_ref, owner_ref, left_ref, q_ref, k_ref, v_ref, kv_ref, *refs):
    *halo_refs, done_ref, out_ref, k_s, v_s = refs
    rows, width = out_ref.shape
    core = lax.axis_index("tm") % 2
    own = pl.multiple_of(core * rows + REACH, STRETCH)
    k_s[REACH:, :] = k_ref[pl.ds(own, rows), :]
    v_s[REACH:, :] = v_ref[pl.ds(own, rows), :]

    @pl.when(core == 0)
    def _():
        project_halo(halo_refs, kv_ref, k_s, v_s)

    @pl.when(core == 1)
    def _():
        k_s[:REACH, :] = k_ref[rows : rows + REACH, :]
        v_s[:REACH, :] = v_ref[rows : rows + REACH, :]

    chunks = rows // STRETCH
    base = core * chunks
    count = jnp.where(core == 0, LEFT, chunks)

    def block_of(i):
        return base + i

    attend(start_ref, owner_ref, left_ref, q_ref, k_s, v_s, base, count, block_of, out_ref)

    @pl.when(core == 0)
    def _():
        out_ref[REACH:, :] = done_ref[rows : 2 * rows - REACH, :]


def attend(start_ref, owner_ref, left_ref, q_s, k_s, v_s, k_base, count, block_of, out_ref):
    width = out_ref.shape[1]
    chunks = q_s.shape[0] // STRETCH
    pair = lax.axis_index("tm") // 2
    lane = lax.broadcasted_iota(jnp.int32, (1, width), 1)
    heads = width // HEAD_DIM

    def attend_block(chunk, start, lowest, q_row, k_row, span, out_ref, out_row):
        first_key = (chunk + 1) * STRETCH - span
        key_frame = first_key + lax.broadcasted_iota(jnp.int32, (1, STRETCH), 1)
        bias = jnp.where(key_frame >= lowest, 0.0, -jnp.inf).astype(jnp.float32)
        frame = chunk * STRETCH + lax.broadcasted_iota(jnp.int32, (STRETCH, 1), 0)
        live = frame >= start
        windows = [head_window(head) for head in range(heads)]
        insides = [
            ((lane >= head * HEAD_DIM) & (lane < (head + 1) * HEAD_DIM))[:, first:last]
            for head, (first, last) in enumerate(windows)
        ]
        tiles = [jnp.zeros((STRETCH, LANES), jnp.float32) for _ in range(width // LANES)]

        def score(head):
            first, last = windows[head]
            q = q_s[pl.ds(q_row, STRETCH), first:last]
            q = jnp.where(insides[head], q, jnp.zeros_like(q))
            return dot(q, k_s[pl.ds(k_row, span), first:last], ((1,), (1,)))

        def weigh(scores):
            scores = [scores[:, at : at + STRETCH] for at in range(0, span, STRETCH)]
            scores[0] = scores[0] + bias
            top = functools.reduce(jnp.maximum, scores)
            top = jnp.max(top, axis=-1, keepdims=True)
            expo = [jnp.exp2((part - top) * EXP_SCALE) for part in scores]
            total = jnp.sum(functools.reduce(jnp.add, expo), axis=-1, keepdims=True)
            share = 1.0 / total
            return jnp.concatenate([(part * share).astype(jnp.bfloat16) for part in expo], axis=1)

        def mix(head, probs):
            first, last = windows[head]
            mixed = dot(probs, v_s[pl.ds(k_row, span), first:last])
            for tile in range(first // LANES, last // LANES):
                at = tile * LANES - first
                tiles[tile] = jnp.where(
                    insides[head][:, at : at + LANES], mixed[:, at : at + LANES], tiles[tile]
                )

        scores = score(0)
        probs = None
        for head in range(heads):
            following = score(head + 1) if head + 1 < heads else None
            weighed = weigh(scores)
            if probs is not None:
                mix(head - 1, probs)
            scores, probs = following, weighed
        mix(heads - 1, probs)
        for tile, value in enumerate(tiles):
            value = jnp.where(live, value, 0.0).astype(jnp.bfloat16)
            out_ref[pl.ds(out_row, STRETCH), tile * LANES : (tile + 1) * LANES] = value

    @pl.loop(0, count)
    def _(i):
        block = block_of(i)
        out_row = pl.multiple_of(i * STRETCH, STRETCH)
        q_row = pl.multiple_of(block * STRETCH, STRETCH)
        chunk = pair * chunks + block
        left = left_ref[0, chunk]
        start = start_ref[0, owner_ref[0, chunk]]
        lowest = jnp.maximum((chunk - left) * STRETCH, start)
        for back in range(LEFT + 1):

            @pl.when(left == back)
            def _():
                k_row = pl.multiple_of((block - k_base + LEFT - back) * STRETCH, STRETCH)
                span = (back + 1) * STRETCH
                attend_block(chunk, start, lowest, q_row, k_row, span, out_ref, out_row)


def after(value, *others):
    return lax.optimization_barrier((value, *others))[0]


SMEM_SPEC = pl.BlockSpec(memory_space=pltpu.SMEM)
VMEM_SPEC = pl.BlockSpec(memory_space=pltpu.VMEM)
ANY_SPEC = pl.BlockSpec(memory_space=pl.ANY)


def half_kernel(w_ref, out_ref, sems):
    width = out_ref.shape[1] // 3
    core = lax.axis_index("tm") % 2
    pairs = []
    for third in range(3):
        at = pl.multiple_of((2 * third + core) * width, LANES)
        pairs.append((w_ref.at[:, pl.ds(at, width)], out_ref.at[:, third * width : (third + 1) * width]))
    for copy in start_all(sems, pairs):
        copy.wait()


def take_half(w):
    return pl.pallas_call(
        half_kernel,
        out_shape=jax.ShapeDtypeStruct((w.shape[0], w.shape[1] // 2), w.dtype),
        in_specs=[pl.BlockSpec(memory_space=pltpu.HBM)],
        out_specs=VMEM_SPEC,
        scratch_shapes=[pltpu.SemaphoreType.DMA((3,))],
        compiler_params=pltpu.CompilerParams(vmem_limit_bytes=4 * MIB),
        name="take_half",
    )(w)


def join_kernel(own_ref, other_ref, out_ref, sems):
    rows, width = own_ref.shape
    core = lax.axis_index("tm") % 2
    own_at = pl.multiple_of(core * width, LANES)
    other_at = pl.multiple_of((1 - core) * width, LANES)
    pairs = [
        (own_ref, out_ref.at[:, pl.ds(own_at, width)]),
        (other_ref.at[:rows, :], out_ref.at[:, pl.ds(other_at, width)]),
    ]
    for copy in start_all(sems, pairs):
        copy.wait()


def join(own, other):
    rows, width = own.shape
    return pl.pallas_call(
        join_kernel,
        out_shape=jax.ShapeDtypeStruct((rows, 2 * width), own.dtype),
        in_specs=[ANY_SPEC] * 2,
        out_specs=ANY_SPEC,
        scratch_shapes=[pltpu.SemaphoreType.DMA((2,))],
        compiler_params=pltpu.CompilerParams(vmem_limit_bytes=4 * MIB),
        name="join",
    )(own, other)


def project_early(blocks, step, inputs, partner, sums=()):
    rows = inputs.shape[0]
    depth = blocks.step_depth(step)
    operands = blocks.step_operands(step)
    cols = operands[0].shape[1]
    return pl.pallas_call(
        functools.partial(early_kernel, blocks, step),
        out_shape=[jax.ShapeDtypeStruct((rows, cols), jnp.float32)] * 2,
        in_specs=[ANY_SPEC] * (len(operands) + 2) + [VMEM_SPEC] * len(sums),
        out_specs=[VMEM_SPEC] * 2,
        scratch_shapes=[
            pltpu.VMEM((depth, cols), jnp.bfloat16),
            pltpu.VMEM((rows, depth), jnp.bfloat16),
            pltpu.VMEM((rows, depth), jnp.bfloat16),
            pltpu.SemaphoreType.DMA((len(operands) + 2,)),
        ],
        compiler_params=pltpu.CompilerParams(vmem_limit_bytes=20 * MIB),
        cost_estimate=pl.CostEstimate(flops=0, bytes_accessed=0, transcendentals=0),
        name="project_early",
    )(*operands, inputs, partner, *sums)


def tail_kernel(x_ref, *refs):
    *outs, sems = refs
    first = x_ref.shape[0] - len(outs) * STRETCH
    pairs = [
        (x_ref.at[first + i * STRETCH : first + (i + 1) * STRETCH, :], out)
        for i, out in enumerate(outs)
    ]
    for copy in start_all(sems, pairs):
        copy.wait()


def take_tail(x):
    return pl.pallas_call(
        tail_kernel,
        out_shape=[jax.ShapeDtypeStruct((STRETCH, x.shape[1]), x.dtype)] * LEFT,
        in_specs=[ANY_SPEC],
        out_specs=[VMEM_SPEC] * LEFT,
        scratch_shapes=[pltpu.SemaphoreType.DMA((LEFT,))],
        compiler_params=pltpu.CompilerParams(vmem_limit_bytes=4 * MIB),
        name="take_tail",
    )(x)


def project_late_attend(tables, blocks, inputs, partner, halo, sums):
    rows, depth = inputs.shape
    late_depth = blocks.step_depth(-1)
    cols = blocks.operands[0].shape[1]
    width = cols // 3
    keys = jax.ShapeDtypeStruct((2 * rows + REACH, width), jnp.bfloat16)
    return pl.pallas_call(
        functools.partial(late_kernel, blocks),
        out_shape=[
            jax.ShapeDtypeStruct((2 * rows - REACH, width), jnp.bfloat16),
            jax.ShapeDtypeStruct((2 * rows, width), jnp.bfloat16),
            keys,
            keys,
            jax.ShapeDtypeStruct((depth, 2 * width), jnp.bfloat16),
        ],
        in_specs=[SMEM_SPEC] * 3 + [ANY_SPEC] * (len(blocks.operands) + 2) + [VMEM_SPEC] * (LEFT + 2),
        out_specs=[VMEM_SPEC] * 5,
        scratch_shapes=[
            pltpu.VMEM((late_depth, cols), jnp.bfloat16),
            pltpu.VMEM((rows, late_depth), jnp.bfloat16),
            pltpu.VMEM((rows, late_depth), jnp.bfloat16),
            pltpu.SemaphoreType.DMA((len(blocks.operands) + len(blocks.steps[-1]) + 2,)),
        ],
        compiler_params=pltpu.CompilerParams(vmem_limit_bytes=24 * MIB),
        name="project_late_attend",
    )(*tables, *blocks.operands, inputs, partner, *halo, *sums)


def attend_own(tables, queries, keys, values, weights, halo, done):
    rows, width = queries.shape
    rows //= 2
    return pl.pallas_call(
        own_kernel,
        out_shape=jax.ShapeDtypeStruct((rows, width), jnp.bfloat16),
        in_specs=[SMEM_SPEC] * 3 + [VMEM_SPEC] * (LEFT + 5),
        out_specs=VMEM_SPEC,
        scratch_shapes=[pltpu.VMEM((rows + REACH, width), jnp.bfloat16)] * 2,
        compiler_params=pltpu.CompilerParams(vmem_limit_bytes=20 * MIB),
        name="attend_own",
    )(*tables, queries, keys, values, weights, *halo, done)


def at_end():
    place = lax.axis_index("dp") // 2
    return jnp.where((place == 0) | (place == 3), 1, 0)


def choose_kernel(between_ref, end_ref, out_ref, sems):
    for copy in start_all(sems, [((between_ref, end_ref), at_end(), out_ref)]):
        copy.wait()


def choose(between, end):
    return pl.pallas_call(
        choose_kernel,
        out_shape=jax.ShapeDtypeStruct(end.shape, end.dtype),
        in_specs=[ANY_SPEC] * 2,
        out_specs=VMEM_SPEC,
        scratch_shapes=[pltpu.SemaphoreType.DMA((1,))],
        compiler_params=pltpu.CompilerParams(vmem_limit_bytes=2 * MIB),
        name="choose",
    )(between, end)


def gather_neighbours(half):
    size = half.shape[0]

    def along(name, block, hops):
        with jax.named_scope(name):
            return lax.ppermute(
                block, "dp", [(2 * a + s, 2 * b + s) for a, b in hops for s in range(2)]
            )

    def across(name, block, places):
        with jax.named_scope(name):
            return lax.ppermute(
                block, "dp", [(2 * a + s, 2 * a + 1 - s) for a in places for s in range(2)]
            )

    line = range(4)
    outward = [(1, 0), (2, 3)]
    between = [(1, 2), (2, 1)]
    near = along("near", half, outward + [(0, 1), (3, 2)])
    mid = along("mid", half, between)
    half_across = across("half_across", half, line)
    mid_far = along("mid_far", near, between)
    near_across = across("near_across", after(near, half_across, mid), line)
    end_mid = along("end_mid", mid, outward)
    end_far = along("end_far", after(mid_far, end_mid), outward)
    second = choose(mid, end_mid)
    second_across = across("second_across", after(second, near_across), line)
    third = choose(mid_far, end_far)
    third_across = across("third_across", after(third, second_across), line)

    def find():
        index = lax.axis_index("dp")
        place, side = index // 2, index % 2
        is_end = at_end()
        second = jnp.where(is_end == 1, place ^ 2, 3 - place)
        third = jnp.where(is_end == 1, 3 - place, place ^ 2)
        spots = (place, place ^ 1, second, third)
        found = [(2 * spot + (side ^ n)) * size for spot in spots for n in range(2)]
        return found, [place // 2 * 4 * size, second * 2 * size, third * 2 * size]

    blocks = [
        half,
        half_across,
        near,
        near_across,
        second,
        second_across,
        third,
        third_across,
    ]
    marks = (near_across, mid_far, end_mid), (second_across,), (third_across,)
    return Blocks(blocks, ((0, 1, 2, 3), (4, 5), (6, 7)), find), marks


def local(frames, w_qkv, utt_start, stretch_utt, left_stretches):
    inputs = frames[0]
    depth = inputs.shape[1]
    members = lax.axis_size("tm")

    half = take_half(w_qkv)

    tail = take_tail(after(inputs, half))
    with jax.named_scope("partner"):
        partner = lax.ppermute(inputs, "tm", [(i, i ^ 1) for i in range(members)])
    if lax.axis_size("dp") == 8:
        blocks, marks = gather_neighbours(half)
    else:
        weights = lax.all_gather(half, "dp", axis=0, tiled=True)
        firsts = [depth // GROUPS * i for i in (0, 2, 3)]
        parts = [weights[i:j] for i, j in zip(firsts, firsts[1:] + [depth])]
        blocks = Blocks(parts, ((0,), (1,), (2,)), lambda: (firsts, firsts))
        marks = ((half,),) * 3

    sums = project_early(blocks, 0, inputs, partner)
    marks = marks[0], (*marks[1], *sums)
    with jax.named_scope("halo"):
        onward = [(i, i + 2) for i in range(1, members - 2, 2)]
        halo = [lax.ppermute(after(x, *mark), "tm", onward) for x, mark in zip(tail, marks)]

    tables = (utt_start, stretch_utt, left_stretches)
    sums = project_early(blocks, 1, inputs, partner, sums)
    with jax.named_scope("halo_first"):
        back = [(i + 1, i) for i in range(0, members, 2)]
        halo_first = [lax.ppermute(after(x, *sums), "tm", back) for x in halo]
    attended, queries, keys, values, weights = project_late_attend(
        tables, blocks, inputs, partner, halo, sums
    )
    with jax.named_scope("swap"):
        other = lax.ppermute(attended, "tm", [(i, i ^ 1) for i in range(members)])
    own_out = attend_own(tables, queries, keys, values, weights, halo_first, attended)
    return join(own_out, other)[None]


def solution(mesh):
    return jax.shard_map(
        local,
        mesh=mesh,
        in_specs=(P("dp", "tm", None), P("dp", None), P("dp", None), P("dp", None), P("dp", None)),
        out_specs=P("dp", "tm", None),
        check_vma=False,
    )
```
